128 devices in a mesh: lat: 32 (over y, x_hi, z), lon: 2 (over x_lo), section: 2 (over core).
Axes of the slice: x: 4 (x_hi: 2, x_lo: 2; x = x_hi * 2 + x_lo), y: 4, z: 4, core: 2. Of those that a mesh axis runs over, the one named last changes fastest.
Arguments:
- boundary: bfloat16 [2, 2, 2, 192, 24, 1024], P('section', None, None, 'lat', 'lon'), may hold values from -6 to 6
- tile_kinds: int32 [2, 32, 2], P('section', 'lat', 'lon'), may hold values from 0 to 3
- proj_in: bfloat16 [2, 1024, 3072], P('section'), may hold values from -0.1875 to 0.1875
- proj_out: bfloat16 [2, 1024, 1024], P('section'), may hold values from -0.375 to 0.375
- offset_bias: float32 [2, 16, 759], P('section'), may hold values from -4 to 250
Outputs:
- boundary_out: bfloat16 [2, 2, 2, 192, 24, 1024], P('section', None, None, 'lat', 'lon')
- weight_grads: float32 [2, 1024, 4096], P('section', ('lat', 'lon'))
- bias_grads: float32 [2, 16, 759], P('section')
The draws below stay inside these ranges and needn't reach their ends.
All inputs are finite; a program needn't handle non-finite values.
Results may differ from the reference program's by a relative error of at most 0.025.
Values may be sent and summed in bfloat16 or wider, within the bound.
No kernel may reach another device: no remote copies, remote signals or barrier semaphores. Data moves between devices by JAX's collectives and lax.ppermute only.
A program may use at most 192 MiB of HBM per device.

```python
import jax
import jax.numpy as jnp
from jax import lax

D = 1024
HEADS = 16
HEAD_DIM = 64
LEV = 2
WIN_LAT = 6
WIN_LON = 12
KINDS = 4
MICRO = 2
WT = 144
OFFSETS = 759
NLAT = 192
NLON = 24


def draw_offset_bias(key, part):
    key = jax.random.fold_in(key, 7)
    base_key = jax.random.fold_in(key, 1)
    rank_key = jax.random.fold_in(key, 2)
    reach_key = jax.random.fold_in(key, 3)
    gap_key = jax.random.fold_in(key, 4)
    background = jnp.clip(jax.random.normal(base_key, (2, HEADS, OFFSETS), jnp.float32), -4.0, 4.0)
    lowest = 110.0
    highest = 240.0
    planted_count = max(2, HEADS // 5)
    head_rank = jnp.stack([jax.random.permutation(jax.random.fold_in(rank_key, member), HEADS) for member in range(2)])
    planted = head_rank < planted_count
    strength = lowest + (highest - lowest) * head_rank.astype(jnp.float32) / (planted_count - 1)
    reach_cols = jax.random.randint(reach_key, (2, HEADS), 1, 5)
    gap_size = jax.random.uniform(gap_key, (2, HEADS), jnp.float32, 1.0, 3.0)
    center = ((LEV - 1) * (2 * WIN_LAT - 1) + WIN_LAT - 1) * (2 * WIN_LON - 1) + WIN_LON - 1
    slot_ids = jnp.arange(OFFSETS)[None, None, :]
    upper_hit = planted[:, :, None] & (slot_ids == center + reach_cols[:, :, None])
    lower_hit = planted[:, :, None] & (slot_ids == center - reach_cols[:, :, None])
    drawn = jnp.where(upper_hit, strength[:, :, None], background)
    return jnp.where(lower_hit, (strength - gap_size)[:, :, None], drawn)


def place_ends(array, own_key, low, high):
    shape = array.shape
    index_at = [jax.random.randint(jax.random.fold_in(own_key, axis), (), 0, shape[axis]) for axis in range(len(shape))]
    array = array.at[tuple(index_at)].set(low)
    longest = shape.index(max(shape))
    index_at[longest] = (index_at[longest] + 1) % shape[longest]
    return array.at[tuple(index_at)].set(high)


def level_of(rng, shape, cuts, smallest, top_value):
    factor_of, own = 1.0, jax.random.fold_in(rng, 6)
    for dim, shards_of in cuts:
        steps = jnp.exp(jax.random.uniform(jax.random.fold_in(own, dim), (shards_of,), jnp.float32, smallest / len(cuts), top_value / len(cuts)))
        factor_of = factor_of * jnp.repeat(steps, shape[dim] // shards_of).reshape([-1 if axis == dim else 1 for axis in range(len(shape))])
    return factor_of


def scatter_about(key, extent, scale, most, shards=(), held_as=jnp.bfloat16):
    factor_of = level_of(key, extent, shards, -0.22, 0.18) if shards else 1.0
    entries = jax.random.normal(key, extent, jnp.float32) * scale * factor_of
    return jnp.minimum(jnp.maximum(entries, -most), most).astype(held_as)


def setup_inputs(seed: int = 0) -> dict:
    keys = jax.random.split(jax.random.key(seed), 6)
    return {
        "boundary": scatter_about(keys[0], (2, MICRO, LEV, NLAT, NLON, D), 1.0, 6.0, ((0, 2), (3, 32), (4, 2))),
        "tile_kinds": place_ends(jax.random.randint(keys[1], (2, NLAT // WIN_LAT, NLON // WIN_LON), 0, KINDS), jax.random.fold_in(keys[1], 1), 0, KINDS - 1).astype(jnp.int32),
        "proj_in": scatter_about(keys[2], (2, D, 3 * D), D ** -0.5, 0.1875, ((0, 2),)),
        "proj_out": scatter_about(keys[3], (2, D, D), (D // 4) ** -0.5, 0.375, ((0, 2),)),
        "offset_bias": draw_offset_bias(jax.random.fold_in(keys[5], 71), 0),
    }


NORM_EPS = 1e-05
MASKED = -1e+30

def normed(volume):
    values = volume.astype(jnp.float32)
    average = lax.optimization_barrier(jnp.mean(values, axis=-1, keepdims=True))
    centered = values - average
    variance = lax.optimization_barrier(jnp.mean(centered * centered, axis=-1, keepdims=True))
    return (centered * lax.rsqrt(variance + NORM_EPS)).astype(jnp.bfloat16)

def to_windows(volume):
    micro_count, levels, lat_rows, lon_cols, features = volume.shape
    pieces = volume.reshape(micro_count, levels, lat_rows // WIN_LAT, WIN_LAT, lon_cols // WIN_LON, WIN_LON, features)
    pieces = pieces.transpose(0, 2, 4, 1, 3, 5, 6)
    return pieces.reshape(-1, levels * WIN_LAT * WIN_LON, features)

def from_windows(windows, shape):
    micro_count, levels, lat_rows, lon_cols = shape
    features = windows.shape[-1]
    pieces = windows.reshape(micro_count, lat_rows // WIN_LAT, lon_cols // WIN_LON, levels, WIN_LAT, WIN_LON, features)
    pieces = pieces.transpose(0, 3, 1, 4, 2, 5, 6)
    return pieces.reshape(micro_count, levels, lat_rows, lon_cols, features)

def offset_index():
    token = jnp.arange(WT, dtype=jnp.int32)
    level = token // (WIN_LAT * WIN_LON)
    row_of = token // WIN_LON % WIN_LAT
    col_of = token % WIN_LON
    off_level = level[:, None] - level[None, :] + (LEV - 1)
    off_row = row_of[:, None] - row_of[None, :] + (WIN_LAT - 1)
    off_col = col_of[:, None] - col_of[None, :] + (WIN_LON - 1)
    return ((off_level * (2 * WIN_LAT - 1) + off_row) * (2 * WIN_LON - 1) + off_col).astype(jnp.int32)

def pair_bias(table):
    return jnp.take(table, offset_index(), axis=1)

def attend(projected, table, allowed):
    window_count, window_len = (projected.shape[0], projected.shape[1])
    pieces = projected.reshape(window_count, window_len, 3, HEADS, HEAD_DIM).astype(jnp.float32)
    queries, key_part, value_part = (pieces[:, :, 0], pieces[:, :, 1], pieces[:, :, 2])
    scores = jnp.einsum('wqhd,wkhd->whqk', queries, key_part) * HEAD_DIM ** (-0.5)
    scores = jnp.where(allowed[:, None], scores + pair_bias(table)[None], MASKED)
    peak = lax.stop_gradient(lax.optimization_barrier(jnp.max(scores, axis=-1, keepdims=True)))
    weights = jnp.exp(scores - peak)
    chances = (weights / lax.optimization_barrier(jnp.sum(weights, axis=-1, keepdims=True))).astype(jnp.bfloat16)
    context = jnp.einsum('whqk,wkhd->wqhd', chances.astype(jnp.float32), value_part)
    return context.reshape(window_count, window_len, HEADS * HEAD_DIM).astype(jnp.bfloat16)

def block_core(moved, proj_one, proj_two, table, allowed):
    features = moved.shape[-1]
    normal = normed(moved).reshape(-1, features)
    projected = jnp.dot(normal, proj_one, preferred_element_type=jnp.float32).astype(jnp.bfloat16)
    windows = to_windows(projected.reshape(moved.shape[:4] + (3 * features,)))
    context = from_windows(attend(windows, table, allowed), moved.shape[:4]).reshape(-1, features)
    mixed = jnp.dot(context, proj_two, preferred_element_type=jnp.float32)
    result = (moved.reshape(-1, features).astype(jnp.float32) + mixed).astype(jnp.bfloat16)
    return result.reshape(moved.shape)

def block_grad(moved, grad_out, proj_one, proj_two, table, allowed):
    features = moved.shape[-1]
    normal, norm_back = jax.vjp(normed, moved)
    normal_flat = normal.reshape(-1, features)
    projected = jnp.dot(normal_flat, proj_one, preferred_element_type=jnp.float32).astype(jnp.bfloat16)
    windows = to_windows(projected.reshape(moved.shape[:4] + (3 * features,)))

    def attend_open(part_in, table_in):
        return attend(part_in, table_in, allowed)
    context_win, attend_back = jax.vjp(attend_open, windows, table)
    context = from_windows(context_win, moved.shape[:4]).reshape(-1, features)
    grad_flat = grad_out.reshape(-1, features)
    grad_context = lax.dot_general(grad_flat, proj_two, (((1,), (1,)), ((), ())), preferred_element_type=jnp.float32).astype(jnp.bfloat16)
    grad_windows, grad_offsets = attend_back(to_windows(grad_context.reshape(moved.shape)))
    grad_proj = from_windows(grad_windows, moved.shape[:4]).reshape(-1, 3 * features)
    grad_normal = lax.dot_general(grad_proj, proj_one, (((1,), (1,)), ((), ())), preferred_element_type=jnp.float32).astype(jnp.bfloat16)
    grad_norm_in = norm_back(grad_normal.reshape(moved.shape))[0]
    grad_moved = (grad_out.astype(jnp.float32) + grad_norm_in.astype(jnp.float32)).astype(jnp.bfloat16)
    return (grad_moved, normal_flat, grad_proj, context, grad_flat, grad_offsets)

def window_mask(section_id, tile_kinds, micro_count):
    kinds = jnp.tile(tile_kinds[section_id].reshape(-1), micro_count)
    token = jnp.arange(WT, dtype=jnp.int32)
    low_row = token // WIN_LON % WIN_LAT < WIN_LAT // 2
    low_col = token % WIN_LON < WIN_LON // 2
    row_same = low_row[:, None] == low_row[None, :]
    col_same = low_col[:, None] == low_col[None, :]
    split_rows = (kinds % 2 == 1)[:, None, None]
    split_cols = (kinds // 2 == 1)[:, None, None]
    return (row_same[None] | ~split_rows) & (col_same[None] | ~split_cols)

def weight_sums(normal_flat, grad_proj, context, grad_flat):
    into = lax.dot_general(normal_flat, grad_proj, (((0,), (0,)), ((), ())), preferred_element_type=jnp.float32)
    outof = lax.dot_general(context, grad_flat, (((0,), (0,)), ((), ())), preferred_element_type=jnp.float32)
    return jnp.concatenate([into, outof], axis=1)

def reference(boundary, tile_kinds, proj_in, proj_out, offset_bias):
    inputs = boundary[0]
    grad_top = boundary[1]
    forth = (-(WIN_LAT // 2), -(WIN_LON // 2))
    backs = (WIN_LAT // 2, WIN_LON // 2)
    allowed_one = window_mask(0, tile_kinds, MICRO)
    allowed_two = window_mask(1, tile_kinds, MICRO)
    first_out = block_core(inputs, proj_in[0], proj_out[0], offset_bias[0], allowed_one)
    moved_two = jnp.roll(first_out, forth, axis=(2, 3))
    second_out = jnp.roll(block_core(moved_two, proj_in[1], proj_out[1], offset_bias[1], allowed_two), backs, axis=(2, 3))
    grad_moved_two, normal_two, proj_grad_two, context_two, flat_two, table_two = block_grad(moved_two, jnp.roll(grad_top, forth, axis=(2, 3)), proj_in[1], proj_out[1], offset_bias[1], allowed_two)
    grad_first = jnp.roll(grad_moved_two, backs, axis=(2, 3))
    grad_inputs, normal_one, proj_grad_one, context_one, flat_one, table_one = block_grad(inputs, grad_first, proj_in[0], proj_out[0], offset_bias[0], allowed_one)
    weight_grads = jnp.stack([weight_sums(normal_one, proj_grad_one, context_one, flat_one), weight_sums(normal_two, proj_grad_two, context_two, flat_two)])
    bias_grads = jnp.stack([table_one, table_two])
    boundary_out = jnp.stack([grad_inputs, second_out])
    return (boundary_out, weight_grads, bias_grads)
```

```python
import functools

import jax
import jax.numpy as jnp
import numpy as np
from jax import lax
from jax.experimental import pallas as pl
from jax.experimental.pallas import tpu as pltpu
from jax.sharding import PartitionSpec as P

D = 1024
HEADS = 16
LEV = 2
MICRO = 2
WIN_LAT = 6
WIN_LON = 12
WT = 144
TOK = MICRO * WT
QT = TOK // 4
OFFSETS = 759
OPAD = 768
REACH = 384
PAIRS = HEADS // 2
GROUP = 4
BIAS_ROWS = 16
NORM_EPS = 1e-05
MASKED = -1e30
BF = jnp.bfloat16
F32 = jnp.float32
VLIMIT = 56 * 1024 * 1024

ANY = pl.BlockSpec(memory_space=pl.ANY)
VMEM = pl.BlockSpec(memory_space=pltpu.VMEM)
SMEM = pl.BlockSpec(memory_space=pltpu.SMEM)


def constants():
    tok = np.arange(WT)
    lev, row, col = tok // 72, tok // 12 % 6, tok % 12
    reach = 379 - (253 * lev + 23 * row + col)
    onehot = np.zeros((256, REACH), np.float32)
    onehot[tok, reach] = 1
    rows_differ = ((row < 3)[:, None] != (row < 3)[None, :]).astype(np.float32)
    cols_differ = ((col < 6)[:, None] != (col < 6)[None, :]).astype(np.float32)
    pick = np.zeros((4, QT, TOK), np.float32)
    for half_row in range(2):
        for half_col in range(2):
            at = 0
            for micro in range(MICRO):
                for level in range(LEV):
                    for r in range(3):
                        for c in range(6):
                            src = micro * WT + level * 72 + (3 * half_row + r) * 12 + 6 * half_col + c
                            pick[half_row * 2 + half_col, at, src] = 1
                            at += 1
    return onehot, rows_differ, cols_differ, pick


ONEHOT, ROWS_DIFFER, COLS_DIFFER, PICK = constants()
SHIFTS = [253 * (a // 6) + 23 * (a % 6) for a in range(12)]


def dot(a, b):
    return jnp.dot(a, b, preferred_element_type=F32)


def dot_nt(a, b):
    return lax.dot_general(a, b, (((1,), (1,)), ((), ())), preferred_element_type=F32)


def dot_tn(a, b):
    return lax.dot_general(a, b, (((0,), (0,)), ((), ())), preferred_element_type=F32)


def call(body, name, out_shape, in_specs, scratch, flops, nbytes):
    out_specs = jax.tree.map(lambda _: VMEM, out_shape)
    return pl.pallas_call(
        body,
        out_shape=out_shape,
        in_specs=in_specs,
        out_specs=out_specs,
        scratch_shapes=scratch,
        compiler_params=pltpu.CompilerParams(vmem_limit_bytes=VLIMIT),
        cost_estimate=pl.CostEstimate(flops=flops, bytes_accessed=nbytes, transcendentals=0),
        name=name,
    )


def shape(*dims, dtype=BF):
    return jax.ShapeDtypeStruct(dims, dtype)


def load_groups(x_ref, dst):
    for g in range(TOK // 12):
        dst[12 * g : 12 * g + 12, :] = x_ref[g].astype(F32)


def store_groups(src, out_ref):
    for g in range(TOK // 12):
        out_ref[g] = src[12 * g : 12 * g + 12, :].astype(BF)


def insert(piece_refs, pickt_ref):
    total = dot(pickt_ref[0], piece_refs[0][...])
    for q in range(1, 4):
        total = total + dot(pickt_ref[q], piece_refs[q][...])
    return total


def extract(value, pick_ref, out_refs):
    for q in range(4):
        out_refs[q][...] = dot(pick_ref[q], value).astype(BF)


def bias_body(who, kind, x_ref, table_ref, oht_ref, rdiff, cdiff, pick_ref, out_ref, c0, c1, c2, c3, xs, tab, wide, tall, edge):
    tab[...] = jnp.zeros_like(tab)
    tab[:, :OFFSETS] = table_ref[...]
    table = tab[...]
    for cq in range(12):
        near = table if cq == 0 else pltpu.roll(table, OPAD - cq, 1)
        for a in range(12):
            moved = near if SHIFTS[a] == 0 else pltpu.roll(near, OPAD - SHIFTS[a], 1)
            wide[(a * 12 + cq) * 16 : (a * 12 + cq) * 16 + 16, :] = moved[:, :REACH]
    for a in range(12):
        x = wide[a * 192 : a * 192 + 192, :]
        top = x.astype(BF)
        rest = x - top.astype(F32)
        middle = rest.astype(BF)
        low = (rest - middle.astype(F32)).astype(BF)
        got = dot(top, oht_ref[...]) + (dot(middle, oht_ref[...]) + dot(low, oht_ref[...]))
        for cq in range(12):
            rows = pl.ds(a * 12 + cq, 16, stride=WT)
            tall[rows, :] = got[cq * 16 : cq * 16 + 16, :128]
            edge[rows, :] = got[cq * 16 : cq * 16 + 16, 128:]
    split_rows = (kind[0] % 2).astype(F32)
    split_cols = (kind[0] // 2).astype(F32)
    closed = rdiff[...] * split_rows + cdiff[...] * split_cols > 0.0
    for h in range(HEADS):
        rows = slice(h * WT, h * WT + WT)
        out_ref[rows, :128] = jnp.where(closed[:, :128], MASKED, tall[rows, :])
        out_ref[rows, 128:] = jnp.where(closed[:, 128:], MASKED, edge[rows, : WT - 128])

    @pl.when(who[0] == 1)
    def _():
        load_groups(x_ref, xs)
        extract(xs[...].astype(BF), pick_ref, (c0, c1, c2, c3))


def lane_masks():
    lane = lax.broadcasted_iota(jnp.int32, (1, 128), 1)
    return (lane < 64), (lane >= 64)


def stacked(block, scale):
    low, high = lane_masks()
    one = jnp.asarray(scale, F32)
    zero = jnp.zeros((), F32)
    wide = block.astype(F32)
    return jnp.concatenate([jnp.where(low, wide * one, zero), jnp.where(high, wide * one, zero)], axis=0).astype(BF)


def norm_rows(xs, nc_ref, at, count):
    x = xs[at : at + count, :]
    mean = jnp.mean(x, axis=-1, keepdims=True)
    centered = x - mean
    var = jnp.mean(centered * centered, axis=-1, keepdims=True)
    nc_ref[at : at + count, :D] = (centered * lax.rsqrt(var + NORM_EPS)).astype(BF)


def chances_of(proj_ref, bias_ref, w, p):
    lanes = pl.ds(pl.multiple_of(p * 128, 128), 128)
    klanes = pl.ds(pl.multiple_of(D + p * 128, 128), 128)
    rows = slice(w * WT, w * WT + WT)
    qs = stacked(proj_ref[rows, lanes], 0.125)
    k = proj_ref[rows, klanes]
    s = dot_nt(qs, k) + bias_ref[pl.ds(pl.multiple_of(p * TOK, 8), TOK), :]
    peak = jnp.max(s, axis=-1, keepdims=True)
    e = jnp.exp(s - peak)
    chances = e * (1.0 / jnp.sum(e, axis=-1, keepdims=True))
    return qs, k, chances


def forward_core(xs, win, wout, bias_ref, nc_ref, proj_ref, out):
    for at in range(0, TOK, 48):
        norm_rows(xs, nc_ref, at, 48)
    for c in range(0, 3 * D, 512):
        proj_ref[:, c : c + 512] = dot(nc_ref[:, :D], win[:, c : c + 512]).astype(BF)

    @pl.loop(0, PAIRS)
    def _(p):
        vlanes = pl.ds(pl.multiple_of(2 * D + p * 128, 128), 128)
        for w in range(MICRO):
            rows = slice(w * WT, w * WT + WT)
            _, _, chances = chances_of(proj_ref, bias_ref, w, p)
            ch = chances.astype(BF)
            vs = stacked(proj_ref[rows, vlanes], 1.0)
            ctx = dot(ch[:WT], vs[:WT]) + dot(ch[WT:], vs[WT:])
            nc_ref[rows, pl.ds(pl.multiple_of(D + p * 128, 128), 128)] = ctx.astype(BF)

    for c in range(0, D, 512):
        out[:, c : c + 512] = xs[:, c : c + 512] + dot(nc_ref[:, D:], wout[:, c : c + 512])


def backward_core(who, xs, go, win, wout, bias_ref, nc_ref, proj_ref, oh_ref, late, gctx, gp, bacc, edge, fold, out):
    gctx[...] = dot_nt(go[...], wout[...]).astype(BF)
    edge[...] = jnp.zeros_like(edge)

    @pl.loop(0, PAIRS)
    def _(p):
        lanes = pl.ds(pl.multiple_of(p * 128, 128), 128)
        klanes = pl.ds(pl.multiple_of(D + p * 128, 128), 128)
        vlanes = pl.ds(pl.multiple_of(2 * D + p * 128, 128), 128)
        total = None
        for w in range(MICRO):
            rows = slice(w * WT, w * WT + WT)
            qs, k, chances = chances_of(proj_ref, bias_ref, w, p)
            dcs = stacked(gctx[rows, lanes], 1.0)
            dp = dot_nt(dcs, proj_ref[rows, vlanes])
            centre = jnp.sum(dp * chances, axis=-1, keepdims=True)
            ds = chances * (dp - centre)
            total = ds if total is None else total + ds
            dsb = ds.astype(BF)
            gp[rows, vlanes] = dot_tn(chances.astype(BF), dcs).astype(BF)
            gp[rows, klanes] = dot_tn(dsb, qs).astype(BF)
            ks = stacked(k, 0.125)
            gp[rows, lanes] = (dot(dsb[:WT], ks[:WT]) + dot(dsb[WT:], ks[WT:])).astype(BF)
        both = pl.ds(pl.multiple_of(p * TOK, 8), TOK)
        bacc[both, :] = total[:, :128]
        edge[both, : WT - 128] = total[:, 128:]

    for at in range(0, TOK, 96):
        rows = slice(at, at + 96)
        dn = dot_nt(gp[rows, :], win[...]).astype(BF).astype(F32)
        x = xs[rows, :]
        mean = jnp.mean(x, axis=-1, keepdims=True)
        centered = x - mean
        var = jnp.mean(centered * centered, axis=-1, keepdims=True)
        scale = lax.rsqrt(var + NORM_EPS)
        n = centered * scale
        along = jnp.mean(dn * n, axis=-1, keepdims=True)
        level = jnp.mean(dn, axis=-1, keepdims=True)
        dx = (scale * (dn - level - n * along)).astype(BF).astype(F32)
        out[rows, :] = go[rows, :].astype(F32) + dx

    fold[...] = jnp.zeros_like(fold)
    total = jnp.zeros((BIAS_ROWS, OPAD), F32)
    for a in range(12):
        part = jnp.zeros((BIAS_ROWS, OPAD), F32)
        taken = [pl.ds(a * 12 + cq, 16, stride=WT) for cq in range(12)]
        x = jnp.concatenate(
            [jnp.concatenate([ref[rows, :] for rows in taken], axis=0) for ref in (bacc, edge)], axis=1
        )
        top = x.astype(BF)
        low = (x - top.astype(F32)).astype(BF)
        u = dot(top, oh_ref[...]) + dot(low, oh_ref[...])
        u = jnp.concatenate([u, jnp.zeros((192, OPAD - REACH), F32)], axis=1)
        for cq in range(12):
            one = u[cq * 16 : cq * 16 + 16, :]
            part = part + (one if cq == 0 else pltpu.roll(one, cq, 1))
        total = total + (part if SHIFTS[a] == 0 else pltpu.roll(part, SHIFTS[a], 1))
    fold[:, :OPAD] = total

    for d in range(GROUP):
        j = lax.rem(who[1] + d, GROUP)
        late[d][:TOK, :OPAD] = gp[:, pl.ds(pl.multiple_of(j * 768, 128), 768)]
        late[d][:TOK, OPAD:] = go[:, pl.ds(pl.multiple_of(j * 256, 128), 256)]
        slab = fold[:, pl.ds(pl.multiple_of(j * 256, 128), 256)]
        top = slab.astype(BF)
        late[d][TOK:, :256] = top
        late[d][TOK:, 256:512] = (slab - top.astype(F32)).astype(BF)
        late[d][TOK:, 512:] = jnp.zeros((BIAS_ROWS, 512), BF)


def first_forward_body(who, x_ref, win, wout, bias_ref, pick_ref, nc_ref, proj_ref, p0, p1, p2, p3, xs, out):
    @pl.when(who[0] == 0)
    def _():
        load_groups(x_ref, xs)
        forward_core(xs, win, wout, bias_ref, nc_ref, proj_ref, out)
        extract(out[...].astype(BF), pick_ref, (p0, p1, p2, p3))


def second_body(who, r0, r1, r2, r3, c0, c1, c2, c3, win, wout, bias_ref, pick_ref, pickt_ref, oh_ref,
                nc_ref, s0, s1, s2, s3, g0, g1, g2, g3, l0, l1, l2, l3,
                xs, out, go, proj, gctx, gp, bacc, edge, fold):
    @pl.when(who[0] == 1)
    def _():
        xs[...] = insert((r0, r1, r2, r3), pickt_ref)
        go[...] = insert((c0, c1, c2, c3), pickt_ref).astype(BF)
        forward_core(xs, win, wout, bias_ref, nc_ref, proj, out)
        extract(out[...].astype(BF), pick_ref, (s0, s1, s2, s3))
        backward_core(who, xs, go, win, wout, bias_ref, nc_ref, proj, oh_ref, (l0, l1, l2, l3), gctx, gp, bacc, edge, fold, out)
        extract(out[...].astype(BF), pick_ref, (g0, g1, g2, g3))


def first_backward_body(who, x_ref, g0, g1, g2, g3, nc_ref, proj_ref, win, wout, bias_ref, pickt_ref, oh_ref,
                        out_ref, l0, l1, l2, l3, xs, out, go, gctx, gp, bacc, edge, fold):
    @pl.when(who[0] == 0)
    def _():
        load_groups(x_ref, xs)
        go[...] = insert((g0, g1, g2, g3), pickt_ref).astype(BF)
        backward_core(who, xs, go, win, wout, bias_ref, nc_ref, proj_ref, oh_ref, (l0, l1, l2, l3), gctx, gp, bacc, edge, fold, out)
        store_groups(out, out_ref)


def result_body(who, grad_ref, s0, s1, s2, s3, pickt_ref, out_ref, xs):
    @pl.when(who[0] == 0)
    def _():
        out_ref[...] = grad_ref[...]

    @pl.when(who[0] == 1)
    def _():
        xs[...] = insert((s0, s1, s2, s3), pickt_ref)
        store_groups(xs, out_ref)


def weight_body(who, *refs):
    early_a, early_b, late_a, late_b = (refs[4 * i : 4 * i + 4] for i in range(4))
    out_ref, held, grads, terms, sem = refs[16:]

    def copies(early, late):
        made = []
        for d in range(GROUP):
            rows = pl.ds(TOK * d, TOK)
            made.append(pltpu.make_async_copy(early[d], held.at[rows], sem.at[d, 0]))
            made.append(pltpu.make_async_copy(late[d].at[pl.ds(0, TOK)], grads.at[rows], sem.at[d, 1]))
            made.append(pltpu.make_async_copy(late[d].at[pl.ds(TOK, BIAS_ROWS)], terms.at[d], sem.at[d, 2]))
        return made

    @pl.when(who[0] == 0)
    def _():
        for one in copies(early_a, late_a):
            one.start()

    @pl.when(who[0] == 1)
    def _():
        for one in copies(early_b, late_b):
            one.start()

    for one in copies(early_a, late_a):
        one.wait()

    @pl.loop(0, 4)
    def _(rb):
        dst = pl.ds(pl.multiple_of(rb * 16, 16), 16)
        into = dot_tn(held[:, pl.ds(pl.multiple_of(rb * 256, 128), 256)], grads[:, :768])
        for cb in range(6):
            out_ref[dst, cb * 16 : cb * 16 + 16, :] = into[:, cb * 128 : cb * 128 + 128].astype(BF).reshape(16, 16, 128)
        outof = dot_tn(held[:, pl.ds(pl.multiple_of(D + rb * 256, 128), 256)], grads[:, 768:])
        for cb in range(2):
            out_ref[dst, 96 + cb * 16 : 112 + cb * 16, :] = outof[:, cb * 128 : cb * 128 + 128].astype(BF).reshape(16, 16, 128)

    slab = jnp.zeros((BIAS_ROWS, 256), F32)
    for d in range(GROUP):
        slab = slab + (terms[d, :, :256].astype(F32) + terms[d, :, 256:512].astype(F32))
    for half in range(2):
        piece = slab[:, half * 128 : half * 128 + 128].astype(BF)
        out_ref[:, 128 + half * 16 : 144 + half * 16, :] = jnp.broadcast_to(piece[None], (64, BIAS_ROWS, 128))


def sum_body(in_ref, w_ref, b_ref, bias):
    for z in range(GROUP):
        total = None
        for outer in range(8):
            for lon in range(2):
                one = in_ref[(outer * 4 + z) * 2 + lon].astype(F32)
                total = one if total is None else total + one
        for cb in range(6):
            w_ref[:, z * 768 + cb * 128 : z * 768 + cb * 128 + 128] = total[cb * 16 : cb * 16 + 16]
        for cb in range(2):
            at = 3 * D + z * 256 + cb * 128
            w_ref[:, at : at + 128] = total[96 + cb * 16 : 112 + cb * 16]
            bias[:, z * 256 + cb * 128 : z * 256 + cb * 128 + 128] = total[128 + cb * 16 : 144 + cb * 16]
    b_ref[...] = bias[:, :OFFSETS]


def per_device(boundary, tile_kinds, proj_in, proj_out, offset_bias):
    axes = ("lat", "lon", "section")
    nlat, nlon = lax.axis_size("lat"), lax.axis_size("lon")
    section = lax.axis_index("section")
    depth = lax.axis_index("lat") % GROUP
    who = jnp.stack([section, depth]).astype(jnp.int32)
    kind = tile_kinds.reshape(1)
    x = boundary.reshape(TOK // 12, 12, D)
    win = proj_in[0]
    wout = proj_out[0]
    onehot = jnp.asarray(ONEHOT, BF)
    onehot_t = jnp.asarray(ONEHOT.T, BF)
    pick = jnp.asarray(PICK, BF)
    pick_t = jnp.asarray(PICK.transpose(0, 2, 1), BF)

    def flat(lat, lon, sec):
        return ((lat % nlat) * nlon + lon % nlon) * 2 + sec

    def roll_pairs(dl, dn, from_section, to_section):
        return [
            (flat(i, j, from_section), flat(i + dl, j + dn, to_section))
            for i in range(nlat)
            for j in range(nlon)
        ]

    def ring_pairs(step, sections):
        return [
            (flat(i, j, s), flat(i - i % GROUP + (i + step) % GROUP, j, s))
            for i in range(nlat)
            for j in range(nlon)
            for s in sections
        ]

    def forth(pieces, src, dst):
        got = []
        for dl in range(2):
            for dn in range(2):
                piece = pieces[(1 - dl) * 2 + (1 - dn)]
                if src == dst and dl == 0 and dn == 0:
                    got.append(piece)
                else:
                    got.append(lax.ppermute(piece, axes, roll_pairs(-dl, -dn, src, dst)))
        return got

    def back(pieces, src, dst):
        got = [None] * 4
        for dl in range(2):
            for dn in range(2):
                piece = pieces[dl * 2 + dn]
                if not (src == dst and dl == 0 and dn == 0):
                    piece = lax.ppermute(piece, axes, roll_pairs(dl, dn, src, dst))
                got[(1 - dl) * 2 + (1 - dn)] = piece
        return got

    def round_ring(values, sections):
        return [values[0]] + [
            lax.ppermute(values[d], axes, ring_pairs(d, sections)) for d in range(1, GROUP)
        ]

    quarter = [shape(QT, D)] * 4
    late = [shape(TOK + BIAS_ROWS, D)] * 4
    f32 = functools.partial(shape, dtype=F32)
    vf32 = lambda *dims: pltpu.VMEM(dims, F32)
    vbf = lambda *dims: pltpu.VMEM(dims, BF)

    bias, *cots = call(
        bias_body, "bias_table", [f32(HEADS * WT, WT)] + quarter,
        [SMEM, SMEM] + [VMEM] * 6,
        [vf32(TOK, D), vf32(HEADS, OPAD), vf32(12 * 192, REACH), vf32(HEADS * WT, 128), vf32(HEADS * WT, 128)], 2_000_000_000, 4_000_000,
    )(who, kind, x, offset_bias[0], onehot_t, jnp.asarray(ROWS_DIFFER), jnp.asarray(COLS_DIFFER), pick)
    cots = forth(cots, 1, 1)

    nc_a, proj_a, *pieces = call(
        first_forward_body, "first_forward", [shape(TOK, 2 * D), shape(TOK, 3 * D)] + quarter,
        [SMEM] + [VMEM] * 5,
        [vf32(TOK, D), vf32(TOK, D)], 3_000_000_000, 20_000_000,
    )(who, x, win, wout, bias, pick)
    received = forth(pieces, 0, 1)
    received, nc_a = lax.optimization_barrier((received, nc_a))
    early_a = round_ring([nc_a] * 4, (0,))

    back_scratch = [vbf(TOK, D), vbf(TOK, 3 * D), vf32(HEADS * WT, 128), vf32(HEADS * WT, 128), vf32(BIAS_ROWS, D)]
    nc_b, *more = call(
        second_body, "second_both", [shape(TOK, 2 * D)] + quarter * 2 + late,
        [SMEM] + [VMEM] * 14,
        [vf32(TOK, D), vf32(TOK, D), vbf(TOK, D), vbf(TOK, 3 * D)] + back_scratch, 9_000_000_000, 20_000_000,
    )(who, *received, *cots, win, wout, bias, pick, pick_t, onehot)
    second_out, grads, late_b = more[:4], more[4:8], more[8:]
    grads = back(grads, 1, 0)
    grads, second_out, late_b, nc_b = lax.optimization_barrier((grads, second_out, late_b, nc_b))
    late_b = round_ring(late_b, (1,))
    early_b = round_ring([nc_b] * 4, (1,))
    second_out = back(second_out, 1, 1)

    grad_in, *late_a = call(
        first_backward_body, "first_backward", [shape(TOK // 12, 12, D)] + late,
        [SMEM] + [VMEM] * 12,
        [vf32(TOK, D), vf32(TOK, D), vbf(TOK, D)] + back_scratch, 6_000_000_000, 20_000_000,
    )(who, x, *grads, nc_a, proj_a, win, wout, bias, pick_t, onehot)
    late_a = round_ring(late_a, (0,))

    result = call(
        result_body, "result", shape(TOK // 12, 12, D), [SMEM] + [VMEM] * 6, [vf32(TOK, D)], 170_000_000, 2_000_000,
    )(who, grad_in, *second_out, pick_t)

    terms = call(
        weight_body, "weight_terms", shape(64, 160, 128), [SMEM] + [ANY] * 16,
        [vbf(GROUP * TOK, 2 * D), vbf(GROUP * TOK, D), vbf(GROUP, BIAS_ROWS, D), pltpu.SemaphoreType.DMA((GROUP, 3))],
        2_400_000_000, 10_000_000,
    )(who, *early_a, *early_b, *late_a, *late_b)
    terms = lax.all_to_all(terms, ("lat", "lon"), 0, 0, tiled=True)

    weights, table = call(
        sum_body, "sum_terms", [f32(16, 4 * D), f32(HEADS, OFFSETS)], [VMEM], [vf32(HEADS, D)], 3_000_000, 3_000_000,
    )(terms)
    return (result.reshape(boundary.shape), weights[None], table[None])


def solution(mesh):
    return jax.shard_map(
        per_device,
        mesh=mesh,
        in_specs=(
            P("section", None, None, "lat", "lon", None),
            P("section", "lat", "lon"),
            P("section", None, None),
            P("section", None, None),
            P("section", None, None),
        ),
        out_specs=(
            P("section", None, None, "lat", "lon", None),
            P("section", ("lat", "lon"), None),
            P("section", None, None),
        ),
        check_vma=False,
    )
```

```python
import functools

import jax
import jax.numpy as jnp
import numpy as np
from jax import lax
from jax.experimental import pallas as pl
from jax.experimental.pallas import tpu as pltpu
from jax.sharding import PartitionSpec as P

D = 1024
HEADS = 16
LEV = 2
MICRO = 2
WIN_LAT = 6
WIN_LON = 12
WT = 144
TOK = MICRO * WT
QT = TOK // 4
OFFSETS = 759
OPAD = 768
LEVEL_STEP = 253
ROW_STEP = 23
PAIRS = HEADS // 2
GROUP = 4
BIAS_ROWS = 16
NORM_EPS = 1e-05
MASKED = -1e30
BF = jnp.bfloat16
F32 = jnp.float32
VLIMIT = 58 * 1024 * 1024
SMALL = 24 * 1024 * 1024

HBM = pl.BlockSpec(memory_space=pltpu.HBM)
VMEM = pl.BlockSpec(memory_space=pltpu.VMEM)
SMEM = pl.BlockSpec(memory_space=pltpu.SMEM)


def constants():
    tok = np.arange(WT)
    lev, row, col = tok // 72, tok // 12 % 6, tok % 12
    onehot = np.zeros((256, 256), np.float32)
    onehot[tok, 128 * lev + 126 - 23 * row - col] = 1
    rows_differ = ((row < 3)[:, None] != (row < 3)[None, :]).astype(np.float32)
    cols_differ = ((col < 6)[:, None] != (col < 6)[None, :]).astype(np.float32)
    pick = np.zeros((4, QT, TOK), np.float32)
    for half_row in range(2):
        for half_col in range(2):
            at = 0
            for micro in range(MICRO):
                for level in range(LEV):
                    for r in range(3):
                        for c in range(6):
                            src = micro * WT + level * 72 + (3 * half_row + r) * 12 + 6 * half_col + c
                            pick[half_row * 2 + half_col, at, src] = 1
                            at += 1
    return onehot, rows_differ, cols_differ, pick


ONEHOT, ROWS_DIFFER, COLS_DIFFER, PICK = constants()


def dot(a, b):
    return jnp.dot(a, b, preferred_element_type=F32)


def dot_nt(a, b):
    return lax.dot_general(a, b, (((1,), (1,)), ((), ())), preferred_element_type=F32)


def dot_tn(a, b):
    return lax.dot_general(a, b, (((0,), (0,)), ((), ())), preferred_element_type=F32)


def call(body, name, out_shape, in_specs, scratch, flops, nbytes, out_specs=None, limit=VLIMIT):
    if out_specs is None:
        out_specs = jax.tree.map(lambda _: VMEM, out_shape)
    return pl.pallas_call(
        body,
        out_shape=out_shape,
        in_specs=in_specs,
        out_specs=out_specs,
        scratch_shapes=scratch,
        compiler_params=pltpu.CompilerParams(vmem_limit_bytes=limit),
        cost_estimate=pl.CostEstimate(flops=flops, bytes_accessed=nbytes, transcendentals=0),
        name=name,
    )


def begin(src, dst, sem):
    copy = pltpu.make_async_copy(src, dst, sem)
    copy.start()
    return copy


def begin_weights(win, wout, win_v, wout_v, sem):
    made = []
    for i in range(6):
        cols = pl.ds(512 * i, 512)
        made.append(begin(win.at[:, cols], win_v.at[:, cols], sem.at[i]))
    made.append(begin(wout, wout_v, sem.at[6]))
    return made


def shape(*dims, dtype=BF):
    return jax.ShapeDtypeStruct(dims, dtype)


def load_groups(x_ref, dst):
    for g in range(TOK // 12):
        dst[12 * g : 12 * g + 12, :] = x_ref[g].astype(F32)


def store_groups(src, out_ref):
    for g in range(TOK // 12):
        out_ref[g] = src[12 * g : 12 * g + 12, :].astype(BF)


def insert(piece_refs, pickt_ref):
    total = dot(pickt_ref[0], piece_refs[0][...])
    for q in range(1, 4):
        total = total + dot(pickt_ref[q], piece_refs[q][...])
    return total


def extract(value, pick_ref, out_refs):
    for q in range(4):
        out_refs[q][...] = dot(pick_ref[q], value).astype(BF)


def build_bias(kind, table_ref, oht_ref, rdiff, cdiff, out, tab, tops, mids, lows, tall, edge):
    tab[...] = jnp.zeros_like(tab)
    tab[:, :OFFSETS] = table_ref[...]
    for dl in range(3):
        for rq in range(6):
            for cq in range(12):
                start = LEVEL_STEP * dl + ROW_STEP * rq + cq
                at = ((dl * 6 + rq) * 12 + cq) * 16
                x = tab[:, start : start + 128]
                top = x.astype(BF)
                rest = x - top.astype(F32)
                mid = rest.astype(BF)
                tops[at : at + 16, :] = top
                mids[at : at + 16, :] = mid
                lows[at : at + 16, :] = (rest - mid.astype(F32)).astype(BF)
    for lq in range(2):
        for rq in range(6):
            one = ((1 + lq) * 6 + rq) * 192
            two = (lq * 6 + rq) * 192
            got = None
            for piece in (tops, mids, lows):
                x = jnp.concatenate([piece[one : one + 192, :], piece[two : two + 192, :]], axis=1)
                part = dot(x, oht_ref[...])
                got = part if got is None else got + part
            for cq in range(12):
                rows = pl.ds((lq * 6 + rq) * 12 + cq, 16, stride=WT)
                tall[rows, :] = got[cq * 16 : cq * 16 + 16, :128]
                edge[rows, :] = got[cq * 16 : cq * 16 + 16, 128:]
    split_rows = (kind[0] % 2).astype(F32)
    split_cols = (kind[0] // 2).astype(F32)
    closed = rdiff[...] * split_rows + cdiff[...] * split_cols > 0.0
    for h in range(HEADS):
        rows = slice(h * WT, h * WT + WT)
        out[rows, :128] = jnp.where(closed[:, :128], MASKED, tall[rows, :])
        out[rows, 128:] = jnp.where(closed[:, 128:], MASKED, edge[rows, : WT - 128])


def head_masks(scale):
    lane = lax.broadcasted_iota(jnp.int32, (1, 128), 1)
    low = jnp.where(lane < 64, scale, 0.0).astype(BF)
    high = jnp.where(lane >= 64, scale, 0.0).astype(BF)
    return low, high


def stacked(block, masks):
    return jnp.concatenate([block * masks[0], block * masks[1]], axis=0)


def norm_rows(xs, n_ref, at, count):
    x = xs[at : at + count, :]
    mean = jnp.mean(x, axis=-1, keepdims=True)
    centered = x - mean
    var = jnp.mean(centered * centered, axis=-1, keepdims=True)
    n_ref[at : at + count, :] = (centered * lax.rsqrt(var + NORM_EPS)).astype(BF)


def pair_lanes(p, base):
    return pl.ds(pl.multiple_of(base + p * 128, 128), 128)


def pair_rows(p):
    return pl.ds(pl.multiple_of(p * TOK, 8), TOK)


def forward_core(xs, win, wout, bias_ref, n_ref, c_ref, proj_ref, aug_ref, out, weights, bias_ready, made):
    for at in range(0, TOK, 48):
        norm_rows(xs, n_ref, at, 48)
    made("n")
    for i in range(6):
        weights[i].wait()
        cols = slice(512 * i, 512 * i + 512)
        proj_ref[:, cols] = dot(n_ref[...], win[:, cols]).astype(BF)
    made("proj")
    bias_ready()

    @pl.loop(0, PAIRS)
    def _(p):
        eighth = head_masks(0.125)
        ones = head_masks(1.0)
        lane = lax.broadcasted_iota(jnp.int32, (1, 128), 1)
        spot = lane % 64
        for w in range(MICRO):
            rows = slice(w * WT, w * WT + WT)
            qs = stacked(proj_ref[rows, pair_lanes(p, 0)], eighth)
            k = proj_ref[rows, pair_lanes(p, D)]
            v = proj_ref[rows, pair_lanes(p, 2 * D)]
            s = dot_nt(qs, k) + bias_ref[pair_rows(p), :]
            peak = jnp.max(s, axis=-1, keepdims=True)
            e = jnp.exp(s - peak).astype(BF)
            wide = [
                jnp.concatenate([v * one, jnp.broadcast_to(one, (WT, 128))], axis=1) for one in ones
            ]
            both = dot(e[:WT], wide[0]) + dot(e[WT:], wide[1])
            total = both[:, 128:]
            c_ref[rows, pair_lanes(p, 0)] = (both[:, :128] / total).astype(BF)
            lse = jnp.where(lane < 64, peak[:WT], peak[WT:]) + jnp.log(total)
            top = lse.astype(BF).astype(F32)
            mid = (lse - top).astype(BF).astype(F32)
            low = lse - top - mid
            aug = jnp.where(spot == 0, -top, jnp.where(spot == 1, -mid, jnp.where(spot == 2, -low, 0.0)))
            aug_ref[pl.ds(pl.multiple_of((p * 2 + w) * TOK, 16), TOK), :] = stacked(aug.astype(BF), ones)

    made("c")
    weights[6].wait()
    for c in range(0, D, 512):
        out[:, c : c + 512] = xs[:, c : c + 512] + dot(c_ref[...], wout[:, c : c + 512])


def backward_core(who, xs, go, win, wout, bias_ref, c_ref, proj_ref, aug_ref, oh_ref, gctx, gp, bacc, edge, fold, terms, out,
                  weights, ready, late_ref, late_sem):
    sent = []
    part = [lax.rem(who[1] + step, GROUP) for step in range(GROUP)]
    for step in range(GROUP):
        cols = pl.ds(pl.multiple_of(256 * part[step], 128), 256)
        sent.append(begin(go.at[:, cols], late_ref[step].at[pl.ds(0, TOK), pl.ds(768, 256)], late_sem.at[step, 0]))
    if weights:
        weights[6].wait()
    for c in range(0, D, 256):
        gctx[:, c : c + 256] = dot_nt(go[...], wout[c : c + 256, :]).astype(BF)
    edge[...] = jnp.zeros_like(edge)
    ready()

    @pl.loop(0, PAIRS)
    def _(p):
        eighth = head_masks(0.125)
        ones = head_masks(1.0)
        lane = lax.broadcasted_iota(jnp.int32, (1, 128), 1)
        fill = jnp.broadcast_to(jnp.where(lane % 64 < 3, 1.0, 0.0).astype(BF), (WT, 128))
        full = jnp.ones((WT, 128), BF)
        total = None
        for w in range(MICRO):
            rows = slice(w * WT, w * WT + WT)
            qs = stacked(proj_ref[rows, pair_lanes(p, 0)], eighth)
            k = proj_ref[rows, pair_lanes(p, D)]
            v = proj_ref[rows, pair_lanes(p, 2 * D)]
            aug = aug_ref[pl.ds(pl.multiple_of((p * 2 + w) * TOK, 16), TOK), :]
            s = dot_nt(jnp.concatenate([qs, aug], axis=1), jnp.concatenate([k, fill], axis=1))
            chances = jnp.exp(s + bias_ref[pair_rows(p), :])
            dc = gctx[rows, pair_lanes(p, 0)]
            dcs = stacked(dc, ones)
            along = -(dc.astype(F32) * c_ref[rows, pair_lanes(p, 0)].astype(F32))
            alongs = stacked(along.astype(BF), ones)
            slope = dot_nt(jnp.concatenate([dcs, alongs], axis=1), jnp.concatenate([v, full], axis=1))
            ds = chances * slope
            total = ds if total is None else total + ds
            dsb = ds.astype(BF)
            gp[rows, pair_lanes(p, 2 * D)] = dot_tn(chances.astype(BF), dcs).astype(BF)
            gp[rows, pair_lanes(p, D)] = dot_tn(dsb, qs).astype(BF)
            ks = [k * one for one in eighth]
            gp[rows, pair_lanes(p, 0)] = (dot(dsb[:WT], ks[0]) + dot(dsb[WT:], ks[1])).astype(BF)
        bacc[pair_rows(p), :] = total[:, :128]
        edge[pair_rows(p), : WT - 128] = total[:, 128:]

    for step in range(GROUP):
        cols = pl.ds(pl.multiple_of(768 * part[step], 128), 768)
        sent.append(begin(gp.at[:, cols], late_ref[step].at[pl.ds(0, TOK), pl.ds(0, 768)], late_sem.at[step, 1]))

    acc = [jnp.zeros((BIAS_ROWS, 256), F32) for _ in range(3)]
    blank = jnp.zeros((BIAS_ROWS, 128), F32)
    for rq in range(6):
        got = []
        for lq in range(2):
            taken = [pl.ds((lq * 6 + rq) * 12 + cq, 16, stride=WT) for cq in range(12)]
            x = jnp.concatenate(
                [jnp.concatenate([ref[rows, :] for rows in taken], axis=0) for ref in (bacc, edge)], axis=1
            )
            top = x.astype(BF)
            low = (x - top.astype(F32)).astype(BF)
            got.append(dot(top, oh_ref[...]) + dot(low, oh_ref[...]))
        levels = [got[0][:, 128:], got[0][:, :128] + got[1][:, 128:], got[1][:, :128]]
        for dl in range(3):
            for cq in range(12):
                one = jnp.concatenate([levels[dl][cq * 16 : cq * 16 + 16], blank], axis=1)
                shift = ROW_STEP * rq + cq
                acc[dl] = acc[dl] + (pltpu.roll(one, shift, 1) if shift else one)
    folded = jnp.zeros((BIAS_ROWS, D), F32)
    for dl in range(3):
        one = jnp.concatenate([acc[dl], jnp.zeros((BIAS_ROWS, D - 256), F32)], axis=1)
        folded = folded + (pltpu.roll(one, LEVEL_STEP * dl, 1) if dl else one)
    fold[...] = folded
    for step in range(GROUP):
        slab = fold[:, pl.ds(pl.multiple_of(256 * part[step], 128), 256)]
        top = slab.astype(BF)
        terms[step, :, :256] = top
        terms[step, :, 256:512] = (slab - top.astype(F32)).astype(BF)
        terms[step, :, 512:] = jnp.zeros((BIAS_ROWS, 512), BF)
        sent.append(begin(terms.at[step], late_ref[step].at[pl.ds(TOK, BIAS_ROWS), :], late_sem.at[step, 2]))

    if weights:
        for i in range(6):
            weights[i].wait()
    for c in range(0, D, 256):
        out[:, c : c + 256] = dot_nt(gp[...], win[c : c + 256, :]).astype(BF).astype(F32)
    for at in range(0, TOK, 48):
        rows = slice(at, at + 48)
        dn = out[rows, :]
        x = xs[rows, :]
        mean = jnp.mean(x, axis=-1, keepdims=True)
        centered = x - mean
        var = jnp.mean(centered * centered, axis=-1, keepdims=True)
        scale = lax.rsqrt(var + NORM_EPS)
        n = centered * scale
        along = jnp.mean(dn * n, axis=-1, keepdims=True)
        level = jnp.mean(dn, axis=-1, keepdims=True)
        dx = (scale * (dn - level - n * along)).astype(BF).astype(F32)
        out[rows, :] = go[rows, :].astype(F32) + dx
    return sent


def first_forward_body(who, kind, x_ref, table_ref, oht_ref, rdiff, cdiff, pick_ref, win, wout,
                       bias_out, nc_out, proj_out, aug_out, p0, p1, p2, p3,
                       win_v, wout_v, bias_v, n, c, proj, aug, xs, out, tab, tops, mids, lows, tall, edge, wsem, osem):
    @pl.when(who[0] == 0)
    def _():
        begin_weights(win, wout, win_v, wout_v, wsem)

    build_bias(kind, table_ref, oht_ref, rdiff, cdiff, bias_v, tab, tops, mids, lows, tall, edge)
    bias_copy = begin(bias_v, bias_out, osem.at[4])

    @pl.when(who[0] == 0)
    def _():
        weights = [
            pltpu.make_async_copy(win.at[:, pl.ds(512 * i, 512)], win_v.at[:, pl.ds(512 * i, 512)], wsem.at[i])
            for i in range(6)
        ] + [pltpu.make_async_copy(wout, wout_v, wsem.at[6])]
        load_groups(x_ref, xs)
        sent = []

        def made(name):
            if name == "n":
                sent.append(begin(n, nc_out.at[:, pl.ds(0, D)], osem.at[0]))
            if name == "proj":
                sent.append(begin(proj, proj_out, osem.at[1]))
            if name == "c":
                sent.append(begin(c, nc_out.at[:, pl.ds(D, D)], osem.at[2]))
                sent.append(begin(aug, aug_out, osem.at[3]))

        forward_core(xs, win_v, wout_v, bias_v, n, c, proj, aug, out, weights, lambda: None, made)
        extract(out[...].astype(BF), pick_ref, (p0, p1, p2, p3))
        for one in sent:
            one.wait()

    @pl.when(who[0] == 1)
    def _():
        load_groups(x_ref, xs)
        extract(xs[...].astype(BF), pick_ref, (p0, p1, p2, p3))

    bias_copy.wait()


def second_body(who, r0, r1, r2, r3, c0, c1, c2, c3, pick_ref, pickt_ref, oh_ref, bias_ref, win, wout,
                nc_out, l0, l1, l2, l3, s0, s1, s2, s3, g0, g1, g2, g3,
                win_v, wout_v, bias_v, c, proj, aug, xs, out, go, gctx, gp, bacc, edge, fold, terms,
                wsem, isem, lsem, n):
    @pl.when(who[0] == 1)
    def _():
        weights = begin_weights(win, wout, win_v, wout_v, wsem)
        bias_copy = begin(bias_ref, bias_v, isem.at[0])
        xs[...] = insert((r0, r1, r2, r3), pickt_ref)
        sent = []

        def made(name):
            if name == "n":
                sent.append(begin(n, nc_out.at[:, pl.ds(0, D)], isem.at[1]))
            if name == "c":
                sent.append(begin(c, nc_out.at[:, pl.ds(D, D)], isem.at[2]))

        forward_core(xs, win_v, wout_v, bias_v, n, c, proj, aug, out, weights, bias_copy.wait, made)
        extract(out[...].astype(BF), pick_ref, (s0, s1, s2, s3))
        go[...] = insert((c0, c1, c2, c3), pickt_ref).astype(BF)
        sent += backward_core(who, xs, go, win_v, wout_v, bias_v, c, proj, aug, oh_ref, gctx, gp, bacc, edge, fold, terms,
                              out, None, lambda: None, (l0, l1, l2, l3), lsem)
        extract(out[...].astype(BF), pick_ref, (g0, g1, g2, g3))
        for one in sent:
            one.wait()


def first_backward_body(who, x_ref, g0, g1, g2, g3, pickt_ref, oh_ref,
                        nc_ref, proj_ref, aug_ref, bias_ref, win, wout, b0, b1, b2, b3,
                        l0, l1, l2, l3, out_ref,
                        win_v, wout_v, bias_v, c, proj, aug, xs, out, go, gctx, gp, bacc, edge, fold, terms,
                        wsem, isem, lsem, hold):
    @pl.when(who[0] == 0)
    def _():
        weights = [None] * 7
        weights[6] = begin(wout, wout_v, wsem.at[6])
        copies = [
            begin(proj_ref, proj, isem.at[0]),
            begin(bias_ref, bias_v, isem.at[1]),
            begin(aug_ref, aug, isem.at[2]),
            begin(nc_ref.at[:, pl.ds(D, D)], c, isem.at[3]),
        ]
        for i in range(6):
            cols = pl.ds(512 * i, 512)
            weights[i] = begin(win.at[:, cols], win_v.at[:, cols], wsem.at[i])
        go[...] = insert((g0, g1, g2, g3), pickt_ref).astype(BF)
        load_groups(x_ref, xs)

        def ready():
            for one in copies:
                one.wait()

        sent = backward_core(who, xs, go, win_v, wout_v, bias_v, c, proj, aug, oh_ref, gctx, gp, bacc, edge, fold, terms,
                             out, weights, ready, (l0, l1, l2, l3), lsem)
        store_groups(out, out_ref)
        for one in sent:
            one.wait()

    @pl.when(who[0] == 1)
    def _():
        came = [begin(src, hold.at[j], lsem.at[j, 0]) for j, src in enumerate((b0, b1, b2, b3))]
        gone = []
        for j, dst in enumerate((l0, l1, l2, l3)):
            came[j].wait()
            gone.append(begin(hold.at[j], dst, lsem.at[j, 1]))
        for one in gone:
            one.wait()


def result_body(who, grad_ref, s0, s1, s2, s3, pickt_ref, out_ref, xs):
    @pl.when(who[0] == 0)
    def _():
        out_ref[...] = grad_ref[...]

    @pl.when(who[0] == 1)
    def _():
        xs[...] = insert((s0, s1, s2, s3), pickt_ref)
        store_groups(xs, out_ref)


def flip_body(who, *refs):
    early_a, early_b = refs[:GROUP], refs[GROUP : 2 * GROUP]
    out_ref, held, flipped, sem, osem = refs[2 * GROUP :]

    def copies(early):
        return [
            pltpu.make_async_copy(early[j], held.at[pl.ds(TOK * j, TOK)], sem.at[j]) for j in range(GROUP)
        ]

    @pl.when(who[0] == 0)
    def _():
        for one in copies(early_a):
            one.start()

    @pl.when(who[0] == 1)
    def _():
        for one in copies(early_b):
            one.start()

    for one in copies(early_a):
        one.wait()

    @pl.loop(0, 8)
    def _(i):
        at = pl.ds(pl.multiple_of(i * 256, 256), 256)
        flipped[at, :] = held[:, at].T
        pltpu.make_async_copy(flipped.at[at], out_ref.at[at], osem.at[i]).start()

    for i in range(8):
        at = pl.ds(i * 256, 256)
        pltpu.make_async_copy(flipped.at[at], out_ref.at[at], osem.at[i]).wait()


def weight_body(nct_ref, l0, l1, l2, l3, out_ref, nct, grads, terms, lsem, nsem):
    late = (l0, l1, l2, l3)
    copies = []
    for j in range(GROUP):
        copies.append(begin(late[j].at[pl.ds(0, TOK)], grads.at[pl.ds(TOK * j, TOK)], lsem.at[j, 0]))
        copies.append(begin(late[j].at[pl.ds(TOK, BIAS_ROWS)], terms.at[j], lsem.at[j, 1]))
    chunks = []
    for rb in range(4):
        for base in (0, D):
            rows = pl.ds(base + 256 * rb, 256)
            chunks.append(begin(nct_ref.at[rows], nct.at[rows], nsem.at[len(chunks)]))
    for one in copies:
        one.wait()

    slab = jnp.zeros((BIAS_ROWS, 256), F32)
    for j in range(GROUP):
        slab = slab + (terms[j, :, :256].astype(F32) + terms[j, :, 256:512].astype(F32))
    for half in range(2):
        piece = slab[:, half * 128 : half * 128 + 128].astype(BF)
        out_ref[:, 128 + half * 16 : 144 + half * 16, :] = jnp.broadcast_to(piece[None], (64, BIAS_ROWS, 128))

    for rb in range(4):
        dst = slice(rb * 16, rb * 16 + 16)
        chunks[2 * rb].wait()
        into = dot(nct[rb * 256 : rb * 256 + 256, :], grads[:, :768])
        for cb in range(6):
            out_ref[dst, cb * 16 : cb * 16 + 16, :] = into[:, cb * 128 : cb * 128 + 128].astype(BF).reshape(16, 16, 128)
        chunks[2 * rb + 1].wait()
        outof = dot(nct[D + rb * 256 : D + rb * 256 + 256, :], grads[:, 768:])
        for cb in range(2):
            out_ref[dst, 96 + cb * 16 : 112 + cb * 16, :] = outof[:, cb * 128 : cb * 128 + 128].astype(BF).reshape(16, 16, 128)


def sum_body(who, in_ref, w_ref, b_ref, bias):
    def fill(place):
        for part in range(GROUP):
            total = None
            for i in range(4):
                for xh in range(2):
                    for xl in range(2):
                        y, z = place(part, i)
                        one = in_ref[((y * 2 + xh) * 4 + z) * 2 + xl].astype(F32)
                        total = one if total is None else total + one
            for cb in range(6):
                w_ref[:, part * 768 + cb * 128 : part * 768 + cb * 128 + 128] = total[cb * 16 : cb * 16 + 16]
            for cb in range(2):
                at = 3 * D + part * 256 + cb * 128
                w_ref[:, at : at + 128] = total[96 + cb * 16 : 112 + cb * 16]
                bias[:, part * 256 + cb * 128 : part * 256 + cb * 128 + 128] = total[128 + cb * 16 : 144 + cb * 16]
        b_ref[...] = bias[:, :OFFSETS]

    @pl.when(who[0] == 0)
    def _():
        fill(lambda part, i: (i, part))

    @pl.when(who[0] == 1)
    def _():
        fill(lambda part, i: (part, i))


def per_device(boundary, tile_kinds, proj_in, proj_out, offset_bias):
    axes = ("lat", "lon", "section")
    nlat, nlon = lax.axis_size("lat"), lax.axis_size("lon")
    section = lax.axis_index("section")
    lat = lax.axis_index("lat")
    depth = jnp.where(section == 0, lat % GROUP, lat // (nlat // GROUP))
    who = jnp.stack([section, depth]).astype(jnp.int32)
    kind = tile_kinds.reshape(1)
    x = boundary.reshape(TOK // 12, 12, D)
    win = proj_in[0]
    wout = proj_out[0]
    onehot = jnp.asarray(ONEHOT, BF)
    onehot_t = jnp.asarray(ONEHOT.T, BF)
    pick = jnp.asarray(PICK, BF)
    pick_t = jnp.asarray(PICK.transpose(0, 2, 1), BF)

    def flat(lat, lon, sec):
        return ((lat % nlat) * nlon + lon % nlon) * 2 + sec

    def roll_pairs(dl, dn, from_section, to_section):
        return [
            (flat(i, j, from_section), flat(i + dl, j + dn, to_section))
            for i in range(nlat)
            for j in range(nlon)
        ]

    def forth(pieces, src, dst):
        got = []
        for dl in range(2):
            for dn in range(2):
                piece = pieces[(1 - dl) * 2 + (1 - dn)]
                if src == dst and dl == 0 and dn == 0:
                    got.append(piece)
                else:
                    got.append(lax.ppermute(piece, axes, roll_pairs(-dl, -dn, src, dst)))
        return got

    def back(pieces, src, dst):
        got = [None] * 4
        for dl in range(2):
            for dn in range(2):
                piece = pieces[dl * 2 + dn]
                if not (src == dst and dl == 0 and dn == 0):
                    piece = lax.ppermute(piece, axes, roll_pairs(dl, dn, src, dst))
                got[(1 - dl) * 2 + (1 - dn)] = piece
        return got

    def rings(stride, size, sec):
        chips = nlat * nlon
        return [
            [2 * (block + i + stride * m) + sec for m in range(GROUP)]
            for block in range(0, chips, size)
            for i in range(stride)
        ]

    z_rings = rings(nlon, GROUP * nlon, 0)
    y_rings = rings(nlat * nlon // GROUP, nlat * nlon, 1)

    def gather(value, groups):
        return [value] + [
            lax.ppermute(value, axes, [(g[m], g[(m + step) % GROUP]) for g in groups for m in range(GROUP)])
            for step in range(1, GROUP)
        ]

    def deal(values, groups):
        return [values[0]] + [
            lax.ppermute(values[step], axes, [(g[m], g[(m + step) % GROUP]) for g in groups for m in range(GROUP)])
            for step in range(1, GROUP)
        ]

    quarter = [shape(QT, D)] * 4
    f32 = functools.partial(shape, dtype=F32)
    vf32 = lambda *dims: pltpu.VMEM(dims, F32)
    vbf = lambda *dims: pltpu.VMEM(dims, BF)
    dma = lambda *dims: pltpu.SemaphoreType.DMA(dims)
    wide = shape(TOK, 3 * D)
    both = shape(TOK, 2 * D)
    augs = shape(PAIRS * MICRO * TOK, 128)
    late_shape = [shape(TOK + BIAS_ROWS, D)] * GROUP
    weights_v = [vbf(D, 3 * D), vbf(D, D), vf32(HEADS * WT, WT)]
    tall = [vf32(HEADS * WT, 128), vf32(HEADS * WT, 128)]
    pieces_v = [vbf(3 * 1152, 128)] * 3
    front_v = [vbf(TOK, D), vbf(TOK, D), vbf(TOK, 3 * D), vbf(PAIRS * MICRO * TOK, 128), vf32(TOK, D), vf32(TOK, D)]
    back_v = (
        weights_v
        + [vbf(TOK, D), vbf(TOK, 3 * D), vbf(PAIRS * MICRO * TOK, 128), vf32(TOK, D), vf32(TOK, D)]
        + [vbf(TOK, D), vbf(TOK, D), vbf(TOK, 3 * D)]
        + tall
        + [vf32(BIAS_ROWS, D), vbf(GROUP, BIAS_ROWS, D), dma(7), dma(4), dma(GROUP, 3)]
    )

    bias, nc_a, proj_a, aug_a, *pieces = call(
        first_forward_body, "first_forward", [f32(HEADS * WT, WT), both, wide, augs] + quarter,
        [SMEM, SMEM] + [VMEM] * 6 + [HBM] * 2,
        weights_v + front_v + [vf32(HEADS, OPAD)] + pieces_v + tall + [dma(7), dma(5)],
        5_000_000_000, 20_000_000, [HBM] * 4 + [VMEM] * 4,
    )(who, kind, x, offset_bias[0], onehot_t, jnp.asarray(ROWS_DIFFER), jnp.asarray(COLS_DIFFER), pick, win, wout)
    cots = forth(pieces, 1, 1)
    pieces, cots = lax.optimization_barrier((pieces, cots))
    received = forth(pieces, 0, 1)
    received, nc_a = lax.optimization_barrier((received, nc_a))
    early_a = gather(nc_a, z_rings)

    nc_b, *pieces = call(
        second_body, "second_both", [both] + late_shape + quarter * 2,
        [SMEM] + [VMEM] * 11 + [HBM] * 3,
        back_v + [vbf(TOK, D)], 12_000_000_000, 20_000_000, [HBM] * 5 + [VMEM] * 8,
    )(who, *received, *cots, pick, pick_t, onehot, bias, win, wout)
    late_b, second_out, grads = pieces[:4], pieces[4:8], pieces[8:]
    grads, early_a = lax.optimization_barrier((grads, early_a))
    grads = back(grads, 1, 0)
    grads, nc_b, second_out = lax.optimization_barrier((grads, nc_b, second_out))
    early_b = gather(nc_b, y_rings)

    *late, grad_in = call(
        first_backward_body, "first_backward", late_shape + [shape(TOK // 12, 12, D)],
        [SMEM] + [VMEM] * 7 + [HBM] * 10,
        back_v + [vbf(GROUP, TOK + BIAS_ROWS, D)], 8_000_000_000, 20_000_000, [HBM] * 4 + [VMEM],
    )(who, x, *grads, pick_t, onehot, nc_a, proj_a, aug_a, bias, win, wout, *late_b)
    grad_in, second_out = lax.optimization_barrier((grad_in, second_out))
    late = deal(late, z_rings + y_rings)
    second_out = back(second_out, 1, 1)

    flipped = call(
        flip_body, "flip", shape(2 * D, GROUP * TOK), [SMEM] + [HBM] * 8,
        [vbf(GROUP * TOK, 2 * D), vbf(2 * D, GROUP * TOK), dma(GROUP), dma(8)], 10_000_000, 10_000_000, HBM,
    )(who, *early_a, *early_b)
    result = call(
        result_body, "result", shape(TOK // 12, 12, D), [SMEM] + [VMEM] * 6, [vf32(TOK, D)], 170_000_000, 2_000_000,
        limit=SMALL,
    )(who, grad_in, *second_out, pick_t)

    terms = call(
        weight_body, "weight_terms", shape(64, 160, 128), [HBM] * 5,
        [vbf(2 * D, GROUP * TOK), vbf(GROUP * TOK, D), vbf(GROUP, BIAS_ROWS, D), dma(GROUP, 2), dma(8)],
        2_400_000_000, 10_000_000,
    )(flipped, *late)
    terms = lax.all_to_all(terms, ("lat", "lon"), 0, 0, tiled=True)

    weights, table = call(
        sum_body, "sum_terms", [f32(16, 4 * D), f32(HEADS, OFFSETS)], [SMEM, VMEM], [vf32(HEADS, D)], 3_000_000, 3_000_000,
        limit=SMALL,
    )(who, terms)
    return (result.reshape(boundary.shape), weights[None], table[None])


def solution(mesh):
    return jax.shard_map(
        per_device,
        mesh=mesh,
        in_specs=(
            P("section", None, None, "lat", "lon", None),
            P("section", "lat", "lon"),
            P("section", None, None),
            P("section", None, None),
            P("section", None, None),
        ),
        out_specs=(
            P("section", None, None, "lat", "lon", None),
            P("section", ("lat", "lon"), None),
            P("section", None, None),
        ),
        check_vma=False,
    )
```

```python
import functools

import jax
import jax.numpy as jnp
import numpy as np
from jax import lax
from jax.experimental import pallas as pl
from jax.experimental.pallas import tpu as pltpu
from jax.sharding import PartitionSpec as P

D = 1024
HEADS = 16
LEV = 2
MICRO = 2
WIN_LAT = 6
WIN_LON = 12
WT = 144
TOK = MICRO * WT
QT = TOK // 4
OFFSETS = 759
OPAD = 768
LEVEL_STEP = 253
ROW_STEP = 23
PAIRS = HEADS // 2
GROUP = 4
BIAS_ROWS = 16
NORM_EPS = 1e-05
MASKED = -1e30
BF = jnp.bfloat16
F32 = jnp.float32
VLIMIT = 58 * 1024 * 1024
SMALL = 24 * 1024 * 1024

HBM = pl.BlockSpec(memory_space=pltpu.HBM)
VMEM = pl.BlockSpec(memory_space=pltpu.VMEM)
SMEM = pl.BlockSpec(memory_space=pltpu.SMEM)


def constants():
    tok = np.arange(WT)
    lev, row, col = tok // 72, tok // 12 % 6, tok % 12
    onehot = np.zeros((256, 256), np.float32)
    onehot[tok, 128 * lev + 126 - 23 * row - col] = 1
    rows_differ = ((row < 3)[:, None] != (row < 3)[None, :]).astype(np.float32)
    cols_differ = ((col < 6)[:, None] != (col < 6)[None, :]).astype(np.float32)
    pick = np.zeros((4, QT, TOK), np.float32)
    for half_row in range(2):
        for half_col in range(2):
            at = 0
            for micro in range(MICRO):
                for level in range(LEV):
                    for r in range(3):
                        for c in range(6):
                            src = micro * WT + level * 72 + (3 * half_row + r) * 12 + 6 * half_col + c
                            pick[half_row * 2 + half_col, at, src] = 1
                            at += 1
    return onehot, rows_differ, cols_differ, pick


ONEHOT, ROWS_DIFFER, COLS_DIFFER, PICK = constants()


def dot(a, b):
    return jnp.dot(a, b, preferred_element_type=F32)


def dot_nt(a, b):
    return lax.dot_general(a, b, (((1,), (1,)), ((), ())), preferred_element_type=F32)


def dot_tn(a, b):
    return lax.dot_general(a, b, (((0,), (0,)), ((), ())), preferred_element_type=F32)


def call(body, name, out_shape, in_specs, scratch, flops, nbytes, out_specs=None, limit=VLIMIT):
    if out_specs is None:
        out_specs = jax.tree.map(lambda _: VMEM, out_shape)
    return pl.pallas_call(
        body,
        out_shape=out_shape,
        in_specs=in_specs,
        out_specs=out_specs,
        scratch_shapes=scratch,
        compiler_params=pltpu.CompilerParams(vmem_limit_bytes=limit),
        cost_estimate=pl.CostEstimate(flops=flops, bytes_accessed=nbytes, transcendentals=0),
        name=name,
    )


def begin(src, dst, sem):
    copy = pltpu.make_async_copy(src, dst, sem)
    copy.start()
    return copy


def begin_weights(win, wout, win_v, wout_v, sem):
    made = []
    for i in range(6):
        cols = pl.ds(512 * i, 512)
        made.append(begin(win.at[:, cols], win_v.at[:, cols], sem.at[i]))
    made.append(begin(wout, wout_v, sem.at[6]))
    return made


def shape(*dims, dtype=BF):
    return jax.ShapeDtypeStruct(dims, dtype)


def load_groups(x_ref, dst):
    for g in range(TOK // 12):
        dst[12 * g : 12 * g + 12, :] = x_ref[g].astype(F32)


def store_groups(src, out_ref):
    for g in range(TOK // 12):
        out_ref[g] = src[12 * g : 12 * g + 12, :].astype(BF)


def insert(piece_refs, pickt_ref):
    total = dot(pickt_ref[0], piece_refs[0][...])
    for q in range(1, 4):
        total = total + dot(pickt_ref[q], piece_refs[q][...])
    return total


def extract(value, pick_ref, out_refs):
    for q in range(4):
        out_refs[q][...] = dot(pick_ref[q], value).astype(BF)


def build_bias(kind, table_ref, oht_ref, rdiff, cdiff, out, tab, tops, mids, lows, tall, edge):
    tab[...] = jnp.zeros_like(tab)
    tab[:, :OFFSETS] = table_ref[...]
    for dl in range(3):
        for rq in range(6):
            for cq in range(12):
                start = LEVEL_STEP * dl + ROW_STEP * rq + cq
                at = ((dl * 6 + rq) * 12 + cq) * 16
                x = tab[:, start : start + 128]
                top = x.astype(BF)
                rest = x - top.astype(F32)
                mid = rest.astype(BF)
                tops[at : at + 16, :] = top
                mids[at : at + 16, :] = mid
                lows[at : at + 16, :] = (rest - mid.astype(F32)).astype(BF)
    for lq in range(2):
        for rq in range(6):
            one = ((1 + lq) * 6 + rq) * 192
            two = (lq * 6 + rq) * 192
            got = None
            for piece in (tops, mids, lows):
                x = jnp.concatenate([piece[one : one + 192, :], piece[two : two + 192, :]], axis=1)
                part = dot(x, oht_ref[...])
                got = part if got is None else got + part
            for cq in range(12):
                rows = pl.ds((lq * 6 + rq) * 12 + cq, 16, stride=WT)
                tall[rows, :] = got[cq * 16 : cq * 16 + 16, :128]
                edge[rows, :] = got[cq * 16 : cq * 16 + 16, 128:]
    split_rows = (kind[0] % 2).astype(F32)
    split_cols = (kind[0] // 2).astype(F32)
    closed = rdiff[...] * split_rows + cdiff[...] * split_cols > 0.0
    for h in range(HEADS):
        rows = slice(h * WT, h * WT + WT)
        out[rows, :128] = jnp.where(closed[:, :128], MASKED, tall[rows, :])
        out[rows, 128:] = jnp.where(closed[:, 128:], MASKED, edge[rows, : WT - 128])


def head_masks(scale):
    lane = lax.broadcasted_iota(jnp.int32, (1, 128), 1)
    low = jnp.where(lane < 64, scale, 0.0).astype(BF)
    high = jnp.where(lane >= 64, scale, 0.0).astype(BF)
    return low, high


def stacked(block, masks):
    return jnp.concatenate([block * masks[0], block * masks[1]], axis=0)


def norm_rows(xs, n_ref, at, count):
    x = xs[at : at + count, :]
    mean = jnp.mean(x, axis=-1, keepdims=True)
    centered = x - mean
    var = jnp.mean(centered * centered, axis=-1, keepdims=True)
    n_ref[at : at + count, :] = (centered * lax.rsqrt(var + NORM_EPS)).astype(BF)


def pair_lanes(p, base):
    return pl.ds(pl.multiple_of(base + p * 128, 128), 128)


def pair_rows(p):
    return pl.ds(pl.multiple_of(p * TOK, 8), TOK)


def forward_core(xs, win, wout, bias_ref, n_ref, c_ref, proj_ref, e_ref, inv_ref, out, weights, bias_ready, made):
    for at in range(0, TOK, 48):
        norm_rows(xs, n_ref, at, 48)
    made("n")
    for i in range(6):
        weights[i].wait()
        cols = slice(512 * i, 512 * i + 512)
        proj_ref[:, cols] = dot(n_ref[...], win[:, cols]).astype(BF)
    made("proj")
    bias_ready()

    @pl.loop(0, PAIRS, unroll=8)
    def _(p):
        eighth = head_masks(0.125)
        ones = head_masks(1.0)
        for w in range(MICRO):
            rows = slice(w * WT, w * WT + WT)
            qs = stacked(proj_ref[rows, pair_lanes(p, 0)], eighth)
            k = proj_ref[rows, pair_lanes(p, D)]
            v = proj_ref[rows, pair_lanes(p, 2 * D)]
            s = dot_nt(qs, k) + bias_ref[pair_rows(p), :]
            peak = jnp.max(s, axis=-1, keepdims=True)
            e = jnp.exp(s - peak).astype(BF)
            e_ref[pl.ds(pl.multiple_of((p * 2 + w) * TOK, 16), TOK), :] = e
            wide = [
                jnp.concatenate([v * one, jnp.broadcast_to(one, (WT, 128))], axis=1) for one in ones
            ]
            both = dot(e[:WT], wide[0]) + dot(e[WT:], wide[1])
            inv = 1.0 / both[:, 128:]
            c_ref[rows, pair_lanes(p, 0)] = (both[:, :128] * inv).astype(BF)
            inv_ref[pl.ds(pl.multiple_of((p * 2 + w) * WT, 16), WT), :] = inv.astype(BF)

    made("c")
    weights[6].wait()
    for c in range(0, D, 512):
        out[:, c : c + 512] = xs[:, c : c + 512] + dot(c_ref[...], wout[:, c : c + 512])


def backward_core(who, xs, go, win, wout, c_ref, proj_ref, e_ref, inv_ref, oh_ref, gctx, gp, bacc, edge, terms, out,
                  weights, ready, late_ref, late_sem):
    sent = []
    part = [lax.rem(who[1] + step, GROUP) for step in range(GROUP)]
    for step in range(GROUP):
        cols = pl.ds(pl.multiple_of(256 * part[step], 128), 256)
        sent.append(begin(go.at[:, cols], late_ref[step].at[pl.ds(0, TOK), pl.ds(768, 256)], late_sem.at[step, 0]))
    if weights:
        weights[6].wait()
    for c in range(0, D, 256):
        gctx[:, c : c + 256] = dot_nt(go[...], wout[c : c + 256, :]).astype(BF)
    edge[...] = jnp.zeros_like(edge)
    ready()

    @pl.loop(0, PAIRS, unroll=4)
    def _(p):
        eighth = head_masks(0.125)
        ones = head_masks(1.0)
        full = jnp.ones((WT, 128), BF)
        total = None
        for w in range(MICRO):
            rows = slice(w * WT, w * WT + WT)
            qs = stacked(proj_ref[rows, pair_lanes(p, 0)], eighth)
            k = proj_ref[rows, pair_lanes(p, D)]
            v = proj_ref[rows, pair_lanes(p, 2 * D)]
            e = e_ref[pl.ds(pl.multiple_of((p * 2 + w) * TOK, 16), TOK), :]
            inv = inv_ref[pl.ds(pl.multiple_of((p * 2 + w) * WT, 16), WT), :]
            dc = (gctx[rows, pair_lanes(p, 0)].astype(F32) * inv.astype(F32)).astype(BF)
            dcs = stacked(dc, ones)
            along = -(dc.astype(F32) * c_ref[rows, pair_lanes(p, 0)].astype(F32))
            alongs = stacked(along.astype(BF), ones)
            slope = dot_nt(jnp.concatenate([dcs, alongs], axis=1), jnp.concatenate([v, full], axis=1))
            ds = e.astype(F32) * slope
            total = ds if total is None else total + ds
            dsb = ds.astype(BF)
            gp[rows, pair_lanes(p, 2 * D)] = dot_tn(e, dcs).astype(BF)
            gp[rows, pair_lanes(p, D)] = dot_tn(dsb, qs).astype(BF)
            ks = [k * one for one in eighth]
            gp[rows, pair_lanes(p, 0)] = (dot(dsb[:WT], ks[0]) + dot(dsb[WT:], ks[1])).astype(BF)
        bacc[pair_rows(p), :] = total[:, :128]
        edge[pair_rows(p), : WT - 128] = total[:, 128:]

    for step in range(GROUP):
        cols = pl.ds(pl.multiple_of(768 * part[step], 128), 768)
        sent.append(begin(gp.at[:, cols], late_ref[step].at[pl.ds(0, TOK), pl.ds(0, 768)], late_sem.at[step, 1]))

    acc = [jnp.zeros((BIAS_ROWS, 256), F32) for _ in range(3)]
    blank = jnp.zeros((BIAS_ROWS, 128), F32)
    for rq in range(6):
        got = []
        for lq in range(2):
            taken = [pl.ds((lq * 6 + rq) * 12 + cq, 16, stride=WT) for cq in range(12)]
            x = jnp.concatenate(
                [jnp.concatenate([ref[rows, :] for rows in taken], axis=0) for ref in (bacc, edge)], axis=1
            )
            top = x.astype(BF)
            low = (x - top.astype(F32)).astype(BF)
            got.append(dot(top, oh_ref[...]) + dot(low, oh_ref[...]))
        levels = [got[0][:, 128:], got[0][:, :128] + got[1][:, 128:], got[1][:, :128]]
        for dl in range(3):
            for cq in range(12):
                one = jnp.concatenate([levels[dl][cq * 16 : cq * 16 + 16], blank], axis=1)
                shift = ROW_STEP * rq + cq
                acc[dl] = acc[dl] + (pltpu.roll(one, shift, 1) if shift else one)
    folded = jnp.zeros((BIAS_ROWS, OPAD), F32)
    for dl in range(3):
        one = jnp.concatenate([acc[dl], jnp.zeros((BIAS_ROWS, OPAD - 256), F32)], axis=1)
        folded = folded + (pltpu.roll(one, LEVEL_STEP * dl, 1) if dl else one)
    terms[:, :OPAD] = folded.astype(BF)
    terms[:, OPAD:] = jnp.zeros((BIAS_ROWS, D - OPAD), BF)
    for step in range(GROUP):
        sent.append(begin(terms, late_ref[step].at[pl.ds(TOK, BIAS_ROWS), :], late_sem.at[step, 2]))

    if weights:
        for i in range(6):
            weights[i].wait()
    for c in range(0, D, 256):
        out[:, c : c + 256] = dot_nt(gp[...], win[c : c + 256, :]).astype(BF).astype(F32)
    for at in range(0, TOK, 48):
        rows = slice(at, at + 48)
        dn = out[rows, :]
        x = xs[rows, :]
        mean = jnp.mean(x, axis=-1, keepdims=True)
        centered = x - mean
        var = jnp.mean(centered * centered, axis=-1, keepdims=True)
        scale = lax.rsqrt(var + NORM_EPS)
        n = centered * scale
        along = jnp.mean(dn * n, axis=-1, keepdims=True)
        level = jnp.mean(dn, axis=-1, keepdims=True)
        dx = (scale * (dn - level - n * along)).astype(BF).astype(F32)
        out[rows, :] = go[rows, :].astype(F32) + dx
    return sent


def first_forward_body(who, kind, x_ref, table_ref, oht_ref, rdiff, cdiff, pick_ref, win, wout,
                       bias_out, n_out, c_out, proj_out, e_out, inv_out, p0, p1, p2, p3,
                       win_v, wout_v, bias_v, n, c, proj, e, inv, xs, out, tab, tops, mids, lows, tall, edge, wsem, osem):
    @pl.when(who[0] == 0)
    def _():
        begin_weights(win, wout, win_v, wout_v, wsem)

    build_bias(kind, table_ref, oht_ref, rdiff, cdiff, bias_v, tab, tops, mids, lows, tall, edge)
    bias_copy = begin(bias_v, bias_out, osem.at[4])

    @pl.when(who[0] == 0)
    def _():
        weights = [
            pltpu.make_async_copy(win.at[:, pl.ds(512 * i, 512)], win_v.at[:, pl.ds(512 * i, 512)], wsem.at[i])
            for i in range(6)
        ] + [pltpu.make_async_copy(wout, wout_v, wsem.at[6])]
        load_groups(x_ref, xs)
        sent = []

        def made(name):
            if name == "n":
                sent.append(begin(n, n_out, osem.at[0]))
            if name == "proj":
                sent.append(begin(proj, proj_out, osem.at[1]))
            if name == "c":
                sent.append(begin(c, c_out, osem.at[2]))
                sent.append(begin(e, e_out, osem.at[3]))
                sent.append(begin(inv, inv_out, osem.at[5]))

        forward_core(xs, win_v, wout_v, bias_v, n, c, proj, e, inv, out, weights, lambda: None, made)
        extract(out[...].astype(BF), pick_ref, (p0, p1, p2, p3))
        for one in sent:
            one.wait()

    @pl.when(who[0] == 1)
    def _():
        load_groups(x_ref, xs)
        extract(xs[...].astype(BF), pick_ref, (p0, p1, p2, p3))

    bias_copy.wait()


def second_body(who, r0, r1, r2, r3, c0, c1, c2, c3, pick_ref, pickt_ref, oh_ref, ca_ref, bias_ref, win, wout,
                mid_out, cb_out, l0, l1, l2, l3, s0, s1, s2, s3, g0, g1, g2, g3,
                win_v, wout_v, c, proj, e, inv, xs, out, go, gctx, gp, bacc, edge, terms,
                wsem, isem, lsem, n, bias_v):
    @pl.when(who[0] == 1)
    def _():
        weights = begin_weights(win, wout, win_v, wout_v, wsem)
        bias_copy = begin(bias_ref, bias_v, isem.at[0])
        xs[...] = insert((r0, r1, r2, r3), pickt_ref)
        sent = []

        def made(name):
            if name == "n":
                sent.append(begin(n, mid_out, isem.at[1]))
            if name == "c":
                sent.append(begin(c, cb_out, isem.at[2]))

        forward_core(xs, win_v, wout_v, bias_v, n, c, proj, e, inv, out, weights, bias_copy.wait, made)
        extract(out[...].astype(BF), pick_ref, (s0, s1, s2, s3))
        go[...] = insert((c0, c1, c2, c3), pickt_ref).astype(BF)
        sent += backward_core(who, xs, go, win_v, wout_v, c, proj, e, inv, oh_ref, gctx, gp, bacc, edge, terms,
                              out, None, lambda: None, (l0, l1, l2, l3), lsem)
        extract(out[...].astype(BF), pick_ref, (g0, g1, g2, g3))
        for one in sent:
            one.wait()

    @pl.when(who[0] == 0)
    def _():
        begin(ca_ref, c, isem.at[1]).wait()
        begin(c, mid_out, isem.at[2]).wait()


def first_backward_body(who, x_ref, g0, g1, g2, g3, pickt_ref, oh_ref,
                        ca_ref, proj_ref, e_ref, inv_ref, win, wout, b0, b1, b2, b3,
                        l0, l1, l2, l3, out_ref,
                        win_v, wout_v, c, proj, e, inv, xs, out, go, gctx, gp, bacc, edge, terms,
                        wsem, isem, lsem, hold):
    @pl.when(who[0] == 0)
    def _():
        weights = [None] * 7
        weights[6] = begin(wout, wout_v, wsem.at[6])
        copies = [
            begin(proj_ref, proj, isem.at[0]),
            begin(e_ref, e, isem.at[1]),
            begin(inv_ref, inv, isem.at[2]),
            begin(ca_ref, c, isem.at[3]),
        ]
        for i in range(6):
            cols = pl.ds(512 * i, 512)
            weights[i] = begin(win.at[:, cols], win_v.at[:, cols], wsem.at[i])
        go[...] = insert((g0, g1, g2, g3), pickt_ref).astype(BF)
        load_groups(x_ref, xs)

        def ready():
            for one in copies:
                one.wait()

        sent = backward_core(who, xs, go, win_v, wout_v, c, proj, e, inv, oh_ref, gctx, gp, bacc, edge, terms,
                             out, weights, ready, (l0, l1, l2, l3), lsem)
        store_groups(out, out_ref)
        for one in sent:
            one.wait()

    @pl.when(who[0] == 1)
    def _():
        came = [begin(src, hold.at[j], lsem.at[j, 0]) for j, src in enumerate((b0, b1, b2, b3))]
        gone = []
        for j, dst in enumerate((l0, l1, l2, l3)):
            came[j].wait()
            gone.append(begin(hold.at[j], dst, lsem.at[j, 1]))
        for one in gone:
            one.wait()


def result_body(who, grad_ref, s0, s1, s2, s3, pickt_ref, out_ref, xs):
    @pl.when(who[0] == 0)
    def _():
        out_ref[...] = grad_ref[...]

    @pl.when(who[0] == 1)
    def _():
        xs[...] = insert((s0, s1, s2, s3), pickt_ref)
        store_groups(xs, out_ref)


def flip_body(who, *refs):
    first, middle, last = (refs[GROUP * i : GROUP * i + GROUP] for i in range(3))
    out_ref, held, sem = refs[3 * GROUP :]

    def copies(normals, contexts):
        return [
            pltpu.make_async_copy(src, held.at[pl.ds(TOK * j, TOK), pl.ds(base, D)], sem.at[j, base // D])
            for base, sources in ((0, normals), (D, contexts))
            for j, src in enumerate(sources)
        ]

    @pl.when(who[0] == 0)
    def _():
        for one in copies(first, middle):
            one.start()

    @pl.when(who[0] == 1)
    def _():
        for one in copies(middle, last):
            one.start()

    for one in copies(first, middle):
        one.wait()

    @pl.loop(0, 8)
    def _(i):
        at = pl.ds(pl.multiple_of(i * 256, 256), 256)
        out_ref[at, :] = held[:, at].T


def weight_body(nct, l0, l1, l2, l3, out_ref, table_ref, grads):
    late = (l0, l1, l2, l3)
    table = late[0][TOK:, :OPAD].astype(F32)
    for j in range(GROUP):
        grads[TOK * j : TOK * j + TOK, :] = late[j][:TOK, :]
        if j:
            table = table + late[j][TOK:, :OPAD].astype(F32)
    table_ref[...] = table
    for rb in range(4):
        dst = slice(rb * 16, rb * 16 + 16)
        into = dot(nct[rb * 256 : rb * 256 + 256, :], grads[:, :768])
        for cb in range(6):
            out_ref[dst, cb * 16 : cb * 16 + 16, :] = into[:, cb * 128 : cb * 128 + 128].astype(BF).reshape(16, 16, 128)
        outof = dot(nct[D + rb * 256 : D + rb * 256 + 256, :], grads[:, 768:])
        for cb in range(2):
            out_ref[dst, 96 + cb * 16 : 112 + cb * 16, :] = outof[:, cb * 128 : cb * 128 + 128].astype(BF).reshape(16, 16, 128)


def sum_body(who, in_ref, w_ref):
    def fill(place):
        for part in range(GROUP):
            total = None
            for i in range(4):
                for xh in range(2):
                    for xl in range(2):
                        y, z = place(part, i)
                        one = in_ref[((y * 2 + xh) * 4 + z) * 2 + xl].astype(F32)
                        total = one if total is None else total + one
            for cb in range(6):
                w_ref[:, part * 768 + cb * 128 : part * 768 + cb * 128 + 128] = total[cb * 16 : cb * 16 + 16]
            for cb in range(2):
                at = 3 * D + part * 256 + cb * 128
                w_ref[:, at : at + 128] = total[96 + cb * 16 : 112 + cb * 16]

    @pl.when(who[0] == 0)
    def _():
        fill(lambda part, i: (i, part))

    @pl.when(who[0] == 1)
    def _():
        fill(lambda part, i: (part, i))


def per_device(boundary, tile_kinds, proj_in, proj_out, offset_bias):
    axes = ("lat", "lon", "section")
    nlat, nlon = lax.axis_size("lat"), lax.axis_size("lon")
    section = lax.axis_index("section")
    lat = lax.axis_index("lat")
    depth = jnp.where(section == 0, lat % GROUP, lat // (nlat // GROUP))
    who = jnp.stack([section, depth]).astype(jnp.int32)
    kind = tile_kinds.reshape(1)
    x = boundary.reshape(TOK // 12, 12, D)
    win = proj_in[0]
    wout = proj_out[0]
    onehot = jnp.asarray(ONEHOT, BF)
    onehot_t = jnp.asarray(ONEHOT.T, BF)
    pick = jnp.asarray(PICK, BF)
    pick_t = jnp.asarray(PICK.transpose(0, 2, 1), BF)

    def flat(lat, lon, sec):
        return ((lat % nlat) * nlon + lon % nlon) * 2 + sec

    def roll_pairs(dl, dn, from_section, to_section):
        return [
            (flat(i, j, from_section), flat(i + dl, j + dn, to_section))
            for i in range(nlat)
            for j in range(nlon)
        ]

    def forth(pieces, src, dst):
        got = []
        for dl in range(2):
            for dn in range(2):
                piece = pieces[(1 - dl) * 2 + (1 - dn)]
                if src == dst and dl == 0 and dn == 0:
                    got.append(piece)
                else:
                    got.append(lax.ppermute(piece, axes, roll_pairs(-dl, -dn, src, dst)))
        return got

    def back(pieces, src, dst):
        got = [None] * 4
        for dl in range(2):
            for dn in range(2):
                piece = pieces[dl * 2 + dn]
                if not (src == dst and dl == 0 and dn == 0):
                    piece = lax.ppermute(piece, axes, roll_pairs(dl, dn, src, dst))
                got[(1 - dl) * 2 + (1 - dn)] = piece
        return got

    def rings(axis, sec):
        made = {}
        for y in range(4):
            for x in range(4):
                for z in range(4):
                    key = {"x": (y, z), "y": (x, z), "z": (x, y)}[axis]
                    made.setdefault(key, []).append(flat((y * 2 + x // 2) * 4 + z, x % 2, sec))
        return [made[key] for key in sorted(made)]

    def gather(value, groups):
        return deal([value] * GROUP, groups)

    def deal(values, groups):
        return [values[0]] + [
            lax.ppermute(values[step], axes, [(g[m], g[(m + step) % GROUP]) for g in groups for m in range(GROUP)])
            for step in range(1, GROUP)
        ]

    quarter = [shape(QT, D)] * 4
    f32 = functools.partial(shape, dtype=F32)
    vf32 = lambda *dims: pltpu.VMEM(dims, F32)
    vbf = lambda *dims: pltpu.VMEM(dims, BF)
    dma = lambda *dims: pltpu.SemaphoreType.DMA(dims)
    wide = shape(TOK, 3 * D)
    whole = shape(TOK, D)
    exps = shape(PAIRS * MICRO * TOK, WT)
    invs = shape(PAIRS * MICRO * WT, 128)
    late_shape = [shape(TOK + BIAS_ROWS, D)] * GROUP
    weights_v = [vbf(D, 3 * D), vbf(D, D)]
    soft_v = [vbf(PAIRS * MICRO * TOK, WT), vbf(PAIRS * MICRO * WT, 128)]
    tall = [vf32(HEADS * WT, 128), vf32(HEADS * WT, 128)]
    pieces_v = [vbf(3 * 1152, 128)] * 3
    front_v = [vf32(HEADS * WT, WT), vbf(TOK, D), vbf(TOK, D), vbf(TOK, 3 * D)] + soft_v + [vf32(TOK, D), vf32(TOK, D)]
    back_v = (
        weights_v
        + [vbf(TOK, D), vbf(TOK, 3 * D)] + soft_v + [vf32(TOK, D), vf32(TOK, D)]
        + [vbf(TOK, D), vbf(TOK, D), vbf(TOK, 3 * D)]
        + tall
        + [vbf(BIAS_ROWS, D), dma(7), dma(4), dma(GROUP, 3)]
    )

    bias, n_a, c_a, proj_a, e_a, inv_a, *pieces = call(
        first_forward_body, "first_forward", [f32(HEADS * WT, WT), whole, whole, wide, exps, invs] + quarter,
        [SMEM, SMEM] + [VMEM] * 6 + [HBM] * 2,
        weights_v + front_v + [vf32(HEADS, OPAD)] + pieces_v + tall + [dma(7), dma(6)],
        5_000_000_000, 20_000_000, [HBM] * 6 + [VMEM] * 4,
    )(who, kind, x, offset_bias[0], onehot_t, jnp.asarray(ROWS_DIFFER), jnp.asarray(COLS_DIFFER), pick, win, wout)
    cots = forth(pieces, 1, 1)
    pieces, cots = lax.optimization_barrier((pieces, cots))
    received = forth(pieces, 0, 1)
    received, n_a = lax.optimization_barrier((received, n_a))
    early = gather(n_a, rings("z", 0))

    middle, c_b, *pieces = call(
        second_body, "second_both", [whole] * 2 + late_shape + quarter * 2,
        [SMEM] + [VMEM] * 11 + [HBM] * 4,
        back_v + [vbf(TOK, D), vf32(HEADS * WT, WT)], 12_000_000_000, 20_000_000, [HBM] * 6 + [VMEM] * 8,
    )(who, *received, *cots, pick, pick_t, onehot, c_a, bias, win, wout)
    late_b, second_out, grads = pieces[:4], pieces[4:8], pieces[8:]
    grads, early = lax.optimization_barrier((grads, early))
    grads = back(grads, 1, 0)
    grads, middle, c_b, second_out = lax.optimization_barrier((grads, middle, c_b, second_out))
    middle = gather(middle, rings("z", 0) + rings("y", 1))

    *late, grad_in = call(
        first_backward_body, "first_backward", late_shape + [shape(TOK // 12, 12, D)],
        [SMEM] + [VMEM] * 7 + [HBM] * 10,
        back_v + [vbf(GROUP, TOK + BIAS_ROWS, D)], 8_000_000_000, 20_000_000, [HBM] * 4 + [VMEM],
    )(who, x, *grads, pick_t, onehot, c_a, proj_a, e_a, inv_a, win, wout, *late_b)
    late, grad_in, second_out, c_b, middle = lax.optimization_barrier((late, grad_in, second_out, c_b, middle))
    last = gather(c_b, rings("y", 1))
    late = deal(late, rings("z", 0) + rings("y", 1))
    second_out = back(second_out, 1, 1)

    flipped = call(
        flip_body, "flip", shape(2 * D, GROUP * TOK), [SMEM] + [HBM] * 12,
        [vbf(GROUP * TOK, 2 * D), dma(GROUP, 2)], 10_000_000, 10_000_000, limit=SMALL,
    )(who, *early, *middle, *last)
    result = call(
        result_body, "result", shape(TOK // 12, 12, D), [SMEM] + [VMEM] * 6, [vf32(TOK, D)], 170_000_000, 2_000_000,
        limit=SMALL,
    )(who, grad_in, *second_out, pick_t)

    terms, table = call(
        weight_body, "weight_terms", [shape(64, 128, 128), f32(HEADS, OPAD)], [VMEM] * 5,
        [vbf(GROUP * TOK, D)], 2_400_000_000, 10_000_000, limit=SMALL,
    )(flipped, *late)
    terms = lax.all_to_all(terms, ("lat", "lon"), 0, 0, tiled=True)
    table = sum(gather(table, rings("y", 0) + rings("z", 1)))
    table = sum(gather(table, rings("x", 0) + rings("x", 1)))

    weights = call(
        sum_body, "sum_terms", f32(16, 4 * D), [SMEM, VMEM], [], 3_000_000, 3_000_000, limit=SMALL,
    )(who, terms)
    return (result.reshape(boundary.shape), weights[None], table[None, :, :OFFSETS])


def solution(mesh):
    return jax.shard_map(
        per_device,
        mesh=mesh,
        in_specs=(
            P("section", None, None, "lat", "lon", None),
            P("section", "lat", "lon"),
            P("section", None, None),
            P("section", None, None),
            P("section", None, None),
        ),
        out_specs=(
            P("section", None, None, "lat", "lon", None),
            P("section", ("lat", "lon"), None),
            P("section", None, None),
        ),
        check_vma=False,
    )
```

```python
import functools

import jax
import jax.numpy as jnp
import numpy as np
from jax import lax
from jax.experimental import pallas as pl
from jax.experimental.pallas import tpu as pltpu
from jax.sharding import PartitionSpec as P

D = 1024
HEADS = 16
LEV = 2
MICRO = 2
WIN_LAT = 6
WIN_LON = 12
WT = 144
TOK = MICRO * WT
QT = TOK // 4
OFFSETS = 759
OPAD = 768
LEVEL_STEP = 253
ROW_STEP = 23
PAIRS = HEADS // 2
GROUP = 4
BIAS_ROWS = 16
NORM_EPS = 1e-05
MASKED = -1e30
BF = jnp.bfloat16
F32 = jnp.float32
VLIMIT = 58 * 1024 * 1024
SMALL = 24 * 1024 * 1024

HBM = pl.BlockSpec(memory_space=pltpu.HBM)
VMEM = pl.BlockSpec(memory_space=pltpu.VMEM)
SMEM = pl.BlockSpec(memory_space=pltpu.SMEM)


def constants():
    tok = np.arange(WT)
    row, col, lev = tok // 24, tok // 2 % 12, tok % 2
    onehot = np.zeros((256, 256), np.float32)
    onehot[tok, 128 * lev + 126 - 23 * row - col] = 1
    rows_differ = ((row < 3)[:, None] != (row < 3)[None, :]).astype(np.float32)
    cols_differ = ((col < 6)[:, None] != (col < 6)[None, :]).astype(np.float32)
    pick = np.zeros((4, QT, TOK), np.float32)
    for half_row in range(2):
        for half_col in range(2):
            at = 0
            for micro in range(MICRO):
                for level in range(LEV):
                    for r in range(3):
                        for c in range(6):
                            src = micro * WT + ((3 * half_row + r) * 12 + 6 * half_col + c) * 2 + level
                            pick[half_row * 2 + half_col, at, src] = 1
                            at += 1
    upper = np.concatenate([pick, np.zeros_like(pick)], axis=1).transpose(0, 2, 1)
    lower = np.concatenate([np.zeros_like(pick), pick], axis=1).transpose(0, 2, 1)
    return onehot, rows_differ, cols_differ, pick, upper, lower


ONEHOT, ROWS_DIFFER, COLS_DIFFER, PICK, UPPER, LOWER = constants()


def dot(a, b):
    return jnp.dot(a, b, preferred_element_type=F32)


def dot_nt(a, b):
    return lax.dot_general(a, b, (((1,), (1,)), ((), ())), preferred_element_type=F32)


def dot_tn(a, b):
    return lax.dot_general(a, b, (((0,), (0,)), ((), ())), preferred_element_type=F32)


def call(body, name, out_shape, in_specs, scratch, flops, nbytes, out_specs=None, limit=VLIMIT):
    if out_specs is None:
        out_specs = jax.tree.map(lambda _: VMEM, out_shape)
    return pl.pallas_call(
        body,
        out_shape=out_shape,
        in_specs=in_specs,
        out_specs=out_specs,
        scratch_shapes=scratch,
        compiler_params=pltpu.CompilerParams(vmem_limit_bytes=limit),
        cost_estimate=pl.CostEstimate(flops=flops, bytes_accessed=nbytes, transcendentals=0),
        name=name,
    )


def begin(src, dst, sem):
    copy = pltpu.make_async_copy(src, dst, sem)
    copy.start()
    return copy


def begin_weights(win, wout, win_v, wout_v, sem):
    made = []
    for i in range(6):
        cols = pl.ds(512 * i, 512)
        made.append(begin(win.at[:, cols], win_v.at[:, cols], sem.at[i]))
    made.append(begin(wout, wout_v, sem.at[6]))
    return made


def shape(*dims, dtype=BF):
    return jax.ShapeDtypeStruct(dims, dtype)


def load_block(x_ref, dst):
    dst[...] = x_ref[...].astype(F32).reshape(TOK, D)


def store_block(src, out_ref):
    out_ref[...] = src[...].astype(BF).reshape(TOK // 2, 2, D)


def insert(piece_refs, pick_ref):
    total = dot(pick_ref[0], piece_refs[0][...])
    for q in range(1, 4):
        total = total + dot(pick_ref[q], piece_refs[q][...])
    return total


def extract(first, second, pick_ref, out_refs):
    for q in range(4):
        out_refs[q][...] = jnp.concatenate([dot(pick_ref[q], first), dot(pick_ref[q], second)], axis=0).astype(BF)


def build_bias(kind, table_ref, oht_ref, rdiff, cdiff, out, tab, tops, mids, lows, tall, edge):
    tab[...] = jnp.zeros_like(tab)
    tab[:, :OFFSETS] = table_ref[...]
    for dl in range(3):
        for rq in range(6):
            for cq in range(12):
                start = LEVEL_STEP * dl + ROW_STEP * rq + cq
                at = ((dl * 6 + rq) * 12 + cq) * 16
                x = tab[:, start : start + 128]
                top = x.astype(BF)
                rest = x - top.astype(F32)
                mid = rest.astype(BF)
                tops[at : at + 16, :] = top
                mids[at : at + 16, :] = mid
                lows[at : at + 16, :] = (rest - mid.astype(F32)).astype(BF)
    for lq in range(2):
        for rq in range(6):
            one = ((1 + lq) * 6 + rq) * 192
            two = (lq * 6 + rq) * 192
            got = None
            for piece in (tops, mids, lows):
                x = jnp.concatenate([piece[one : one + 192, :], piece[two : two + 192, :]], axis=1)
                part = dot(x, oht_ref[...])
                got = part if got is None else got + part
            for cq in range(12):
                rows = pl.ds((rq * 12 + cq) * 2 + lq, 16, stride=WT)
                tall[rows, :] = got[cq * 16 : cq * 16 + 16, :128]
                edge[rows, :] = got[cq * 16 : cq * 16 + 16, 128:]
    split_rows = (kind[0] % 2).astype(F32)
    split_cols = (kind[0] // 2).astype(F32)
    closed = rdiff[...] * split_rows + cdiff[...] * split_cols > 0.0
    for h in range(HEADS):
        rows = slice(h * WT, h * WT + WT)
        out[rows, :128] = jnp.where(closed[:, :128], MASKED, tall[rows, :])
        out[rows, 128:] = jnp.where(closed[:, 128:], MASKED, edge[rows, : WT - 128])


def head_masks(scale):
    lane = lax.broadcasted_iota(jnp.int32, (1, 128), 1)
    low = jnp.where(lane < 64, scale, 0.0).astype(BF)
    high = jnp.where(lane >= 64, scale, 0.0).astype(BF)
    return low, high


def stacked(block, masks):
    return jnp.concatenate([block * masks[0], block * masks[1]], axis=0)


def norm_rows(xs, n_ref, at, count):
    x = xs[at : at + count, :]
    mean = jnp.mean(x, axis=-1, keepdims=True)
    centered = x - mean
    var = jnp.mean(centered * centered, axis=-1, keepdims=True)
    n_ref[at : at + count, :] = (centered * lax.rsqrt(var + NORM_EPS)).astype(BF)


def pair_lanes(p, base):
    return pl.ds(pl.multiple_of(base + p * 128, 128), 128)


def pair_rows(p):
    return pl.ds(pl.multiple_of(p * TOK, 8), TOK)


def forward_core(xs, win, wout, bias_ref, n_ref, c_ref, proj_ref, e_ref, inv_ref, out, weights, bias_ready, made):
    for at in range(0, TOK, 48):
        norm_rows(xs, n_ref, at, 48)
    made("n")
    for i in range(6):
        weights[i].wait()
        cols = slice(512 * i, 512 * i + 512)
        proj_ref[:, cols] = dot(n_ref[...], win[:, cols]).astype(BF)
    made("proj")
    bias_ready()

    @pl.loop(0, PAIRS, unroll=8)
    def _(p):
        eighth = head_masks(0.125)
        ones = head_masks(1.0)
        for w in range(MICRO):
            rows = slice(w * WT, w * WT + WT)
            qs = stacked(proj_ref[rows, pair_lanes(p, 0)], eighth)
            k = proj_ref[rows, pair_lanes(p, D)]
            v = proj_ref[rows, pair_lanes(p, 2 * D)]
            s = dot_nt(qs, k) + bias_ref[pair_rows(p), :]
            peak = jnp.max(s, axis=-1, keepdims=True)
            e = jnp.exp(s - peak).astype(BF)
            e_ref[pl.ds(pl.multiple_of((p * 2 + w) * TOK, 16), TOK), :] = e
            wide = [
                jnp.concatenate([v * one, jnp.broadcast_to(one, (WT, 128))], axis=1) for one in ones
            ]
            both = dot(e[:WT], wide[0]) + dot(e[WT:], wide[1])
            inv = 1.0 / both[:, 128:]
            c_ref[rows, pair_lanes(p, 0)] = (both[:, :128] * inv).astype(BF)
            inv_ref[pl.ds(pl.multiple_of((p * 2 + w) * WT, 16), WT), :] = inv.astype(BF)

    made("c")
    weights[6].wait()
    for c in range(0, D, 512):
        out[:, c : c + 512] = xs[:, c : c + 512] + dot(c_ref[...], wout[:, c : c + 512])


def backward_core(xs, go, win, wout, c_ref, proj_ref, e_ref, inv_ref, oh_ref, gctx, gp, bacc, edge, terms, out,
                  weights, ready, late_ref, late_sem):
    sent = []
    lat = lax.axis_index("lat")
    depth = jnp.where(lax.axis_index("section") == 0, lax.rem(lat, GROUP), lax.div(lat, 2 * GROUP))
    part = [lax.rem(depth + step, GROUP) for step in range(GROUP)]
    for step in range(GROUP):
        cols = pl.ds(pl.multiple_of(256 * part[step], 128), 256)
        sent.append(begin(go.at[:, cols], late_ref[step].at[pl.ds(0, TOK), pl.ds(768, 256)], late_sem.at[step, 0]))
    if weights:
        weights[6].wait()
    for c in range(0, D, 256):
        gctx[:, c : c + 256] = dot_nt(go[...], wout[c : c + 256, :]).astype(BF)
    edge[...] = jnp.zeros_like(edge)
    ready()

    @pl.loop(0, PAIRS, unroll=4)
    def _(p):
        eighth = head_masks(0.125)
        ones = head_masks(1.0)
        full = jnp.ones((WT, 128), BF)
        total = None
        for w in range(MICRO):
            rows = slice(w * WT, w * WT + WT)
            qs = stacked(proj_ref[rows, pair_lanes(p, 0)], eighth)
            k = proj_ref[rows, pair_lanes(p, D)]
            v = proj_ref[rows, pair_lanes(p, 2 * D)]
            e = e_ref[pl.ds(pl.multiple_of((p * 2 + w) * TOK, 16), TOK), :]
            inv = inv_ref[pl.ds(pl.multiple_of((p * 2 + w) * WT, 16), WT), :]
            dc = (gctx[rows, pair_lanes(p, 0)].astype(F32) * inv.astype(F32)).astype(BF)
            dcs = stacked(dc, ones)
            along = -(dc.astype(F32) * c_ref[rows, pair_lanes(p, 0)].astype(F32))
            alongs = stacked(along.astype(BF), ones)
            slope = dot_nt(jnp.concatenate([dcs, alongs], axis=1), jnp.concatenate([v, full], axis=1))
            ds = e.astype(F32) * slope
            total = ds if total is None else total + ds
            dsb = ds.astype(BF)
            gp[rows, pair_lanes(p, 2 * D)] = dot_tn(e, dcs).astype(BF)
            gp[rows, pair_lanes(p, D)] = dot_tn(dsb, qs).astype(BF)
            ks = [k * one for one in eighth]
            gp[rows, pair_lanes(p, 0)] = (dot(dsb[:WT], ks[0]) + dot(dsb[WT:], ks[1])).astype(BF)
        bacc[pair_rows(p), :] = total[:, :128]
        edge[pair_rows(p), : WT - 128] = total[:, 128:]

    for step in range(GROUP):
        cols = pl.ds(pl.multiple_of(768 * part[step], 128), 768)
        sent.append(begin(gp.at[:, cols], late_ref[step].at[pl.ds(0, TOK), pl.ds(0, 768)], late_sem.at[step, 1]))

    acc = [jnp.zeros((BIAS_ROWS, 256), F32) for _ in range(3)]
    blank = jnp.zeros((BIAS_ROWS, 128), F32)
    for rq in range(6):
        got = []
        for lq in range(2):
            taken = [pl.ds((rq * 12 + cq) * 2 + lq, 16, stride=WT) for cq in range(12)]
            x = jnp.concatenate(
                [jnp.concatenate([ref[rows, :] for rows in taken], axis=0) for ref in (bacc, edge)], axis=1
            )
            top = x.astype(BF)
            low = (x - top.astype(F32)).astype(BF)
            got.append(dot(top, oh_ref[...]) + dot(low, oh_ref[...]))
        levels = [got[0][:, 128:], got[0][:, :128] + got[1][:, 128:], got[1][:, :128]]
        for dl in range(3):
            for cq in range(12):
                one = jnp.concatenate([levels[dl][cq * 16 : cq * 16 + 16], blank], axis=1)
                shift = ROW_STEP * rq + cq
                acc[dl] = acc[dl] + (pltpu.roll(one, shift, 1) if shift else one)
    folded = jnp.zeros((BIAS_ROWS, OPAD), F32)
    for dl in range(3):
        one = jnp.concatenate([acc[dl], jnp.zeros((BIAS_ROWS, OPAD - 256), F32)], axis=1)
        folded = folded + (pltpu.roll(one, LEVEL_STEP * dl, 1) if dl else one)
    terms[:, :OPAD] = folded.astype(BF)
    terms[:, OPAD:] = jnp.zeros((BIAS_ROWS, D - OPAD), BF)
    for step in range(GROUP):
        sent.append(begin(terms, late_ref[step].at[pl.ds(TOK, BIAS_ROWS), :], late_sem.at[step, 2]))

    if weights:
        for i in range(6):
            weights[i].wait()
    for c in range(0, D, 256):
        out[:, c : c + 256] = dot_nt(gp[...], win[c : c + 256, :]).astype(BF).astype(F32)
    for at in range(0, TOK, 48):
        rows = slice(at, at + 48)
        dn = out[rows, :]
        x = xs[rows, :]
        mean = jnp.mean(x, axis=-1, keepdims=True)
        centered = x - mean
        var = jnp.mean(centered * centered, axis=-1, keepdims=True)
        scale = lax.rsqrt(var + NORM_EPS)
        n = centered * scale
        along = jnp.mean(dn * n, axis=-1, keepdims=True)
        level = jnp.mean(dn, axis=-1, keepdims=True)
        dx = (scale * (dn - level - n * along)).astype(BF).astype(F32)
        out[rows, :] = go[rows, :].astype(F32) + dx
    return sent


def first_forward_body(kind, x_ref, cot_ref, table_ref, oht_ref, rdiff, cdiff, pick_ref, win, wout,
                       bias_out, n_out, c_out, proj_out, e_out, inv_out, p0, p1, p2, p3,
                       win_v, wout_v, bias_v, n, c, proj, e, inv, xs, out, tab, tops, mids, lows, tall, edge, wsem, osem):
    @pl.when(lax.axis_index("section") == 0)
    def _():
        begin_weights(win, wout, win_v, wout_v, wsem)

    build_bias(kind, table_ref, oht_ref, rdiff, cdiff, bias_v, tab, tops, mids, lows, tall, edge)
    bias_copy = begin(bias_v, bias_out, osem.at[4])

    @pl.when(lax.axis_index("section") == 0)
    def _():
        weights = [
            pltpu.make_async_copy(win.at[:, pl.ds(512 * i, 512)], win_v.at[:, pl.ds(512 * i, 512)], wsem.at[i])
            for i in range(6)
        ] + [pltpu.make_async_copy(wout, wout_v, wsem.at[6])]
        load_block(x_ref, xs)
        sent = []

        def made(name):
            if name == "n":
                sent.append(begin(n, n_out, osem.at[0]))
            if name == "proj":
                sent.append(begin(proj, proj_out, osem.at[1]))
            if name == "c":
                sent.append(begin(c, c_out, osem.at[2]))
                sent.append(begin(e, e_out, osem.at[3]))
                sent.append(begin(inv, inv_out, osem.at[5]))

        forward_core(xs, win_v, wout_v, bias_v, n, c, proj, e, inv, out, weights, lambda: None, made)
        load_block(cot_ref, xs)
        extract(out[...].astype(BF), xs[...].astype(BF), pick_ref, (p0, p1, p2, p3))
        for one in sent:
            one.wait()

    bias_copy.wait()


def second_body(r0, r1, r2, r3, pick_ref, upper_ref, lower_ref, oh_ref, ca_ref, bias_ref, win, wout,
                mid_out, cb_out, l0, l1, l2, l3, g0, g1, g2, g3,
                win_v, wout_v, c, proj, e, inv, xs, out, go, gctx, gp, bacc, edge, terms,
                wsem, isem, lsem, n, bias_v, second):
    @pl.when(lax.axis_index("section") == 1)
    def _():
        weights = begin_weights(win, wout, win_v, wout_v, wsem)
        bias_copy = begin(bias_ref, bias_v, isem.at[0])
        xs[...] = insert((r0, r1, r2, r3), upper_ref)
        sent = []

        def made(name):
            if name == "n":
                sent.append(begin(n, mid_out, isem.at[1]))
            if name == "c":
                sent.append(begin(c, cb_out, isem.at[2]))

        forward_core(xs, win_v, wout_v, bias_v, n, c, proj, e, inv, out, weights, bias_copy.wait, made)
        second[...] = out[...].astype(BF)
        go[...] = insert((r0, r1, r2, r3), lower_ref).astype(BF)
        sent += backward_core(xs, go, win_v, wout_v, c, proj, e, inv, oh_ref, gctx, gp, bacc, edge, terms,
                              out, None, lambda: None, (l0, l1, l2, l3), lsem)
        extract(out[...].astype(BF), second[...], pick_ref, (g0, g1, g2, g3))
        for one in sent:
            one.wait()

    @pl.when(lax.axis_index("section") == 0)
    def _():
        begin(ca_ref, c, isem.at[1]).wait()
        begin(c, mid_out, isem.at[2]).wait()


def first_backward_body(x_ref, g0, g1, g2, g3, upper_ref, oh_ref,
                        ca_ref, proj_ref, e_ref, inv_ref, win, wout, b0, b1, b2, b3,
                        l0, l1, l2, l3, out_ref,
                        win_v, wout_v, c, proj, e, inv, xs, out, go, gctx, gp, bacc, edge, terms,
                        wsem, isem, lsem, hold):
    @pl.when(lax.axis_index("section") == 0)
    def _():
        weights = [None] * 7
        weights[6] = begin(wout, wout_v, wsem.at[6])
        copies = [
            begin(proj_ref, proj, isem.at[0]),
            begin(e_ref, e, isem.at[1]),
            begin(inv_ref, inv, isem.at[2]),
            begin(ca_ref, c, isem.at[3]),
        ]
        for i in range(6):
            cols = pl.ds(512 * i, 512)
            weights[i] = begin(win.at[:, cols], win_v.at[:, cols], wsem.at[i])
        go[...] = insert((g0, g1, g2, g3), upper_ref).astype(BF)
        load_block(x_ref, xs)

        def ready():
            for one in copies:
                one.wait()

        sent = backward_core(xs, go, win_v, wout_v, c, proj, e, inv, oh_ref, gctx, gp, bacc, edge, terms,
                             out, weights, ready, (l0, l1, l2, l3), lsem)
        store_block(out, out_ref)
        for one in sent:
            one.wait()

    @pl.when(lax.axis_index("section") == 1)
    def _():
        came = [begin(src, hold.at[j], lsem.at[j, 0]) for j, src in enumerate((b0, b1, b2, b3))]
        gone = []
        for j, dst in enumerate((l0, l1, l2, l3)):
            came[j].wait()
            gone.append(begin(hold.at[j], dst, lsem.at[j, 1]))
        for one in gone:
            one.wait()


def second_result_body(g0, g1, g2, g3, lower_ref, out_ref, xs):
    @pl.when(lax.axis_index("section") == 0)
    def _():
        xs[...] = insert((g0, g1, g2, g3), lower_ref)
        store_block(xs, out_ref)


def flip_body(*refs):
    first, middle, last = (refs[GROUP * i : GROUP * i + GROUP] for i in range(3))
    out_ref, held, sem = refs[3 * GROUP :]

    def copies(normals, contexts):
        return [
            pltpu.make_async_copy(src, held.at[pl.ds(TOK * j, TOK), pl.ds(base, D)], sem.at[j, base // D])
            for base, sources in ((0, normals), (D, contexts))
            for j, src in enumerate(sources)
        ]

    @pl.when(lax.axis_index("section") == 0)
    def _():
        for one in copies(first, middle):
            one.start()

    @pl.when(lax.axis_index("section") == 1)
    def _():
        for one in copies(middle, last):
            one.start()

    for one in copies(first, middle):
        one.wait()

    @pl.loop(0, 8)
    def _(i):
        at = pl.ds(pl.multiple_of(i * 256, 256), 256)
        out_ref[at, :] = held[:, at].T


def weight_body(nct, l0, l1, l2, l3, out, table_ref, grads, made, sem):
    late = (l0, l1, l2, l3)
    table = late[0][TOK:, :OPAD].astype(F32)
    for j in range(GROUP):
        grads[TOK * j : TOK * j + TOK, :] = late[j][:TOK, :]
        if j:
            table = table + late[j][TOK:, :OPAD].astype(F32)
    table_ref[...] = table
    sent = []
    for rb in range(4):
        dst = slice(rb * 16, rb * 16 + 16)
        into = dot(nct[rb * 256 : rb * 256 + 256, :], grads[:, :768])
        for cb in range(6):
            made[dst, cb * 16 : cb * 16 + 16, :] = into[:, cb * 128 : cb * 128 + 128].astype(BF).reshape(16, 16, 128)
        outof = dot(nct[D + rb * 256 : D + rb * 256 + 256, :], grads[:, 768:])
        for cb in range(2):
            made[dst, 96 + cb * 16 : 112 + cb * 16, :] = outof[:, cb * 128 : cb * 128 + 128].astype(BF).reshape(16, 16, 128)
        sent.append(begin(made.at[pl.ds(rb * 16, 16)], out.at[pl.ds(rb * 16, 16)], sem.at[rb]))
    for one in sent:
        one.wait()


def sum_body(in_ref, w_ref):
    def fill(place):
        for part in range(GROUP):
            total = None
            for i in range(4):
                for xh in range(2):
                    for xl in range(2):
                        y, z = place(part, i)
                        one = in_ref[((y * 2 + xh) * 4 + z) * 2 + xl].astype(F32)
                        total = one if total is None else total + one
            for cb in range(6):
                w_ref[:, part * 768 + cb * 128 : part * 768 + cb * 128 + 128] = total[cb * 16 : cb * 16 + 16]
            for cb in range(2):
                at = 3 * D + part * 256 + cb * 128
                w_ref[:, at : at + 128] = total[96 + cb * 16 : 112 + cb * 16]

    @pl.when(lax.axis_index("section") == 0)
    def _():
        fill(lambda part, i: (i, part))

    @pl.when(lax.axis_index("section") == 1)
    def _():
        fill(lambda part, i: (part, i))


def per_device(boundary, tile_kinds, proj_in, proj_out, offset_bias):
    axes = ("lat", "lon", "section")
    nlat, nlon = lax.axis_size("lat"), lax.axis_size("lon")
    section = lax.axis_index("section")
    kind = tile_kinds.reshape(1)
    x = boundary.transpose(0, 1, 3, 4, 2, 5).reshape(TOK // 2, 2, D)
    win = proj_in[0]
    wout = proj_out[0]
    onehot = jnp.asarray(ONEHOT, BF)
    onehot_t = jnp.asarray(ONEHOT.T, BF)
    pick = jnp.asarray(PICK, BF)
    upper = jnp.asarray(UPPER, BF)
    lower = jnp.asarray(LOWER, BF)

    def flat(lat, lon, sec):
        return ((lat % nlat) * nlon + lon % nlon) * 2 + sec

    def roll_pairs(dl, dn, sec):
        return [(flat(i, j, sec), flat(i + dl, j + dn, 1 - sec)) for i in range(nlat) for j in range(nlon)]

    def cross(value, sec):
        return lax.ppermute(value, axes, roll_pairs(0, 0, sec))

    def forth(pieces):
        return [
            lax.ppermute(pieces[(1 - dl) * 2 + (1 - dn)], axes, roll_pairs(-dl, -dn, 0))
            for dl in range(2)
            for dn in range(2)
        ]

    def back(pieces):
        got = [None] * 4
        for dl in range(2):
            for dn in range(2):
                got[(1 - dl) * 2 + (1 - dn)] = lax.ppermute(pieces[dl * 2 + dn], axes, roll_pairs(dl, dn, 1))
        return got

    def rings(axis, sec):
        made = {}
        for y in range(4):
            for x in range(4):
                for z in range(4):
                    key = {"x": (y, z), "y": (x, z), "z": (x, y)}[axis]
                    made.setdefault(key, []).append(flat((y * 2 + x // 2) * 4 + z, x % 2, sec))
        return [made[key] for key in sorted(made)]

    def gather(value, groups):
        return deal([value] * GROUP, groups)

    def deal(values, groups):
        return [values[0]] + [
            lax.ppermute(values[step], axes, [(g[m], g[(m + step) % GROUP]) for g in groups for m in range(GROUP)])
            for step in range(1, GROUP)
        ]

    quarter = [shape(2 * QT, D)] * 4
    block = shape(TOK // 2, 2, D)
    f32 = functools.partial(shape, dtype=F32)
    vf32 = lambda *dims: pltpu.VMEM(dims, F32)
    vbf = lambda *dims: pltpu.VMEM(dims, BF)
    dma = lambda *dims: pltpu.SemaphoreType.DMA(dims)
    wide = shape(TOK, 3 * D)
    whole = shape(TOK, D)
    exps = shape(PAIRS * MICRO * TOK, WT)
    invs = shape(PAIRS * MICRO * WT, 128)
    late_shape = [shape(TOK + BIAS_ROWS, D)] * GROUP
    weights_v = [vbf(D, 3 * D), vbf(D, D)]
    soft_v = [vbf(PAIRS * MICRO * TOK, WT), vbf(PAIRS * MICRO * WT, 128)]
    tall = [vf32(HEADS * WT, 128), vf32(HEADS * WT, 128)]
    pieces_v = [vbf(3 * 1152, 128)] * 3
    front_v = [vf32(HEADS * WT, WT), vbf(TOK, D), vbf(TOK, D), vbf(TOK, 3 * D)] + soft_v + [vf32(TOK, D), vf32(TOK, D)]
    back_v = (
        weights_v
        + [vbf(TOK, D), vbf(TOK, 3 * D)] + soft_v + [vf32(TOK, D), vf32(TOK, D)]
        + [vbf(TOK, D), vbf(TOK, D), vbf(TOK, 3 * D)]
        + tall
        + [vbf(BIAS_ROWS, D), dma(7), dma(4), dma(GROUP, 3)]
    )

    bias, n_a, c_a, proj_a, e_a, inv_a, *pieces = call(
        first_forward_body, "first_forward", [f32(HEADS * WT, WT), whole, whole, wide, exps, invs] + quarter,
        [SMEM] + [VMEM] * 7 + [HBM] * 2,
        weights_v + front_v + [vf32(HEADS, OPAD)] + pieces_v + tall + [dma(7), dma(6)],
        5_000_000_000, 20_000_000, [HBM] * 6 + [VMEM] * 4,
    )(kind, x, cross(x, 1), offset_bias[0], onehot_t, jnp.asarray(ROWS_DIFFER), jnp.asarray(COLS_DIFFER), pick, win, wout)
    received = forth(pieces)
    received, n_a = lax.optimization_barrier((received, n_a))
    early = gather(n_a, rings("z", 0))

    middle, c_b, *pieces = call(
        second_body, "second_both", [whole] * 2 + late_shape + quarter,
        [VMEM] * 8 + [HBM] * 4,
        back_v + [vbf(TOK, D), vf32(HEADS * WT, WT), vbf(TOK, D)], 12_000_000_000, 20_000_000, [HBM] * 6 + [VMEM] * 4,
    )(*received, pick, upper, lower, onehot, c_a, bias, win, wout)
    late_b, grads = pieces[:4], pieces[4:]
    grads, early = lax.optimization_barrier((grads, early))
    grads = back(grads)
    grads, middle, c_b = lax.optimization_barrier((grads, middle, c_b))
    middle = gather(middle, rings("z", 0) + rings("y", 1))

    *late, grad_in = call(
        first_backward_body, "first_backward", late_shape + [block],
        [VMEM] * 7 + [HBM] * 10,
        back_v + [vbf(GROUP, TOK + BIAS_ROWS, D)], 8_000_000_000, 20_000_000, [HBM] * 4 + [VMEM],
    )(x, *grads, upper, onehot, c_a, proj_a, e_a, inv_a, win, wout, *late_b)
    late, grad_in, grads, c_b, middle = lax.optimization_barrier((late, grad_in, grads, c_b, middle))
    last = gather(c_b, rings("y", 1))
    late = deal(late, rings("z", 0) + rings("y", 1))

    flipped = call(
        flip_body, "flip", shape(2 * D, GROUP * TOK), [HBM] * 12,
        [vbf(GROUP * TOK, 2 * D), dma(GROUP, 2)], 10_000_000, 10_000_000, limit=SMALL,
    )(*early, *middle, *last)
    second_out = call(
        second_result_body, "second_result", block, [VMEM] * 5, [vf32(TOK, D)], 170_000_000, 2_000_000, limit=SMALL,
    )(*grads, lower)

    terms, table = call(
        weight_body, "weight_terms", [shape(64, 128, 128), f32(HEADS, OPAD)], [VMEM] * 5,
        [vbf(GROUP * TOK, D), vbf(64, 128, 128), dma(4)], 2_400_000_000, 10_000_000, [HBM, VMEM], limit=SMALL,
    )(flipped, *late)
    terms, second_out = lax.optimization_barrier((terms, second_out))
    terms = lax.all_to_all(terms, ("lat", "lon"), 0, 0, tiled=True)
    result = jnp.where(section == 0, grad_in, cross(second_out, 0))
    result = result.reshape(1, MICRO, 6, 12, 2, D).transpose(0, 1, 4, 2, 3, 5)
    table = sum(gather(table, rings("y", 0) + rings("z", 1)))
    table = sum(gather(table, rings("x", 0) + rings("x", 1)))

    weights = call(
        sum_body, "sum_terms", f32(16, 4 * D), [VMEM], [], 3_000_000, 3_000_000, limit=SMALL,
    )(terms)
    return (result, weights[None], table[None, :, :OFFSETS])


def solution(mesh):
    return jax.shard_map(
        per_device,
        mesh=mesh,
        in_specs=(
            P("section", None, None, "lat", "lon", None),
            P("section", "lat", "lon"),
            P("section", None, None),
            P("section", None, None),
            P("section", None, None),
        ),
        out_specs=(
            P("section", None, None, "lat", "lon", None),
            P("section", ("lat", "lon"), None),
            P("section", None, None),
        ),
        check_vma=False,
    )
```

```python
import functools

import jax
import jax.numpy as jnp
import numpy as np
from jax import lax
from jax.experimental import pallas as pl
from jax.experimental.pallas import tpu as pltpu
from jax.sharding import PartitionSpec as P

D = 1024
HEADS = 16
LEV = 2
MICRO = 2
WIN_LAT = 6
WIN_LON = 12
WT = 144
TOK = MICRO * WT
QT = TOK // 4
OFFSETS = 759
OPAD = 768
LEVEL_STEP = 253
ROW_STEP = 23
PAIRS = HEADS // 2
GROUP = 4
BIAS_ROWS = 16
NORM_EPS = 1e-05
MASKED = -1e30
BF = jnp.bfloat16
F32 = jnp.float32
VLIMIT = 58 * 1024 * 1024
SMALL = 24 * 1024 * 1024

HBM = pl.BlockSpec(memory_space=pltpu.HBM)
VMEM = pl.BlockSpec(memory_space=pltpu.VMEM)
SMEM = pl.BlockSpec(memory_space=pltpu.SMEM)


def constants():
    tok = np.arange(WT)
    row, col, lev = tok // 24, tok // 2 % 12, tok % 2
    onehot = np.zeros((256, 256), np.float32)
    onehot[tok, 128 * lev + 126 - 23 * row - col] = 1
    rows_differ = ((row < 3)[:, None] != (row < 3)[None, :]).astype(np.float32)
    cols_differ = ((col < 6)[:, None] != (col < 6)[None, :]).astype(np.float32)
    pick = np.zeros((4, QT, TOK), np.float32)
    for half_row in range(2):
        for half_col in range(2):
            at = 0
            for micro in range(MICRO):
                for level in range(LEV):
                    for r in range(3):
                        for c in range(6):
                            src = micro * WT + ((3 * half_row + r) * 12 + 6 * half_col + c) * 2 + level
                            pick[half_row * 2 + half_col, at, src] = 1
                            at += 1
    upper = np.concatenate([pick, np.zeros_like(pick)], axis=1).transpose(0, 2, 1)
    lower = np.concatenate([np.zeros_like(pick), pick], axis=1).transpose(0, 2, 1)
    return onehot, rows_differ, cols_differ, pick, upper, lower


ONEHOT, ROWS_DIFFER, COLS_DIFFER, PICK, UPPER, LOWER = constants()


def dot(a, b):
    return jnp.dot(a, b, preferred_element_type=F32)


def dot_nt(a, b):
    return lax.dot_general(a, b, (((1,), (1,)), ((), ())), preferred_element_type=F32)


def dot_tn(a, b):
    return lax.dot_general(a, b, (((0,), (0,)), ((), ())), preferred_element_type=F32)


def call(body, name, out_shape, in_specs, scratch, flops, nbytes, out_specs=None, limit=VLIMIT):
    if out_specs is None:
        out_specs = jax.tree.map(lambda _: VMEM, out_shape)
    return pl.pallas_call(
        body,
        out_shape=out_shape,
        in_specs=in_specs,
        out_specs=out_specs,
        scratch_shapes=scratch,
        compiler_params=pltpu.CompilerParams(vmem_limit_bytes=limit),
        cost_estimate=pl.CostEstimate(flops=flops, bytes_accessed=nbytes, transcendentals=0),
        name=name,
    )


def begin(src, dst, sem):
    copy = pltpu.make_async_copy(src, dst, sem)
    copy.start()
    return copy


def begin_weights(win, wout, win_v, wout_v, sem):
    made = []
    for i in range(6):
        cols = pl.ds(512 * i, 512)
        made.append(begin(win.at[:, cols], win_v.at[:, cols], sem.at[i]))
    made.append(begin(wout, wout_v, sem.at[6]))
    return made


def shape(*dims, dtype=BF):
    return jax.ShapeDtypeStruct(dims, dtype)


def load_block(x_ref, dst):
    dst[...] = x_ref[...].astype(F32).reshape(TOK, D)


def store_block(src, out_ref):
    out_ref[...] = src[...].astype(BF).reshape(TOK // 2, 2, D)


def insert(piece_refs, pick_ref):
    total = dot(pick_ref[0], piece_refs[0][...])
    for q in range(1, 4):
        total = total + dot(pick_ref[q], piece_refs[q][...])
    return total


def extract(first, second, pick_ref, out_refs):
    for q in range(4):
        out_refs[q][...] = jnp.concatenate([dot(pick_ref[q], first), dot(pick_ref[q], second)], axis=0).astype(BF)


def build_bias(kind, table_ref, oht_ref, rdiff, cdiff, out, tab, tops, mids, lows, tall, edge):
    tab[...] = jnp.zeros_like(tab)
    tab[:, :OFFSETS] = table_ref[...]
    for dl in range(3):
        for rq in range(6):
            for cq in range(12):
                start = LEVEL_STEP * dl + ROW_STEP * rq + cq
                at = ((dl * 6 + rq) * 12 + cq) * 16
                x = tab[:, start : start + 128]
                top = x.astype(BF)
                rest = x - top.astype(F32)
                mid = rest.astype(BF)
                tops[at : at + 16, :] = top
                mids[at : at + 16, :] = mid
                lows[at : at + 16, :] = (rest - mid.astype(F32)).astype(BF)
    for lq in range(2):
        for rq in range(6):
            one = ((1 + lq) * 6 + rq) * 192
            two = (lq * 6 + rq) * 192
            got = None
            for piece in (tops, mids, lows):
                x = jnp.concatenate([piece[one : one + 192, :], piece[two : two + 192, :]], axis=1)
                part = dot(x, oht_ref[...])
                got = part if got is None else got + part
            for cq in range(12):
                rows = pl.ds((rq * 12 + cq) * 2 + lq, 16, stride=WT)
                tall[rows, :] = got[cq * 16 : cq * 16 + 16, :128]
                edge[rows, :] = got[cq * 16 : cq * 16 + 16, 128:]
    split_rows = (kind[0] % 2).astype(F32)
    split_cols = (kind[0] // 2).astype(F32)
    closed = rdiff[...] * split_rows + cdiff[...] * split_cols > 0.0
    for h in range(HEADS):
        rows = slice(h * WT, h * WT + WT)
        out[rows, :128] = jnp.where(closed[:, :128], MASKED, tall[rows, :])
        out[rows, 128:] = jnp.where(closed[:, 128:], MASKED, edge[rows, : WT - 128])


def head_masks(scale):
    lane = lax.broadcasted_iota(jnp.int32, (1, 128), 1)
    low = jnp.where(lane < 64, scale, 0.0).astype(BF)
    high = jnp.where(lane >= 64, scale, 0.0).astype(BF)
    return low, high


def stacked(block, masks):
    return jnp.concatenate([block * masks[0], block * masks[1]], axis=0)


def norm_rows(xs, n_ref, at, count):
    x = xs[at : at + count, :]
    mean = jnp.mean(x, axis=-1, keepdims=True)
    centered = x - mean
    var = jnp.mean(centered * centered, axis=-1, keepdims=True)
    n_ref[at : at + count, :] = (centered * lax.rsqrt(var + NORM_EPS)).astype(BF)


def pair_lanes(p, base):
    return pl.ds(pl.multiple_of(base + p * 128, 128), 128)


def pair_rows(p):
    return pl.ds(pl.multiple_of(p * TOK, 8), TOK)


def forward_core(xs, win, wout, bias_ref, n_ref, c_ref, proj_ref, e_ref, inv_ref, out, weights, bias_ready, made):
    for at in range(0, TOK, 48):
        norm_rows(xs, n_ref, at, 48)
    made("n")
    for i in range(6):
        weights[i].wait()
        cols = slice(512 * i, 512 * i + 512)
        proj_ref[:, cols] = dot(n_ref[...], win[:, cols]).astype(BF)
    made("proj")
    bias_ready()

    @pl.loop(0, PAIRS, unroll=8)
    def _(p):
        eighth = head_masks(0.125)
        ones = head_masks(1.0)
        for w in range(MICRO):
            rows = slice(w * WT, w * WT + WT)
            qs = stacked(proj_ref[rows, pair_lanes(p, 0)], eighth)
            k = proj_ref[rows, pair_lanes(p, D)]
            v = proj_ref[rows, pair_lanes(p, 2 * D)]
            s = dot_nt(qs, k) + bias_ref[pair_rows(p), :]
            peak = jnp.max(s, axis=-1, keepdims=True)
            e = jnp.exp(s - peak).astype(BF)
            e_ref[pl.ds(pl.multiple_of((p * 2 + w) * TOK, 16), TOK), :] = e
            wide = [
                jnp.concatenate([v * one, jnp.broadcast_to(one, (WT, 128))], axis=1) for one in ones
            ]
            both = dot(e[:WT], wide[0]) + dot(e[WT:], wide[1])
            inv = 1.0 / both[:, 128:]
            c_ref[rows, pair_lanes(p, 0)] = (both[:, :128] * inv).astype(BF)
            inv_ref[pl.ds(pl.multiple_of((p * 2 + w) * WT, 16), WT), :] = inv.astype(BF)

    made("c")
    weights[6].wait()
    for c in range(0, D, 512):
        out[:, c : c + 512] = xs[:, c : c + 512] + dot(c_ref[...], wout[:, c : c + 512])


def ring_depth():
    lat = lax.axis_index("lat")
    return jnp.where(lax.axis_index("section") == 0, lax.rem(lat, GROUP), lax.div(lat, 2 * GROUP))


def backward_core(xs, go, win, wout, c_ref, proj_ref, e_ref, inv_ref, oh_ref, gctx, gp, bacc, edge, terms, out,
                  weights, ready, late_ref, late_sem):
    sent = []
    depth = ring_depth()
    part = [lax.rem(depth + step, GROUP) for step in range(GROUP)]
    for step in range(GROUP):
        cols = pl.ds(pl.multiple_of(256 * part[step], 128), 256)
        sent.append(begin(go.at[:, cols], late_ref[step].at[pl.ds(0, TOK), pl.ds(768, 256)], late_sem.at[step, 0]))
    if weights:
        weights[6].wait()
    for c in range(0, D, 256):
        gctx[:, c : c + 256] = dot_nt(go[...], wout[c : c + 256, :]).astype(BF)
    edge[...] = jnp.zeros_like(edge)
    ready()

    @pl.loop(0, PAIRS, unroll=4)
    def _(p):
        eighth = head_masks(0.125)
        ones = head_masks(1.0)
        full = jnp.ones((WT, 128), BF)
        total = None
        for w in range(MICRO):
            rows = slice(w * WT, w * WT + WT)
            qs = stacked(proj_ref[rows, pair_lanes(p, 0)], eighth)
            k = proj_ref[rows, pair_lanes(p, D)]
            v = proj_ref[rows, pair_lanes(p, 2 * D)]
            e = e_ref[pl.ds(pl.multiple_of((p * 2 + w) * TOK, 16), TOK), :]
            inv = inv_ref[pl.ds(pl.multiple_of((p * 2 + w) * WT, 16), WT), :]
            dc = (gctx[rows, pair_lanes(p, 0)].astype(F32) * inv.astype(F32)).astype(BF)
            dcs = stacked(dc, ones)
            along = -(dc.astype(F32) * c_ref[rows, pair_lanes(p, 0)].astype(F32))
            alongs = stacked(along.astype(BF), ones)
            slope = dot_nt(jnp.concatenate([dcs, alongs], axis=1), jnp.concatenate([v, full], axis=1))
            ds = e.astype(F32) * slope
            total = ds if total is None else total + ds
            dsb = ds.astype(BF)
            gp[rows, pair_lanes(p, 2 * D)] = dot_tn(e, dcs).astype(BF)
            gp[rows, pair_lanes(p, D)] = dot_tn(dsb, qs).astype(BF)
            ks = [k * one for one in eighth]
            gp[rows, pair_lanes(p, 0)] = (dot(dsb[:WT], ks[0]) + dot(dsb[WT:], ks[1])).astype(BF)
        bacc[pair_rows(p), :] = total[:, :128]
        edge[pair_rows(p), : WT - 128] = total[:, 128:]

    for step in range(GROUP):
        cols = pl.ds(pl.multiple_of(768 * part[step], 128), 768)
        sent.append(begin(gp.at[:, cols], late_ref[step].at[pl.ds(0, TOK), pl.ds(0, 768)], late_sem.at[step, 1]))

    acc = [jnp.zeros((BIAS_ROWS, 256), F32) for _ in range(3)]
    blank = jnp.zeros((BIAS_ROWS, 128), F32)
    for rq in range(6):
        got = []
        for lq in range(2):
            taken = [pl.ds((rq * 12 + cq) * 2 + lq, 16, stride=WT) for cq in range(12)]
            x = jnp.concatenate(
                [jnp.concatenate([ref[rows, :] for rows in taken], axis=0) for ref in (bacc, edge)], axis=1
            )
            top = x.astype(BF)
            low = (x - top.astype(F32)).astype(BF)
            got.append(dot(top, oh_ref[...]) + dot(low, oh_ref[...]))
        levels = [got[0][:, 128:], got[0][:, :128] + got[1][:, 128:], got[1][:, :128]]
        for dl in range(3):
            for cq in range(12):
                one = jnp.concatenate([levels[dl][cq * 16 : cq * 16 + 16], blank], axis=1)
                shift = ROW_STEP * rq + cq
                acc[dl] = acc[dl] + (pltpu.roll(one, shift, 1) if shift else one)
    folded = jnp.zeros((BIAS_ROWS, OPAD), F32)
    for dl in range(3):
        one = jnp.concatenate([acc[dl], jnp.zeros((BIAS_ROWS, OPAD - 256), F32)], axis=1)
        folded = folded + (pltpu.roll(one, LEVEL_STEP * dl, 1) if dl else one)
    terms[:, :OPAD] = folded.astype(BF)
    terms[:, OPAD:] = jnp.zeros((BIAS_ROWS, D - OPAD), BF)
    for step in range(GROUP):
        sent.append(begin(terms, late_ref[step].at[pl.ds(TOK, BIAS_ROWS), :], late_sem.at[step, 2]))

    if weights:
        for i in range(6):
            weights[i].wait()
    for c in range(0, D, 256):
        out[:, c : c + 256] = dot_nt(gp[...], win[c : c + 256, :]).astype(BF).astype(F32)
    for at in range(0, TOK, 48):
        rows = slice(at, at + 48)
        dn = out[rows, :]
        x = xs[rows, :]
        mean = jnp.mean(x, axis=-1, keepdims=True)
        centered = x - mean
        var = jnp.mean(centered * centered, axis=-1, keepdims=True)
        scale = lax.rsqrt(var + NORM_EPS)
        n = centered * scale
        along = jnp.mean(dn * n, axis=-1, keepdims=True)
        level = jnp.mean(dn, axis=-1, keepdims=True)
        dx = (scale * (dn - level - n * along)).astype(BF).astype(F32)
        out[rows, :] = go[rows, :].astype(F32) + dx
    return sent


def first_forward_body(kind, x_ref, cot_ref, table_ref, oht_ref, rdiff, cdiff, pick_ref, win, wout,
                       bias_out, n_out, c_out, proj_out, e_out, inv_out, p0, p1, p2, p3,
                       win_v, wout_v, bias_v, n, c, proj, e, inv, xs, out, tab, tops, mids, lows, tall, edge, wsem, osem):
    @pl.when(lax.axis_index("section") == 0)
    def _():
        begin_weights(win, wout, win_v, wout_v, wsem)

    build_bias(kind, table_ref, oht_ref, rdiff, cdiff, bias_v, tab, tops, mids, lows, tall, edge)
    bias_copy = begin(bias_v, bias_out, osem.at[4])

    @pl.when(lax.axis_index("section") == 0)
    def _():
        weights = [
            pltpu.make_async_copy(win.at[:, pl.ds(512 * i, 512)], win_v.at[:, pl.ds(512 * i, 512)], wsem.at[i])
            for i in range(6)
        ] + [pltpu.make_async_copy(wout, wout_v, wsem.at[6])]
        load_block(x_ref, xs)
        sent = []

        def made(name):
            if name == "n":
                sent.append(begin(n, n_out, osem.at[0]))
            if name == "proj":
                sent.append(begin(proj, proj_out, osem.at[1]))
            if name == "c":
                sent.append(begin(c, c_out, osem.at[2]))
                sent.append(begin(e, e_out, osem.at[3]))
                sent.append(begin(inv, inv_out, osem.at[5]))

        forward_core(xs, win_v, wout_v, bias_v, n, c, proj, e, inv, out, weights, lambda: None, made)
        load_block(cot_ref, xs)
        extract(out[...].astype(BF), xs[...].astype(BF), pick_ref, (p0, p1, p2, p3))
        for one in sent:
            one.wait()

    bias_copy.wait()


def second_body(r0, r1, r2, r3, pick_ref, upper_ref, lower_ref, oh_ref, na_ref, ca_ref, bias_ref, win, wout,
                nc_out, l0, l1, l2, l3, g0, g1, g2, g3,
                win_v, wout_v, c, proj, e, inv, xs, out, go, gctx, gp, bacc, edge, terms,
                wsem, isem, lsem, n, bias_v, second):
    @pl.when(lax.axis_index("section") == 1)
    def _():
        weights = begin_weights(win, wout, win_v, wout_v, wsem)
        bias_copy = begin(bias_ref, bias_v, isem.at[0])
        xs[...] = insert((r0, r1, r2, r3), upper_ref)
        sent = []

        def made(name):
            if name == "n":
                sent.append(begin(n, nc_out.at[:, pl.ds(0, D)], isem.at[1]))
            if name == "c":
                sent.append(begin(c, nc_out.at[:, pl.ds(D, D)], isem.at[2]))

        forward_core(xs, win_v, wout_v, bias_v, n, c, proj, e, inv, out, weights, bias_copy.wait, made)
        second[...] = out[...].astype(BF)
        go[...] = insert((r0, r1, r2, r3), lower_ref).astype(BF)
        sent += backward_core(xs, go, win_v, wout_v, c, proj, e, inv, oh_ref, gctx, gp, bacc, edge, terms,
                              out, None, lambda: None, (l0, l1, l2, l3), lsem)
        extract(out[...].astype(BF), second[...], pick_ref, (g0, g1, g2, g3))
        for one in sent:
            one.wait()

    @pl.when(lax.axis_index("section") == 0)
    def _():
        came = [begin(na_ref, n, isem.at[0]), begin(ca_ref, c, isem.at[1])]
        came[0].wait()
        gone = begin(n, nc_out.at[:, pl.ds(0, D)], isem.at[2])
        came[1].wait()
        begin(c, nc_out.at[:, pl.ds(D, D)], isem.at[3]).wait()
        gone.wait()


def first_backward_body(x_ref, g0, g1, g2, g3, upper_ref, oh_ref,
                        ca_ref, proj_ref, e_ref, inv_ref, win, wout, b0, b1, b2, b3,
                        l0, l1, l2, l3, out_ref,
                        win_v, wout_v, c, proj, e, inv, xs, out, go, gctx, gp, bacc, edge, terms,
                        wsem, isem, lsem, hold):
    @pl.when(lax.axis_index("section") == 0)
    def _():
        weights = [None] * 7
        weights[6] = begin(wout, wout_v, wsem.at[6])
        copies = [
            begin(proj_ref, proj, isem.at[0]),
            begin(e_ref, e, isem.at[1]),
            begin(inv_ref, inv, isem.at[2]),
            begin(ca_ref, c, isem.at[3]),
        ]
        for i in range(6):
            cols = pl.ds(512 * i, 512)
            weights[i] = begin(win.at[:, cols], win_v.at[:, cols], wsem.at[i])
        go[...] = insert((g0, g1, g2, g3), upper_ref).astype(BF)
        load_block(x_ref, xs)

        def ready():
            for one in copies:
                one.wait()

        sent = backward_core(xs, go, win_v, wout_v, c, proj, e, inv, oh_ref, gctx, gp, bacc, edge, terms,
                             out, weights, ready, (l0, l1, l2, l3), lsem)
        store_block(out, out_ref)
        for one in sent:
            one.wait()

    @pl.when(lax.axis_index("section") == 1)
    def _():
        came = [begin(src, hold.at[j], lsem.at[j, 0]) for j, src in enumerate((b0, b1, b2, b3))]
        gone = []
        for j, dst in enumerate((l0, l1, l2, l3)):
            came[j].wait()
            gone.append(begin(hold.at[j], dst, lsem.at[j, 1]))
        for one in gone:
            one.wait()


def second_result_body(g0, g1, g2, g3, lower_ref, out_ref, xs):
    @pl.when(lax.axis_index("section") == 0)
    def _():
        xs[...] = insert((g0, g1, g2, g3), lower_ref)
        store_block(xs, out_ref)


def flip_body(n0, n1, n2, n3, out_ref, held, sem):
    copies = [begin(src, held.at[pl.ds(TOK * j, TOK)], sem.at[j]) for j, src in enumerate((n0, n1, n2, n3))]
    for one in copies:
        one.wait()

    @pl.loop(0, 8)
    def _(i):
        at = pl.ds(pl.multiple_of(i * 256, 256), 256)
        out_ref[at, :] = held[:, at].T


def weight_body(nct, l0, l1, l2, l3, out, grads, made, tab, sem):
    late = (l0, l1, l2, l3)
    table = late[0][TOK:, :OPAD].astype(F32)
    for j in range(GROUP):
        grads[TOK * j : TOK * j + TOK, :] = late[j][:TOK, :]
        if j:
            table = table + late[j][TOK:, :OPAD].astype(F32)
    tab[...] = table
    depth = ring_depth()
    share = jnp.concatenate(
        [
            tab[:, pl.ds(pl.multiple_of(128 * depth, 128), 128)],
            tab[pl.ds(pl.multiple_of(8 * lax.rem(depth, 2), 8), 8), pl.ds(pl.multiple_of(512 + 128 * lax.div(depth, 2), 128), 128)],
        ],
        axis=0,
    ).astype(BF)
    made[:, 128:, :] = jnp.broadcast_to(share[None], (64, 24, 128))
    sent = []
    for rb in range(4):
        dst = slice(rb * 16, rb * 16 + 16)
        into = dot(nct[rb * 256 : rb * 256 + 256, :], grads[:, :768])
        for cb in range(6):
            made[dst, cb * 16 : cb * 16 + 16, :] = into[:, cb * 128 : cb * 128 + 128].astype(BF).reshape(16, 16, 128)
        outof = dot(nct[D + rb * 256 : D + rb * 256 + 256, :], grads[:, 768:])
        for cb in range(2):
            made[dst, 96 + cb * 16 : 112 + cb * 16, :] = outof[:, cb * 128 : cb * 128 + 128].astype(BF).reshape(16, 16, 128)
        sent.append(begin(made.at[pl.ds(rb * 16, 16)], out.at[pl.ds(rb * 16, 16)], sem.at[rb]))
    for one in sent:
        one.wait()


def sum_body(in_ref, w_ref, b_ref, bias):
    def fill(place):
        for part in range(GROUP):
            total = None
            for i in range(4):
                for xh in range(2):
                    for xl in range(2):
                        y, z = place(part, i)
                        one = in_ref[((y * 2 + xh) * 4 + z) * 2 + xl].astype(F32)
                        total = one if total is None else total + one
            for cb in range(6):
                w_ref[:, part * 768 + cb * 128 : part * 768 + cb * 128 + 128] = total[cb * 16 : cb * 16 + 16]
            for cb in range(2):
                at = 3 * D + part * 256 + cb * 128
                w_ref[:, at : at + 128] = total[96 + cb * 16 : 112 + cb * 16]
            bias[:, part * 128 : part * 128 + 128] = total[128:144]
            at = 8 * (part % 2)
            bias[at : at + 8, 512 + 128 * (part // 2) : 640 + 128 * (part // 2)] = total[144:152]
        b_ref[...] = bias[:, :OFFSETS]

    @pl.when(lax.axis_index("section") == 0)
    def _():
        fill(lambda part, i: (i, part))

    @pl.when(lax.axis_index("section") == 1)
    def _():
        fill(lambda part, i: (part, i))


def per_device(boundary, tile_kinds, proj_in, proj_out, offset_bias):
    axes = ("lat", "lon", "section")
    nlat, nlon = lax.axis_size("lat"), lax.axis_size("lon")
    section = lax.axis_index("section")
    kind = tile_kinds.reshape(1)
    x = boundary.transpose(0, 1, 3, 4, 2, 5).reshape(TOK // 2, 2, D)
    win = proj_in[0]
    wout = proj_out[0]
    onehot = jnp.asarray(ONEHOT, BF)
    onehot_t = jnp.asarray(ONEHOT.T, BF)
    pick = jnp.asarray(PICK, BF)
    upper = jnp.asarray(UPPER, BF)
    lower = jnp.asarray(LOWER, BF)

    def flat(lat, lon, sec):
        return ((lat % nlat) * nlon + lon % nlon) * 2 + sec

    def roll_pairs(dl, dn, sec):
        return [(flat(i, j, sec), flat(i + dl, j + dn, 1 - sec)) for i in range(nlat) for j in range(nlon)]

    def cross(value, sec):
        return lax.ppermute(value, axes, roll_pairs(0, 0, sec))

    far_first = [(1, 1), (1, 0), (0, 1), (0, 0)]

    def forth(pieces):
        got = [None] * 4
        for dl, dn in far_first:
            piece = pieces[(1 - dl) * 2 + (1 - dn)]
            got[dl * 2 + dn] = lax.ppermute(piece, axes, roll_pairs(-dl, -dn, 0))
        return got

    def back(pieces):
        got = [None] * 4
        for dl, dn in far_first:
            got[(1 - dl) * 2 + (1 - dn)] = lax.ppermute(pieces[dl * 2 + dn], axes, roll_pairs(dl, dn, 1))
        return got

    def rings(axis, sec):
        made = {}
        for y in range(4):
            for x in range(4):
                for z in range(4):
                    key = {"x": (y, z), "y": (x, z), "z": (x, y)}[axis]
                    made.setdefault(key, []).append(flat((y * 2 + x // 2) * 4 + z, x % 2, sec))
        return [made[key] for key in sorted(made)]

    def gather(value, groups):
        return deal([value] * GROUP, groups)

    def deal(values, groups):
        return [values[0]] + [
            lax.ppermute(values[step], axes, [(g[m], g[(m + step) % GROUP]) for g in groups for m in range(GROUP)])
            for step in range(1, GROUP)
        ]

    quarter = [shape(2 * QT, D)] * 4
    block = shape(TOK // 2, 2, D)
    f32 = functools.partial(shape, dtype=F32)
    vf32 = lambda *dims: pltpu.VMEM(dims, F32)
    vbf = lambda *dims: pltpu.VMEM(dims, BF)
    dma = lambda *dims: pltpu.SemaphoreType.DMA(dims)
    wide = shape(TOK, 3 * D)
    whole = shape(TOK, D)
    exps = shape(PAIRS * MICRO * TOK, WT)
    invs = shape(PAIRS * MICRO * WT, 128)
    late_shape = [shape(TOK + BIAS_ROWS, D)] * GROUP
    weights_v = [vbf(D, 3 * D), vbf(D, D)]
    soft_v = [vbf(PAIRS * MICRO * TOK, WT), vbf(PAIRS * MICRO * WT, 128)]
    tall = [vf32(HEADS * WT, 128), vf32(HEADS * WT, 128)]
    pieces_v = [vbf(3 * 1152, 128)] * 3
    front_v = [vf32(HEADS * WT, WT), vbf(TOK, D), vbf(TOK, D), vbf(TOK, 3 * D)] + soft_v + [vf32(TOK, D), vf32(TOK, D)]
    back_v = (
        weights_v
        + [vbf(TOK, D), vbf(TOK, 3 * D)] + soft_v + [vf32(TOK, D), vf32(TOK, D)]
        + [vbf(TOK, D), vbf(TOK, D), vbf(TOK, 3 * D)]
        + tall
        + [vbf(BIAS_ROWS, D), dma(7), dma(4), dma(GROUP, 3)]
    )

    bias, n_a, c_a, proj_a, e_a, inv_a, *pieces = call(
        first_forward_body, "first_forward", [f32(HEADS * WT, WT), whole, whole, wide, exps, invs] + quarter,
        [SMEM] + [VMEM] * 7 + [HBM] * 2,
        weights_v + front_v + [vf32(HEADS, OPAD)] + pieces_v + tall + [dma(7), dma(6)],
        5_000_000_000, 20_000_000, [HBM] * 6 + [VMEM] * 4,
    )(kind, x, cross(x, 1), offset_bias[0], onehot_t, jnp.asarray(ROWS_DIFFER), jnp.asarray(COLS_DIFFER), pick, win, wout)
    received = forth(pieces)
    both, *pieces = call(
        second_body, "second_both", [shape(TOK, 2 * D)] + late_shape + quarter,
        [VMEM] * 8 + [HBM] * 5,
        back_v + [vbf(TOK, D), vf32(HEADS * WT, WT), vbf(TOK, D)], 12_000_000_000, 20_000_000, [HBM] * 5 + [VMEM] * 4,
    )(*received, pick, upper, lower, onehot, n_a, c_a, bias, win, wout)
    late_b, grads = pieces[:4], pieces[4:]
    grads = back(grads)
    grads, both = lax.optimization_barrier((grads, both))
    both = gather(both, rings("z", 0) + rings("y", 1))

    *late, grad_in = call(
        first_backward_body, "first_backward", late_shape + [block],
        [VMEM] * 7 + [HBM] * 10,
        back_v + [vbf(GROUP, TOK + BIAS_ROWS, D)], 8_000_000_000, 20_000_000, [HBM] * 4 + [VMEM],
    )(x, *grads, upper, onehot, c_a, proj_a, e_a, inv_a, win, wout, *late_b)
    late, grad_in, grads = lax.optimization_barrier((late, grad_in, grads))
    late = deal(late, rings("z", 0) + rings("y", 1))

    flipped = call(
        flip_body, "flip", shape(2 * D, GROUP * TOK), [HBM] * 4,
        [vbf(GROUP * TOK, 2 * D), dma(GROUP)], 10_000_000, 10_000_000, limit=SMALL,
    )(*both)
    second_out = call(
        second_result_body, "second_result", block, [VMEM] * 5, [vf32(TOK, D)], 170_000_000, 2_000_000, limit=SMALL,
    )(*grads, lower)

    terms = call(
        weight_body, "weight_terms", shape(64, 152, 128), [VMEM] * 5,
        [vbf(GROUP * TOK, D), vbf(64, 152, 128), vf32(HEADS, OPAD), dma(4)], 2_400_000_000, 10_000_000, HBM, limit=SMALL,
    )(flipped, *late)
    terms, second_out = lax.optimization_barrier((terms, cross(second_out, 0)))
    terms = lax.all_to_all(terms, ("lat", "lon"), 0, 0, tiled=True)
    result = jnp.where(section == 0, grad_in, second_out)
    result = result.reshape(1, MICRO, 6, 12, 2, D).transpose(0, 1, 4, 2, 3, 5)
    weights, table = call(
        sum_body, "sum_terms", [f32(16, 4 * D), f32(HEADS, OFFSETS)], [VMEM], [vf32(HEADS, OPAD)], 3_000_000, 3_000_000, limit=SMALL,
    )(terms)
    return (result, weights[None], table[None])


def solution(mesh):
    return jax.shard_map(
        per_device,
        mesh=mesh,
        in_specs=(
            P("section", None, None, "lat", "lon", None),
            P("section", "lat", "lon"),
            P("section", None, None),
            P("section", None, None),
            P("section", None, None),
        ),
        out_specs=(
            P("section", None, None, "lat", "lon", None),
            P("section", ("lat", "lon"), None),
            P("section", None, None),
        ),
        check_vma=False,
    )
```

```python
import functools

import jax
import jax.numpy as jnp
import numpy as np
from jax import lax
from jax.experimental import pallas as pl
from jax.experimental.pallas import tpu as pltpu
from jax.sharding import PartitionSpec as P

D = 1024
HEADS = 16
LEV = 2
MICRO = 2
WIN_LAT = 6
WIN_LON = 12
WT = 144
TOK = MICRO * WT
QT = TOK // 4
OFFSETS = 759
OPAD = 768
LEVEL_STEP = 253
ROW_STEP = 23
PAIRS = HEADS // 2
GROUP = 4
BIAS_ROWS = 16
NORM_EPS = 1e-05
MASKED = -1e30
BF = jnp.bfloat16
F32 = jnp.float32
VLIMIT = 58 * 1024 * 1024
SMALL = 24 * 1024 * 1024

HBM = pl.BlockSpec(memory_space=pltpu.HBM)
VMEM = pl.BlockSpec(memory_space=pltpu.VMEM)
SMEM = pl.BlockSpec(memory_space=pltpu.SMEM)


def constants():
    tok = np.arange(WT)
    row, col, lev = tok // 24, tok // 2 % 12, tok % 2
    onehot = np.zeros((256, 256), np.float32)
    onehot[tok, 128 * lev + 126 - 23 * row - col] = 1
    rows_differ = ((row < 3)[:, None] != (row < 3)[None, :]).astype(np.float32)
    cols_differ = ((col < 6)[:, None] != (col < 6)[None, :]).astype(np.float32)
    pick = np.zeros((4, QT, TOK), np.float32)
    for half_row in range(2):
        for half_col in range(2):
            at = 0
            for micro in range(MICRO):
                for level in range(LEV):
                    for r in range(3):
                        for c in range(6):
                            src = micro * WT + ((3 * half_row + r) * 12 + 6 * half_col + c) * 2 + level
                            pick[half_row * 2 + half_col, at, src] = 1
                            at += 1
    upper = np.concatenate([pick, np.zeros_like(pick)], axis=1).transpose(0, 2, 1)
    lower = np.concatenate([np.zeros_like(pick), pick], axis=1).transpose(0, 2, 1)
    return onehot, rows_differ, cols_differ, pick, upper, lower


ONEHOT, ROWS_DIFFER, COLS_DIFFER, PICK, UPPER, LOWER = constants()


def dot(a, b):
    return jnp.dot(a, b, preferred_element_type=F32)


def dot_nt(a, b):
    return lax.dot_general(a, b, (((1,), (1,)), ((), ())), preferred_element_type=F32)


def dot_tn(a, b):
    return lax.dot_general(a, b, (((0,), (0,)), ((), ())), preferred_element_type=F32)


def call(body, name, out_shape, in_specs, scratch, flops, nbytes, out_specs=None, limit=VLIMIT):
    if out_specs is None:
        out_specs = jax.tree.map(lambda _: VMEM, out_shape)
    return pl.pallas_call(
        body,
        out_shape=out_shape,
        in_specs=in_specs,
        out_specs=out_specs,
        scratch_shapes=scratch,
        compiler_params=pltpu.CompilerParams(vmem_limit_bytes=limit),
        cost_estimate=pl.CostEstimate(flops=flops, bytes_accessed=nbytes, transcendentals=0),
        name=name,
    )


def begin(src, dst, sem):
    copy = pltpu.make_async_copy(src, dst, sem)
    copy.start()
    return copy


def begin_weights(win, wout, win_v, wout_v, sem):
    made = []
    for i in range(6):
        cols = pl.ds(512 * i, 512)
        made.append(begin(win.at[:, cols], win_v.at[:, cols], sem.at[i]))
    made.append(begin(wout, wout_v, sem.at[6]))
    return made


def shape(*dims, dtype=BF):
    return jax.ShapeDtypeStruct(dims, dtype)


def load_block(x_ref, dst):
    dst[...] = x_ref[...].astype(F32).reshape(TOK, D)


def store_block(src, out_ref):
    out_ref[...] = src[...].astype(BF).reshape(TOK // 2, 2, D)


def insert(piece_refs, pick_ref):
    total = dot(pick_ref[0], piece_refs[0][...])
    for q in range(1, 4):
        total = total + dot(pick_ref[q], piece_refs[q][...])
    return total


def extract(first, second, pick_ref, out_refs):
    for q in range(4):
        out_refs[q][...] = jnp.concatenate([dot(pick_ref[q], first), dot(pick_ref[q], second)], axis=0).astype(BF)


def build_bias(kind, table_ref, oht_ref, rdiff, cdiff, out, tab, tops, mids, lows, tall, edge):
    tab[...] = jnp.zeros_like(tab)
    tab[:, :OFFSETS] = table_ref[...]
    for dl in range(3):
        for rq in range(6):
            for cq in range(12):
                start = LEVEL_STEP * dl + ROW_STEP * rq + cq
                at = ((dl * 6 + rq) * 12 + cq) * 16
                x = tab[:, start : start + 128]
                top = x.astype(BF)
                rest = x - top.astype(F32)
                mid = rest.astype(BF)
                tops[at : at + 16, :] = top
                mids[at : at + 16, :] = mid
                lows[at : at + 16, :] = (rest - mid.astype(F32)).astype(BF)
    for lq in range(2):
        for rq in range(6):
            one = ((1 + lq) * 6 + rq) * 192
            two = (lq * 6 + rq) * 192
            got = None
            for piece in (tops, mids, lows):
                x = jnp.concatenate([piece[one : one + 192, :], piece[two : two + 192, :]], axis=1)
                part = dot(x, oht_ref[...])
                got = part if got is None else got + part
            for cq in range(12):
                rows = pl.ds((rq * 12 + cq) * 2 + lq, 16, stride=WT)
                tall[rows, :] = got[cq * 16 : cq * 16 + 16, :128]
                edge[rows, :] = got[cq * 16 : cq * 16 + 16, 128:]
    split_rows = (kind[0] % 2).astype(F32)
    split_cols = (kind[0] // 2).astype(F32)
    closed = rdiff[...] * split_rows + cdiff[...] * split_cols > 0.0
    for h in range(HEADS):
        rows = slice(h * WT, h * WT + WT)
        out[rows, :128] = jnp.where(closed[:, :128], MASKED, tall[rows, :])
        out[rows, 128:] = jnp.where(closed[:, 128:], MASKED, edge[rows, : WT - 128])


def head_masks(scale):
    lane = lax.broadcasted_iota(jnp.int32, (1, 128), 1)
    low = jnp.where(lane < 64, scale, 0.0).astype(BF)
    high = jnp.where(lane >= 64, scale, 0.0).astype(BF)
    return low, high


def stacked(block, masks):
    return jnp.concatenate([block * masks[0], block * masks[1]], axis=0)


def norm_rows(xs, n_ref, at, count):
    x = xs[at : at + count, :]
    mean = jnp.mean(x, axis=-1, keepdims=True)
    centered = x - mean
    var = jnp.mean(centered * centered, axis=-1, keepdims=True)
    n_ref[at : at + count, :] = (centered * lax.rsqrt(var + NORM_EPS)).astype(BF)


def pair_lanes(p, base):
    return pl.ds(pl.multiple_of(base + p * 128, 128), 128)


def pair_rows(p):
    return pl.ds(pl.multiple_of(p * TOK, 8), TOK)


def forward_core(xs, win, wout, bias_ref, n_ref, c_ref, proj_ref, e_ref, inv_ref, out, weights, bias_ready, made):
    for at in range(0, TOK, 48):
        norm_rows(xs, n_ref, at, 48)
    made("n")
    for i in range(6):
        weights[i].wait()
        cols = slice(512 * i, 512 * i + 512)
        proj_ref[:, cols] = dot(n_ref[...], win[:, cols]).astype(BF)
    made("proj")
    bias_ready()

    @pl.loop(0, PAIRS, unroll=8)
    def _(p):
        eighth = head_masks(0.125)
        ones = head_masks(1.0)
        for w in range(MICRO):
            rows = slice(w * WT, w * WT + WT)
            qs = stacked(proj_ref[rows, pair_lanes(p, 0)], eighth)
            k = proj_ref[rows, pair_lanes(p, D)]
            v = proj_ref[rows, pair_lanes(p, 2 * D)]
            s = dot_nt(qs, k) + bias_ref[pair_rows(p), :]
            peak = jnp.max(s, axis=-1, keepdims=True)
            e = jnp.exp(s - peak).astype(BF)
            e_ref[pl.ds(pl.multiple_of((p * 2 + w) * TOK, 16), TOK), :] = e
            wide = [
                jnp.concatenate([v * one, jnp.broadcast_to(one, (WT, 128))], axis=1) for one in ones
            ]
            both = dot(e[:WT], wide[0]) + dot(e[WT:], wide[1])
            inv = 1.0 / both[:, 128:]
            c_ref[rows, pair_lanes(p, 0)] = (both[:, :128] * inv).astype(BF)
            inv_ref[pl.ds(pl.multiple_of((p * 2 + w) * WT, 16), WT), :] = inv.astype(BF)

    made("c")
    weights[6].wait()
    for c in range(0, D, 512):
        out[:, c : c + 512] = xs[:, c : c + 512] + dot(c_ref[...], wout[:, c : c + 512])


def ring_depth():
    lat = lax.axis_index("lat")
    return jnp.where(lax.axis_index("section") == 0, lax.rem(lat, GROUP), lax.div(lat, 2 * GROUP))


def backward_attention(go, wout, c_ref, proj_ref, e_ref, inv_ref, oh_ref, gctx, gp, bacc, edge, terms,
                       ready, ready_pair, late_ref, late_sem):
    sent = []
    depth = ring_depth()
    part = [lax.rem(depth + step, GROUP) for step in range(GROUP)]
    for step in range(GROUP):
        cols = pl.ds(pl.multiple_of(256 * part[step], 128), 256)
        sent.append(begin(go.at[:, cols], late_ref[step].at[pl.ds(0, TOK), pl.ds(768, 256)], late_sem.at[step, 0]))
    ready(0)
    for c in range(0, D, 256):
        gctx[:, c : c + 256] = dot_nt(go[...], wout[c : c + 256, :]).astype(BF)
    edge[...] = jnp.zeros_like(edge)
    ready(1)

    @pl.loop(0, PAIRS, unroll=4)
    def _(p):
        ready_pair(p)
        eighth = head_masks(0.125)
        ones = head_masks(1.0)
        full = jnp.ones((WT, 128), BF)
        total = None
        for w in range(MICRO):
            rows = slice(w * WT, w * WT + WT)
            qs = stacked(proj_ref[rows, pair_lanes(p, 0)], eighth)
            k = proj_ref[rows, pair_lanes(p, D)]
            v = proj_ref[rows, pair_lanes(p, 2 * D)]
            e = e_ref[pl.ds(pl.multiple_of((p * 2 + w) * TOK, 16), TOK), :]
            inv = inv_ref[pl.ds(pl.multiple_of((p * 2 + w) * WT, 16), WT), :]
            dc = (gctx[rows, pair_lanes(p, 0)].astype(F32) * inv.astype(F32)).astype(BF)
            dcs = stacked(dc, ones)
            along = -(dc.astype(F32) * c_ref[rows, pair_lanes(p, 0)].astype(F32))
            alongs = stacked(along.astype(BF), ones)
            slope = dot_nt(jnp.concatenate([dcs, alongs], axis=1), jnp.concatenate([v, full], axis=1))
            ds = e.astype(F32) * slope
            total = ds if total is None else total + ds
            dsb = ds.astype(BF)
            gp[rows, pair_lanes(p, 2 * D)] = dot_tn(e, dcs).astype(BF)
            gp[rows, pair_lanes(p, D)] = dot_tn(dsb, qs).astype(BF)
            ks = [k * one for one in eighth]
            gp[rows, pair_lanes(p, 0)] = (dot(dsb[:WT], ks[0]) + dot(dsb[WT:], ks[1])).astype(BF)
        bacc[pair_rows(p), :] = total[:, :128]
        edge[pair_rows(p), : WT - 128] = total[:, 128:]

    for step in range(GROUP):
        cols = pl.ds(pl.multiple_of(768 * part[step], 128), 768)
        sent.append(begin(gp.at[:, cols], late_ref[step].at[pl.ds(0, TOK), pl.ds(0, 768)], late_sem.at[step, 1]))

    acc = [jnp.zeros((BIAS_ROWS, 256), F32) for _ in range(3)]
    blank = jnp.zeros((BIAS_ROWS, 128), F32)
    for rq in range(6):
        got = []
        for lq in range(2):
            taken = [pl.ds((rq * 12 + cq) * 2 + lq, 16, stride=WT) for cq in range(12)]
            x = jnp.concatenate(
                [jnp.concatenate([ref[rows, :] for rows in taken], axis=0) for ref in (bacc, edge)], axis=1
            )
            top = x.astype(BF)
            low = (x - top.astype(F32)).astype(BF)
            got.append(dot(top, oh_ref[...]) + dot(low, oh_ref[...]))
        levels = [got[0][:, 128:], got[0][:, :128] + got[1][:, 128:], got[1][:, :128]]
        for dl in range(3):
            for cq in range(12):
                one = jnp.concatenate([levels[dl][cq * 16 : cq * 16 + 16], blank], axis=1)
                shift = ROW_STEP * rq + cq
                acc[dl] = acc[dl] + (pltpu.roll(one, shift, 1) if shift else one)
    folded = jnp.zeros((BIAS_ROWS, OPAD), F32)
    for dl in range(3):
        one = jnp.concatenate([acc[dl], jnp.zeros((BIAS_ROWS, OPAD - 256), F32)], axis=1)
        folded = folded + (pltpu.roll(one, LEVEL_STEP * dl, 1) if dl else one)
    terms[:, :OPAD] = folded.astype(BF)
    terms[:, OPAD:] = jnp.zeros((BIAS_ROWS, D - OPAD), BF)
    for step in range(GROUP):
        sent.append(begin(terms, late_ref[step].at[pl.ds(TOK, BIAS_ROWS), :], late_sem.at[step, 2]))

    return sent


def backward_input(xs, go, win, gp, out):
    for c in range(0, D, 256):
        out[:, c : c + 256] = dot_nt(gp[...], win[c : c + 256, :]).astype(BF).astype(F32)
    for at in range(0, TOK, 48):
        rows = slice(at, at + 48)
        dn = out[rows, :]
        x = xs[rows, :]
        mean = jnp.mean(x, axis=-1, keepdims=True)
        centered = x - mean
        var = jnp.mean(centered * centered, axis=-1, keepdims=True)
        scale = lax.rsqrt(var + NORM_EPS)
        n = centered * scale
        along = jnp.mean(dn * n, axis=-1, keepdims=True)
        level = jnp.mean(dn, axis=-1, keepdims=True)
        dx = (scale * (dn - level - n * along)).astype(BF).astype(F32)
        out[rows, :] = go[rows, :].astype(F32) + dx


def first_forward_body(kind, x_ref, table_ref, oht_ref, rdiff, cdiff, win, wout,
                       bias_out, n_out, c_out, proj_out, e_out, inv_out, first_out,
                       win_v, wout_v, bias_v, n, c, proj, e, inv, xs, out, tab, tops, mids, lows, tall, edge, wsem, osem):
    @pl.when(lax.axis_index("section") == 0)
    def _():
        begin_weights(win, wout, win_v, wout_v, wsem)

    build_bias(kind, table_ref, oht_ref, rdiff, cdiff, bias_v, tab, tops, mids, lows, tall, edge)
    bias_copy = begin(bias_v, bias_out, osem.at[4])

    @pl.when(lax.axis_index("section") == 0)
    def _():
        weights = [
            pltpu.make_async_copy(win.at[:, pl.ds(512 * i, 512)], win_v.at[:, pl.ds(512 * i, 512)], wsem.at[i])
            for i in range(6)
        ] + [pltpu.make_async_copy(wout, wout_v, wsem.at[6])]
        load_block(x_ref, xs)
        sent = []

        def made(name):
            if name == "n":
                sent.append(begin(n, n_out, osem.at[0]))
            if name == "proj":
                sent.append(begin(proj, proj_out, osem.at[1]))
            if name == "c":
                sent.append(begin(c, c_out, osem.at[2]))
                sent.append(begin(e, e_out, osem.at[3]))
                sent.append(begin(inv, inv_out, osem.at[5]))

        forward_core(xs, win_v, wout_v, bias_v, n, c, proj, e, inv, out, weights, lambda: None, made)
        first_out[...] = out[...].astype(BF)
        for one in sent:
            one.wait()

    bias_copy.wait()


def pack_body(first_ref, cot_ref, pick_ref, p0, p1, p2, p3, xs):
    @pl.when(lax.axis_index("section") == 0)
    def _():
        load_block(cot_ref, xs)
        extract(first_ref[...], xs[...].astype(BF), pick_ref, (p0, p1, p2, p3))


def second_body(r0, r1, r2, r3, pick_ref, upper_ref, lower_ref, oh_ref, na_ref, ca_ref, bias_ref, win, wout,
                nc_out, l0, l1, l2, l3, g0, g1, g2, g3,
                win_v, wout_v, c, proj, e, inv, xs, out, go, gctx, gp, bacc, edge, terms,
                wsem, isem, lsem, n, bias_v, second, psem):
    @pl.when(lax.axis_index("section") == 1)
    def _():
        weights = begin_weights(win, wout, win_v, wout_v, wsem)
        bias_copy = begin(bias_ref, bias_v, isem.at[0])
        xs[...] = insert((r0, r1, r2, r3), upper_ref)
        sent = []

        def made(name):
            if name == "n":
                sent.extend(begin(n, nc_out.at[j, :, pl.ds(0, D)], psem.at[j, 0]) for j in range(GROUP))
            if name == "c":
                sent.extend(begin(c, nc_out.at[j, :, pl.ds(D, D)], psem.at[j, 1]) for j in range(GROUP))

        forward_core(xs, win_v, wout_v, bias_v, n, c, proj, e, inv, out, weights, bias_copy.wait, made)
        second[...] = out[...].astype(BF)
        go[...] = insert((r0, r1, r2, r3), lower_ref).astype(BF)
        sent += backward_attention(go, wout_v, c, proj, e, inv, oh_ref, gctx, gp, bacc, edge, terms,
                                   lambda stage: None, lambda p: None, (l0, l1, l2, l3), lsem)
        backward_input(xs, go, win_v, gp, out)
        extract(out[...].astype(BF), second[...], pick_ref, (g0, g1, g2, g3))
        for one in sent:
            one.wait()

    @pl.when(lax.axis_index("section") == 0)
    def _():
        came = [begin(na_ref, n, isem.at[0]), begin(ca_ref, c, isem.at[1])]
        came[0].wait()
        gone = [begin(n, nc_out.at[j, :, pl.ds(0, D)], psem.at[j, 0]) for j in range(GROUP)]
        came[1].wait()
        gone += [begin(c, nc_out.at[j, :, pl.ds(D, D)], psem.at[j, 1]) for j in range(GROUP)]
        for one in gone:
            one.wait()


def first_backward_body(g0, g1, g2, g3, upper_ref, oh_ref, c_ref, proj_ref, e_ref, inv_ref, wout, b0, b1, b2, b3,
                        l0, l1, l2, l3, go_out, gp_out,
                        wout_v, c, proj, e, inv, go, gctx, gp, bacc, edge, terms, grads, upper, oh, hold,
                        isem, esem, lsem):
    @pl.when(lax.axis_index("section") == 0)
    def _():
        first = [begin(src, grads.at[q], isem.at[q]) for q, src in enumerate((g0, g1, g2, g3))]
        first.append(begin(upper_ref, upper, isem.at[4]))
        outer = begin(wout, wout_v, isem.at[5])
        rest = [begin(proj_ref, proj, isem.at[6]), begin(c_ref, c, isem.at[7]), begin(inv_ref, inv, isem.at[8])]

        def pair_copy(p):
            rows = pl.ds(pl.multiple_of(p * 2 * TOK, 16), 2 * TOK)
            return pltpu.make_async_copy(e_ref.at[rows], e.at[rows], esem.at[p])

        for p in range(PAIRS):
            pair_copy(p).start()
        last = begin(oh_ref, oh, isem.at[9])
        for one in first:
            one.wait()
        go[...] = insert([grads.at[q] for q in range(4)], upper).astype(BF)
        go_copy = begin(go, go_out, isem.at[10])

        def ready(stage):
            for one in [outer] if stage == 0 else rest:
                one.wait()

        last.wait()
        sent = backward_attention(go, wout_v, c, proj, e, inv, oh, gctx, gp, bacc, edge, terms,
                                  ready, lambda p: pair_copy(p).wait(), (l0, l1, l2, l3), lsem)
        sent += [go_copy, begin(gp, gp_out, isem.at[11])]
        for one in sent:
            one.wait()

    @pl.when(lax.axis_index("section") == 1)
    def _():
        came = [begin(src, hold.at[j], lsem.at[j, 0]) for j, src in enumerate((b0, b1, b2, b3))]
        gone = []
        for j, dst in enumerate((l0, l1, l2, l3)):
            came[j].wait()
            gone.append(begin(hold.at[j], dst, lsem.at[j, 1]))
        for one in gone:
            one.wait()


def input_grad_body(x_ref, go, gp, win, out_ref, xs, out):
    @pl.when(lax.axis_index("section") == 0)
    def _():
        load_block(x_ref, xs)
        backward_input(xs, go, win, gp, out)
        store_block(out, out_ref)


def second_result_body(g0, g1, g2, g3, lower_ref, out_ref, xs):
    @pl.when(lax.axis_index("section") == 0)
    def _():
        xs[...] = insert((g0, g1, g2, g3), lower_ref)
        store_block(xs, out_ref)


def flip_body(in_ref, out_ref, held, sem):
    source = [lax.rem(ring_depth() + GROUP - step, GROUP) for step in range(GROUP)]
    copies = [begin(in_ref.at[source[j]], held.at[pl.ds(TOK * j, TOK)], sem.at[j]) for j in range(GROUP)]
    for one in copies:
        one.wait()

    @pl.loop(0, 8)
    def _(i):
        at = pl.ds(pl.multiple_of(i * 256, 256), 256)
        out_ref[at, :] = held[:, at].T


def weight_body(nct, l0, l1, l2, l3, out, grads, made, tab, sem):
    late = (l0, l1, l2, l3)
    table = late[0][TOK:, :OPAD].astype(F32)
    for j in range(GROUP):
        grads[TOK * j : TOK * j + TOK, :] = late[j][:TOK, :]
        if j:
            table = table + late[j][TOK:, :OPAD].astype(F32)
    tab[...] = table
    depth = ring_depth()
    share = jnp.concatenate(
        [
            tab[:, pl.ds(pl.multiple_of(128 * depth, 128), 128)],
            tab[pl.ds(pl.multiple_of(8 * lax.rem(depth, 2), 8), 8), pl.ds(pl.multiple_of(512 + 128 * lax.div(depth, 2), 128), 128)],
        ],
        axis=0,
    ).astype(BF)
    made[:, 128:, :] = jnp.broadcast_to(share[None], (64, 24, 128))
    sent = []
    for rb in range(4):
        dst = slice(rb * 16, rb * 16 + 16)
        into = dot(nct[rb * 256 : rb * 256 + 256, :], grads[:, :768])
        for cb in range(6):
            made[dst, cb * 16 : cb * 16 + 16, :] = into[:, cb * 128 : cb * 128 + 128].astype(BF).reshape(16, 16, 128)
        outof = dot(nct[D + rb * 256 : D + rb * 256 + 256, :], grads[:, 768:])
        for cb in range(2):
            made[dst, 96 + cb * 16 : 112 + cb * 16, :] = outof[:, cb * 128 : cb * 128 + 128].astype(BF).reshape(16, 16, 128)
        sent.append(begin(made.at[pl.ds(rb * 16, 16)], out.at[pl.ds(rb * 16, 16)], sem.at[rb]))
    for one in sent:
        one.wait()


def sum_body(in_ref, w_ref, b_ref, bias):
    def fill(place):
        for part in range(GROUP):
            total = None
            for i in range(4):
                for xh in range(2):
                    for xl in range(2):
                        y, z = place(part, i)
                        one = in_ref[((y * 2 + xh) * 4 + z) * 2 + xl].astype(F32)
                        total = one if total is None else total + one
            for cb in range(6):
                w_ref[:, part * 768 + cb * 128 : part * 768 + cb * 128 + 128] = total[cb * 16 : cb * 16 + 16]
            for cb in range(2):
                at = 3 * D + part * 256 + cb * 128
                w_ref[:, at : at + 128] = total[96 + cb * 16 : 112 + cb * 16]
            bias[:, part * 128 : part * 128 + 128] = total[128:144]
            at = 8 * (part % 2)
            bias[at : at + 8, 512 + 128 * (part // 2) : 640 + 128 * (part // 2)] = total[144:152]
        b_ref[...] = bias[:, :OFFSETS]

    @pl.when(lax.axis_index("section") == 0)
    def _():
        fill(lambda part, i: (i, part))

    @pl.when(lax.axis_index("section") == 1)
    def _():
        fill(lambda part, i: (part, i))


def per_device(boundary, tile_kinds, proj_in, proj_out, offset_bias):
    axes = ("lat", "lon", "section")
    nlat, nlon = lax.axis_size("lat"), lax.axis_size("lon")
    section = lax.axis_index("section")
    kind = tile_kinds.reshape(1)
    x = boundary.transpose(0, 1, 3, 4, 2, 5).reshape(TOK // 2, 2, D)
    win = proj_in[0]
    wout = proj_out[0]
    onehot = jnp.asarray(ONEHOT, BF)
    onehot_t = jnp.asarray(ONEHOT.T, BF)
    pick = jnp.asarray(PICK, BF)
    upper = jnp.asarray(UPPER, BF)
    lower = jnp.asarray(LOWER, BF)

    def flat(lat, lon, sec):
        return ((lat % nlat) * nlon + lon % nlon) * 2 + sec

    def roll_pairs(dl, dn, sec):
        return [(flat(i, j, sec), flat(i + dl, j + dn, 1 - sec)) for i in range(nlat) for j in range(nlon)]

    def cross(value, sec):
        return lax.ppermute(value, axes, roll_pairs(0, 0, sec))

    far_first = [(1, 1), (1, 0), (0, 1), (0, 0)]

    def forth(pieces):
        got = [None] * 4
        for dl, dn in far_first:
            piece = pieces[(1 - dl) * 2 + (1 - dn)]
            got[dl * 2 + dn] = lax.ppermute(piece, axes, roll_pairs(-dl, -dn, 0))
        return got

    def back(pieces):
        got = [None] * 4
        for dl, dn in far_first:
            got[(1 - dl) * 2 + (1 - dn)] = lax.ppermute(pieces[dl * 2 + dn], axes, roll_pairs(dl, dn, 1))
        return got

    def rings(axis, sec):
        made = {}
        for y in range(4):
            for x in range(4):
                for z in range(4):
                    key = {"x": (y, z), "y": (x, z), "z": (x, y)}[axis]
                    made.setdefault(key, []).append(flat((y * 2 + x // 2) * 4 + z, x % 2, sec))
        return [made[key] for key in sorted(made)]

    def deal(values, groups):
        return [values[0]] + [
            lax.ppermute(values[step], axes, [(g[m], g[(m + step) % GROUP]) for g in groups for m in range(GROUP)])
            for step in range(1, GROUP)
        ]

    quarter = [shape(2 * QT, D)] * 4
    block = shape(TOK // 2, 2, D)
    f32 = functools.partial(shape, dtype=F32)
    vf32 = lambda *dims: pltpu.VMEM(dims, F32)
    vbf = lambda *dims: pltpu.VMEM(dims, BF)
    dma = lambda *dims: pltpu.SemaphoreType.DMA(dims)
    wide = shape(TOK, 3 * D)
    whole = shape(TOK, D)
    exps = shape(PAIRS * MICRO * TOK, WT)
    invs = shape(PAIRS * MICRO * WT, 128)
    late_shape = [shape(TOK + BIAS_ROWS, D)] * GROUP
    weights_v = [vbf(D, 3 * D), vbf(D, D)]
    soft_v = [vbf(PAIRS * MICRO * TOK, WT), vbf(PAIRS * MICRO * WT, 128)]
    tall = [vf32(HEADS * WT, 128), vf32(HEADS * WT, 128)]
    pieces_v = [vbf(3 * 1152, 128)] * 3
    front_v = [vf32(HEADS * WT, WT), vbf(TOK, D), vbf(TOK, D), vbf(TOK, 3 * D)] + soft_v + [vf32(TOK, D), vf32(TOK, D)]
    back_v = (
        weights_v
        + [vbf(TOK, D), vbf(TOK, 3 * D)] + soft_v + [vf32(TOK, D), vf32(TOK, D)]
        + [vbf(TOK, D), vbf(TOK, D), vbf(TOK, 3 * D)]
        + tall
        + [vbf(BIAS_ROWS, D), dma(7), dma(4), dma(GROUP, 3)]
    )

    cot = cross(x, 1)
    bias, n_a, c_a, proj_a, e_a, inv_a, first_out = call(
        first_forward_body, "first_forward", [f32(HEADS * WT, WT), whole, whole, wide, exps, invs, whole],
        [SMEM] + [VMEM] * 5 + [HBM] * 2,
        weights_v + front_v + [vf32(HEADS, OPAD)] + pieces_v + tall + [dma(7), dma(6)],
        5_000_000_000, 20_000_000, [HBM] * 6 + [VMEM],
    )(kind, x, offset_bias[0], onehot_t, jnp.asarray(ROWS_DIFFER), jnp.asarray(COLS_DIFFER), win, wout)
    pieces = call(
        pack_body, "pack", quarter, [VMEM] * 3, [vf32(TOK, D)], 340_000_000, 3_000_000, limit=SMALL,
    )(first_out, cot, pick)
    received = forth(pieces)
    both, *pieces = call(
        second_body, "second_both", [shape(GROUP, TOK, 2 * D)] + late_shape + quarter,
        [VMEM] * 8 + [HBM] * 5,
        back_v + [vbf(TOK, D), vf32(HEADS * WT, WT), vbf(TOK, D), dma(GROUP, 2)], 12_000_000_000, 20_000_000, [HBM] * 5 + [VMEM] * 4,
    )(*received, pick, upper, lower, onehot, n_a, c_a, bias, win, wout)
    late_b, grads = pieces[:4], pieces[4:]
    grads = back(grads)
    both = lax.all_to_all(both, axes, 0, 0, axis_index_groups=rings("z", 0) + rings("y", 1), tiled=True)

    *late, go_a, gp_a = call(
        first_backward_body, "first_backward", late_shape + [whole, wide],
        [HBM] * 15,
        [vbf(D, D), vbf(TOK, D), vbf(TOK, 3 * D)] + soft_v + [vbf(TOK, D), vbf(TOK, D), vbf(TOK, 3 * D)] + tall
        + [vbf(BIAS_ROWS, D), vbf(4, 2 * QT, D), vbf(4, TOK, 2 * QT), vbf(256, 256)]
        + [vbf(GROUP, TOK + BIAS_ROWS, D), dma(12), dma(PAIRS), dma(GROUP, 3)],
        30_000_000_000, 20_000_000, [HBM] * 6,
    )(*grads, upper, onehot, c_a, proj_a, e_a, inv_a, wout, *late_b)
    late, go_a, gp_a, grads = lax.optimization_barrier((late, go_a, gp_a, grads))
    late = deal(late, rings("z", 0) + rings("y", 1))

    grad_in = call(
        input_grad_body, "input_grad", block, [VMEM] * 4, [vf32(TOK, D), vf32(TOK, D)], 2_000_000_000, 10_000_000,
    )(x, go_a, gp_a, win)
    flipped = call(
        flip_body, "flip", shape(2 * D, GROUP * TOK), [HBM],
        [vbf(GROUP * TOK, 2 * D), dma(GROUP)], 10_000_000, 10_000_000, limit=SMALL,
    )(both)
    second_out = call(
        second_result_body, "second_result", block, [VMEM] * 5, [vf32(TOK, D)], 170_000_000, 2_000_000, limit=SMALL,
    )(*grads, lower)

    terms = call(
        weight_body, "weight_terms", shape(64, 152, 128), [VMEM] * 5,
        [vbf(GROUP * TOK, D), vbf(64, 152, 128), vf32(HEADS, OPAD), dma(4)], 2_400_000_000, 10_000_000, HBM, limit=SMALL,
    )(flipped, *late)
    terms, second_out = lax.optimization_barrier((terms, cross(second_out, 0)))
    terms = lax.all_to_all(terms, ("lat", "lon"), 0, 0, tiled=True)
    result = jnp.where(section == 0, grad_in, second_out)
    result = result.reshape(1, MICRO, 6, 12, 2, D).transpose(0, 1, 4, 2, 3, 5)
    weights, table = call(
        sum_body, "sum_terms", [f32(16, 4 * D), f32(HEADS, OFFSETS)], [VMEM], [vf32(HEADS, OPAD)], 3_000_000, 3_000_000, limit=SMALL,
    )(terms)
    return (result, weights[None], table[None])


def solution(mesh):
    return jax.shard_map(
        per_device,
        mesh=mesh,
        in_specs=(
            P("section", None, None, "lat", "lon", None),
            P("section", "lat", "lon"),
            P("section", None, None),
            P("section", None, None),
            P("section", None, None),
        ),
        out_specs=(
            P("section", None, None, "lat", "lon", None),
            P("section", ("lat", "lon"), None),
            P("section", None, None),
        ),
        check_vma=False,
    )
```

```python
import functools

import jax
import jax.numpy as jnp
import numpy as np
from jax import lax
from jax.experimental import pallas as pl
from jax.experimental.pallas import tpu as pltpu
from jax.sharding import PartitionSpec as P

D = 1024
HEADS = 16
LEV = 2
MICRO = 2
WIN_LAT = 6
WIN_LON = 12
WT = 144
TOK = MICRO * WT
QT = TOK // 4
OFFSETS = 759
OPAD = 768
LEVEL_STEP = 253
ROW_STEP = 23
PAIRS = HEADS // 2
GROUP = 4
BIAS_ROWS = 16
NORM_EPS = 1e-05
MASKED = -1e30
BF = jnp.bfloat16
F32 = jnp.float32
VLIMIT = 58 * 1024 * 1024
SMALL = 24 * 1024 * 1024

HBM = pl.BlockSpec(memory_space=pltpu.HBM)
VMEM = pl.BlockSpec(memory_space=pltpu.VMEM)
SMEM = pl.BlockSpec(memory_space=pltpu.SMEM)


def constants():
    tok = np.arange(WT)
    row, col, lev = tok // 24, tok // 2 % 12, tok % 2
    onehot = np.zeros((256, 256), np.float32)
    onehot[tok, 128 * lev + 126 - 23 * row - col] = 1
    rows_differ = ((row < 3)[:, None] != (row < 3)[None, :]).astype(np.float32)
    cols_differ = ((col < 6)[:, None] != (col < 6)[None, :]).astype(np.float32)
    pick = np.zeros((4, QT, TOK), np.float32)
    for half_row in range(2):
        for half_col in range(2):
            at = 0
            for micro in range(MICRO):
                for level in range(LEV):
                    for r in range(3):
                        for c in range(6):
                            src = micro * WT + ((3 * half_row + r) * 12 + 6 * half_col + c) * 2 + level
                            pick[half_row * 2 + half_col, at, src] = 1
                            at += 1
    upper = np.concatenate([pick, np.zeros_like(pick)], axis=1).transpose(0, 2, 1)
    lower = np.concatenate([np.zeros_like(pick), pick], axis=1).transpose(0, 2, 1)
    return onehot, rows_differ, cols_differ, pick, upper, lower


ONEHOT, ROWS_DIFFER, COLS_DIFFER, PICK, UPPER, LOWER = constants()


def dot(a, b):
    return jnp.dot(a, b, preferred_element_type=F32)


def dot_nt(a, b):
    return lax.dot_general(a, b, (((1,), (1,)), ((), ())), preferred_element_type=F32)


def dot_tn(a, b):
    return lax.dot_general(a, b, (((0,), (0,)), ((), ())), preferred_element_type=F32)


def call(body, name, out_shape, in_specs, scratch, flops, nbytes, out_specs=None, limit=VLIMIT):
    if out_specs is None:
        out_specs = jax.tree.map(lambda _: VMEM, out_shape)
    return pl.pallas_call(
        body,
        out_shape=out_shape,
        in_specs=in_specs,
        out_specs=out_specs,
        scratch_shapes=scratch,
        compiler_params=pltpu.CompilerParams(vmem_limit_bytes=limit),
        cost_estimate=pl.CostEstimate(flops=flops, bytes_accessed=nbytes, transcendentals=0),
        name=name,
    )


def begin(src, dst, sem):
    copy = pltpu.make_async_copy(src, dst, sem)
    copy.start()
    return copy


def begin_weights(win, wout, win_v, wout_v, sem):
    made = []
    for i in range(6):
        cols = pl.ds(512 * i, 512)
        made.append(begin(win.at[:, cols], win_v.at[:, cols], sem.at[i]))
    made.append(begin(wout, wout_v, sem.at[6]))
    return made


def shape(*dims, dtype=BF):
    return jax.ShapeDtypeStruct(dims, dtype)


def load_block(x_ref, dst):
    dst[...] = x_ref[...].astype(F32).reshape(TOK, D)


def store_block(src, out_ref):
    out_ref[...] = src[...].astype(BF).reshape(TOK // 2, 2, D)


def insert(piece_refs, pick_ref):
    total = dot(pick_ref[0], piece_refs[0][...])
    for q in range(1, 4):
        total = total + dot(pick_ref[q], piece_refs[q][...])
    return total


def extract(first, second, pick_ref, out_refs):
    for q in range(4):
        out_refs[q][...] = jnp.concatenate([dot(pick_ref[q], first), dot(pick_ref[q], second)], axis=0).astype(BF)


def build_bias(kind, table_ref, oht_ref, rdiff, cdiff, out, tab, tops, mids, lows, tall, edge):
    tab[...] = jnp.zeros_like(tab)
    tab[:, :OFFSETS] = table_ref[...]
    for dl in range(3):
        for rq in range(6):
            for cq in range(12):
                start = LEVEL_STEP * dl + ROW_STEP * rq + cq
                at = ((dl * 6 + rq) * 12 + cq) * 16
                x = tab[:, start : start + 128]
                top = x.astype(BF)
                rest = x - top.astype(F32)
                mid = rest.astype(BF)
                tops[at : at + 16, :] = top
                mids[at : at + 16, :] = mid
                lows[at : at + 16, :] = (rest - mid.astype(F32)).astype(BF)
    for lq in range(2):
        for rq in range(6):
            one = ((1 + lq) * 6 + rq) * 192
            two = (lq * 6 + rq) * 192
            got = None
            for piece in (tops, mids, lows):
                x = jnp.concatenate([piece[one : one + 192, :], piece[two : two + 192, :]], axis=1)
                part = dot(x, oht_ref[...])
                got = part if got is None else got + part
            for cq in range(12):
                rows = pl.ds((rq * 12 + cq) * 2 + lq, 16, stride=WT)
                tall[rows, :] = got[cq * 16 : cq * 16 + 16, :128]
                edge[rows, :] = got[cq * 16 : cq * 16 + 16, 128:]
    split_rows = (kind[0] % 2).astype(F32)
    split_cols = (kind[0] // 2).astype(F32)
    closed = rdiff[...] * split_rows + cdiff[...] * split_cols > 0.0
    for h in range(HEADS):
        rows = slice(h * WT, h * WT + WT)
        out[rows, :128] = jnp.where(closed[:, :128], MASKED, tall[rows, :])
        out[rows, 128:] = jnp.where(closed[:, 128:], MASKED, edge[rows, : WT - 128])


def head_masks(scale):
    lane = lax.broadcasted_iota(jnp.int32, (1, 128), 1)
    low = jnp.where(lane < 64, scale, 0.0).astype(BF)
    high = jnp.where(lane >= 64, scale, 0.0).astype(BF)
    return low, high


def stacked(block, masks):
    return jnp.concatenate([block * masks[0], block * masks[1]], axis=0)


def norm_rows(xs, n_ref, at, count):
    x = xs[at : at + count, :]
    mean = jnp.mean(x, axis=-1, keepdims=True)
    centered = x - mean
    var = jnp.mean(centered * centered, axis=-1, keepdims=True)
    n_ref[at : at + count, :] = (centered * lax.rsqrt(var + NORM_EPS)).astype(BF)


def pair_lanes(p, base):
    return pl.ds(pl.multiple_of(base + p * 128, 128), 128)


def pair_rows(p):
    return pl.ds(pl.multiple_of(p * TOK, 8), TOK)


def forward_core(xs, win, wout, bias_ref, n_ref, c_ref, proj_ref, e_ref, inv_ref, out, weights, bias_ready, made, made_pair):
    for at in range(0, TOK, 48):
        norm_rows(xs, n_ref, at, 48)
    made("n")
    for i in range(6):
        weights[i].wait()
        cols = slice(512 * i, 512 * i + 512)
        proj_ref[:, cols] = dot(n_ref[...], win[:, cols]).astype(BF)
    made("proj")
    bias_ready()

    @pl.loop(0, PAIRS, unroll=8)
    def _(p):
        eighth = head_masks(0.125)
        ones = head_masks(1.0)
        for w in range(MICRO):
            rows = slice(w * WT, w * WT + WT)
            qs = stacked(proj_ref[rows, pair_lanes(p, 0)], eighth)
            k = proj_ref[rows, pair_lanes(p, D)]
            v = proj_ref[rows, pair_lanes(p, 2 * D)]
            s = dot_nt(qs, k) + bias_ref[pair_rows(p), :]
            peak = jnp.max(s, axis=-1, keepdims=True)
            e = jnp.exp(s - peak).astype(BF)
            e_ref[pl.ds(pl.multiple_of((p * 2 + w) * TOK, 16), TOK), :] = e
            wide = [
                jnp.concatenate([v * one, jnp.broadcast_to(one, (WT, 128))], axis=1) for one in ones
            ]
            both = dot(e[:WT], wide[0]) + dot(e[WT:], wide[1])
            inv = 1.0 / both[:, 128:]
            c_ref[rows, pair_lanes(p, 0)] = (both[:, :128] * inv).astype(BF)
            inv_ref[pl.ds(pl.multiple_of((p * 2 + w) * WT, 16), WT), :] = inv.astype(BF)
        made_pair(p)

    made("c")
    weights[6].wait()
    for c in range(0, D, 512):
        out[:, c : c + 512] = xs[:, c : c + 512] + dot(c_ref[...], wout[:, c : c + 512])


def ring_depth():
    lat = lax.axis_index("lat")
    return jnp.where(lax.axis_index("section") == 0, lax.rem(lat, GROUP), lax.div(lat, 2 * GROUP))


def fold_bias(bacc, edge, oh_ref, terms, late_ref, late_sem):
    acc = [jnp.zeros((BIAS_ROWS, 256), F32) for _ in range(3)]
    blank = jnp.zeros((BIAS_ROWS, 128), F32)
    for rq in range(6):
        got = []
        for lq in range(2):
            taken = [pl.ds((rq * 12 + cq) * 2 + lq, 16, stride=WT) for cq in range(12)]
            x = jnp.concatenate(
                [jnp.concatenate([ref[rows, :] for rows in taken], axis=0) for ref in (bacc, edge)], axis=1
            )
            top = x.astype(BF)
            low = (x - top.astype(F32)).astype(BF)
            got.append(dot(top, oh_ref[...]) + dot(low, oh_ref[...]))
        levels = [got[0][:, 128:], got[0][:, :128] + got[1][:, 128:], got[1][:, :128]]
        for dl in range(3):
            for cq in range(12):
                one = jnp.concatenate([levels[dl][cq * 16 : cq * 16 + 16], blank], axis=1)
                shift = ROW_STEP * rq + cq
                acc[dl] = acc[dl] + (pltpu.roll(one, shift, 1) if shift else one)
    folded = jnp.zeros((BIAS_ROWS, OPAD), F32)
    for dl in range(3):
        one = jnp.concatenate([acc[dl], jnp.zeros((BIAS_ROWS, OPAD - 256), F32)], axis=1)
        folded = folded + (pltpu.roll(one, LEVEL_STEP * dl, 1) if dl else one)
    terms[:, :OPAD] = folded.astype(BF)
    terms[:, OPAD:] = jnp.zeros((BIAS_ROWS, D - OPAD), BF)
    return [begin(terms, late_ref[step].at[pl.ds(TOK, BIAS_ROWS), :], late_sem.at[step, 2]) for step in range(GROUP)]


def backward_attention(go, wout, c_ref, proj_ref, e_ref, inv_ref, gctx, gp, bacc, edge,
                       ready, ready_pair, late_ref, late_sem):
    sent = []
    depth = ring_depth()
    part = [lax.rem(depth + step, GROUP) for step in range(GROUP)]
    for step in range(GROUP):
        cols = pl.ds(pl.multiple_of(256 * part[step], 128), 256)
        sent.append(begin(go.at[:, cols], late_ref[step].at[pl.ds(0, TOK), pl.ds(768, 256)], late_sem.at[step, 0]))
    ready(0)
    for c in range(0, D, 256):
        gctx[:, c : c + 256] = dot_nt(go[...], wout[c : c + 256, :]).astype(BF)
    edge[...] = jnp.zeros_like(edge)
    ready(1)

    @pl.loop(0, PAIRS, unroll=4)
    def _(p):
        ready_pair(p)
        eighth = head_masks(0.125)
        ones = head_masks(1.0)
        full = jnp.ones((WT, 128), BF)
        total = None
        for w in range(MICRO):
            rows = slice(w * WT, w * WT + WT)
            qs = stacked(proj_ref[rows, pair_lanes(p, 0)], eighth)
            k = proj_ref[rows, pair_lanes(p, D)]
            v = proj_ref[rows, pair_lanes(p, 2 * D)]
            e = e_ref[pl.ds(pl.multiple_of((p * 2 + w) * TOK, 16), TOK), :]
            inv = inv_ref[pl.ds(pl.multiple_of((p * 2 + w) * WT, 16), WT), :]
            dc = (gctx[rows, pair_lanes(p, 0)].astype(F32) * inv.astype(F32)).astype(BF)
            dcs = stacked(dc, ones)
            along = -(dc.astype(F32) * c_ref[rows, pair_lanes(p, 0)].astype(F32))
            alongs = stacked(along.astype(BF), ones)
            slope = dot_nt(jnp.concatenate([dcs, alongs], axis=1), jnp.concatenate([v, full], axis=1))
            ds = e.astype(F32) * slope
            total = ds if total is None else total + ds
            dsb = ds.astype(BF)
            gp[rows, pair_lanes(p, 2 * D)] = dot_tn(e, dcs).astype(BF)
            gp[rows, pair_lanes(p, D)] = dot_tn(dsb, qs).astype(BF)
            ks = [k * one for one in eighth]
            gp[rows, pair_lanes(p, 0)] = (dot(dsb[:WT], ks[0]) + dot(dsb[WT:], ks[1])).astype(BF)
        bacc[pair_rows(p), :] = total[:, :128]
        edge[pair_rows(p), : WT - 128] = total[:, 128:]

    for step in range(GROUP):
        cols = pl.ds(pl.multiple_of(768 * part[step], 128), 768)
        sent.append(begin(gp.at[:, cols], late_ref[step].at[pl.ds(0, TOK), pl.ds(0, 768)], late_sem.at[step, 1]))

    return sent


def backward_input(xs, go, win, gp, out):
    for c in range(0, D, 256):
        out[:, c : c + 256] = dot_nt(gp[...], win[c : c + 256, :]).astype(BF).astype(F32)
    for at in range(0, TOK, 48):
        rows = slice(at, at + 48)
        dn = out[rows, :]
        x = xs[rows, :]
        mean = jnp.mean(x, axis=-1, keepdims=True)
        centered = x - mean
        var = jnp.mean(centered * centered, axis=-1, keepdims=True)
        scale = lax.rsqrt(var + NORM_EPS)
        n = centered * scale
        along = jnp.mean(dn * n, axis=-1, keepdims=True)
        level = jnp.mean(dn, axis=-1, keepdims=True)
        dx = (scale * (dn - level - n * along)).astype(BF).astype(F32)
        out[rows, :] = go[rows, :].astype(F32) + dx


def first_forward_body(kind, x_ref, table_ref, oht_ref, rdiff, cdiff, win, wout,
                       bias_out, n_out, c_out, proj_out, e_out, inv_out, first_out,
                       win_v, wout_v, bias_v, n, c, proj, e, inv, xs, out, tab, tops, mids, lows, tall, edge, wsem, osem, esem):
    @pl.when(lax.axis_index("section") == 0)
    def _():
        begin_weights(win, wout, win_v, wout_v, wsem)

    build_bias(kind, table_ref, oht_ref, rdiff, cdiff, bias_v, tab, tops, mids, lows, tall, edge)
    bias_copy = begin(bias_v, bias_out, osem.at[4])

    @pl.when(lax.axis_index("section") == 0)
    def _():
        weights = [
            pltpu.make_async_copy(win.at[:, pl.ds(512 * i, 512)], win_v.at[:, pl.ds(512 * i, 512)], wsem.at[i])
            for i in range(6)
        ] + [pltpu.make_async_copy(wout, wout_v, wsem.at[6])]
        load_block(x_ref, xs)
        sent = []

        def made(name):
            if name == "n":
                sent.append(begin(n, n_out, osem.at[0]))
            if name == "proj":
                sent.append(begin(proj, proj_out, osem.at[1]))
            if name == "c":
                sent.append(begin(c, c_out, osem.at[2]))

        def pair_copies(p):
            e_rows = pl.ds(pl.multiple_of(p * 2 * TOK, 16), 2 * TOK)
            inv_rows = pl.ds(pl.multiple_of(p * 2 * WT, 16), 2 * WT)
            return [
                pltpu.make_async_copy(e.at[e_rows], e_out.at[e_rows], esem.at[p, 0]),
                pltpu.make_async_copy(inv.at[inv_rows], inv_out.at[inv_rows], esem.at[p, 1]),
            ]

        def made_pair(p):
            for one in pair_copies(p):
                one.start()

        forward_core(xs, win_v, wout_v, bias_v, n, c, proj, e, inv, out, weights, lambda: None, made, made_pair)
        first_out[...] = out[...].astype(BF)
        for p in range(PAIRS):
            sent += pair_copies(p)
        for one in sent:
            one.wait()

    bias_copy.wait()


def pack_body(first_ref, cot_ref, pick_ref, p0, p1, p2, p3, xs):
    @pl.when(lax.axis_index("section") == 0)
    def _():
        load_block(cot_ref, xs)
        extract(first_ref[...], xs[...].astype(BF), pick_ref, (p0, p1, p2, p3))


def second_body(r0, r1, r2, r3, upper_ref, pick_hbm, lower_hbm, na_ref, ca_ref, bias_ref, win, wout,
                nc_out, l0, l1, l2, l3, bacc_out, edge_out, g0, g1, g2, g3,
                win_v, wout_v, c, proj, e, inv, xs, out, go, gctx, gp, bacc, edge, terms,
                wsem, isem, lsem, n, bias_v, second, psem, pick_ref, lower_ref):
    @pl.when(lax.axis_index("section") == 1)
    def _():
        weights = begin_weights(win, wout, win_v, wout_v, wsem)
        bias_copy = begin(bias_ref, bias_v, isem.at[0])
        maps = [begin(pick_hbm, pick_ref, isem.at[1]), begin(lower_hbm, lower_ref, isem.at[2])]
        xs[...] = insert((r0, r1, r2, r3), upper_ref)
        sent = []

        def made(name):
            if name == "n":
                sent.extend(begin(n, nc_out.at[j, :, pl.ds(0, D)], psem.at[j, 0]) for j in range(GROUP))
            if name == "c":
                sent.extend(begin(c, nc_out.at[j, :, pl.ds(D, D)], psem.at[j, 1]) for j in range(GROUP))

        forward_core(xs, win_v, wout_v, bias_v, n, c, proj, e, inv, out, weights, bias_copy.wait, made, lambda p: None)
        second[...] = out[...].astype(BF)
        for one in maps:
            one.wait()
        go[...] = insert((r0, r1, r2, r3), lower_ref).astype(BF)
        sent += backward_attention(go, wout_v, c, proj, e, inv, gctx, gp, bacc, edge,
                                   lambda stage: None, lambda p: None, (l0, l1, l2, l3), lsem)
        sent += [begin(bacc, bacc_out, lsem.at[0, 2]), begin(edge, edge_out, lsem.at[1, 2])]
        backward_input(xs, go, win_v, gp, out)
        extract(out[...].astype(BF), second[...], pick_ref, (g0, g1, g2, g3))
        for one in sent:
            one.wait()

    @pl.when(lax.axis_index("section") == 0)
    def _():
        came = [begin(na_ref, n, isem.at[0]), begin(ca_ref, c, isem.at[1])]
        came[0].wait()
        gone = [begin(n, nc_out.at[j, :, pl.ds(0, D)], psem.at[j, 0]) for j in range(GROUP)]
        came[1].wait()
        gone += [begin(c, nc_out.at[j, :, pl.ds(D, D)], psem.at[j, 1]) for j in range(GROUP)]
        for one in gone:
            one.wait()


def first_backward_body(g0, g1, g2, g3, upper_ref, oh_ref, c_ref, proj_ref, e_ref, inv_ref, wout, b0, b1, b2, b3, bacc_b, edge_b,
                        l0, l1, l2, l3, go_out, gp_out,
                        wout_v, c, proj, e, inv, go, gctx, gp, bacc, edge, terms, grads, upper, oh, hold,
                        isem, esem, lsem):
    @pl.when(lax.axis_index("section") == 0)
    def _():
        first = [begin(src, grads.at[q], isem.at[q]) for q, src in enumerate((g0, g1, g2, g3))]
        first.append(begin(upper_ref, upper, isem.at[4]))
        outer = begin(wout, wout_v, isem.at[5])
        rest = [begin(proj_ref, proj, isem.at[6]), begin(c_ref, c, isem.at[7]), begin(inv_ref, inv, isem.at[8])]

        def pair_copy(p):
            rows = pl.ds(pl.multiple_of(p * 2 * TOK, 16), 2 * TOK)
            return pltpu.make_async_copy(e_ref.at[rows], e.at[rows], esem.at[p])

        for p in range(PAIRS):
            pair_copy(p).start()
        last = begin(oh_ref, oh, isem.at[9])
        for one in first:
            one.wait()
        go[...] = insert([grads.at[q] for q in range(4)], upper).astype(BF)
        go_copy = begin(go, go_out, isem.at[10])

        def ready(stage):
            for one in [outer] if stage == 0 else rest:
                one.wait()

        sent = backward_attention(go, wout_v, c, proj, e, inv, gctx, gp, bacc, edge,
                                  ready, lambda p: pair_copy(p).wait(), (l0, l1, l2, l3), lsem)
        sent += [go_copy, begin(gp, gp_out, isem.at[11])]
        last.wait()
        sent += fold_bias(bacc, edge, oh, terms, (l0, l1, l2, l3), lsem)
        for one in sent:
            one.wait()

    @pl.when(lax.axis_index("section") == 1)
    def _():
        body = pl.ds(0, TOK)
        came = [begin(src.at[body], hold.at[j], lsem.at[j, 0]) for j, src in enumerate((b0, b1, b2, b3))]
        sums = [begin(bacc_b, bacc, isem.at[0]), begin(edge_b, edge, isem.at[1]), begin(oh_ref, oh, isem.at[2])]
        gone = []
        for j, dst in enumerate((l0, l1, l2, l3)):
            came[j].wait()
            gone.append(begin(hold.at[j], dst.at[body], lsem.at[j, 1]))
        for one in sums:
            one.wait()
        for one in gone + fold_bias(bacc, edge, oh, terms, (l0, l1, l2, l3), lsem):
            one.wait()


def input_grad_body(x_ref, go, gp, win, out_ref, xs, out):
    @pl.when(lax.axis_index("section") == 0)
    def _():
        load_block(x_ref, xs)
        backward_input(xs, go, win, gp, out)
        store_block(out, out_ref)


def second_result_body(g0, g1, g2, g3, lower_ref, out_ref, xs):
    @pl.when(lax.axis_index("section") == 0)
    def _():
        xs[...] = insert((g0, g1, g2, g3), lower_ref)
        store_block(xs, out_ref)


def flip_body(in_ref, out_ref, held, sem):
    source = [lax.rem(ring_depth() + GROUP - step, GROUP) for step in range(GROUP)]
    copies = [begin(in_ref.at[source[j]], held.at[pl.ds(TOK * j, TOK)], sem.at[j]) for j in range(GROUP)]
    for one in copies:
        one.wait()

    @pl.loop(0, 8)
    def _(i):
        at = pl.ds(pl.multiple_of(i * 256, 256), 256)
        out_ref[at, :] = held[:, at].T


def weight_body(nct, l0, l1, l2, l3, out, grads, made, tab, sem):
    late = (l0, l1, l2, l3)
    table = late[0][TOK:, :OPAD].astype(F32)
    for j in range(GROUP):
        grads[TOK * j : TOK * j + TOK, :] = late[j][:TOK, :]
        if j:
            table = table + late[j][TOK:, :OPAD].astype(F32)
    tab[...] = table
    depth = ring_depth()
    share = jnp.concatenate(
        [
            tab[:, pl.ds(pl.multiple_of(128 * depth, 128), 128)],
            tab[pl.ds(pl.multiple_of(8 * lax.rem(depth, 2), 8), 8), pl.ds(pl.multiple_of(512 + 128 * lax.div(depth, 2), 128), 128)],
        ],
        axis=0,
    ).astype(BF)
    made[:, 128:, :] = jnp.broadcast_to(share[None], (64, 24, 128))
    sent = []
    for rb in range(4):
        dst = slice(rb * 16, rb * 16 + 16)
        into = dot(nct[rb * 256 : rb * 256 + 256, :], grads[:, :768])
        for cb in range(6):
            made[dst, cb * 16 : cb * 16 + 16, :] = into[:, cb * 128 : cb * 128 + 128].astype(BF).reshape(16, 16, 128)
        outof = dot(nct[D + rb * 256 : D + rb * 256 + 256, :], grads[:, 768:])
        for cb in range(2):
            made[dst, 96 + cb * 16 : 112 + cb * 16, :] = outof[:, cb * 128 : cb * 128 + 128].astype(BF).reshape(16, 16, 128)
        sent.append(begin(made.at[pl.ds(rb * 16, 16)], out.at[pl.ds(rb * 16, 16)], sem.at[rb]))
    for one in sent:
        one.wait()


def sum_body(in_ref, w_ref, b_ref, bias):
    def fill(place):
        for part in range(GROUP):
            total = None
            for i in range(4):
                for xh in range(2):
                    for xl in range(2):
                        y, z = place(part, i)
                        one = in_ref[((y * 2 + xh) * 4 + z) * 2 + xl].astype(F32)
                        total = one if total is None else total + one
            for cb in range(6):
                w_ref[:, part * 768 + cb * 128 : part * 768 + cb * 128 + 128] = total[cb * 16 : cb * 16 + 16]
            for cb in range(2):
                at = 3 * D + part * 256 + cb * 128
                w_ref[:, at : at + 128] = total[96 + cb * 16 : 112 + cb * 16]
            bias[:, part * 128 : part * 128 + 128] = total[128:144]
            at = 8 * (part % 2)
            bias[at : at + 8, 512 + 128 * (part // 2) : 640 + 128 * (part // 2)] = total[144:152]
        b_ref[...] = bias[:, :OFFSETS]

    @pl.when(lax.axis_index("section") == 0)
    def _():
        fill(lambda part, i: (i, part))

    @pl.when(lax.axis_index("section") == 1)
    def _():
        fill(lambda part, i: (part, i))


def per_device(boundary, tile_kinds, proj_in, proj_out, offset_bias):
    axes = ("lat", "lon", "section")
    nlat, nlon = lax.axis_size("lat"), lax.axis_size("lon")
    section = lax.axis_index("section")
    kind = tile_kinds.reshape(1)
    x = boundary.transpose(0, 1, 3, 4, 2, 5).reshape(TOK // 2, 2, D)
    win = proj_in[0]
    wout = proj_out[0]
    onehot = jnp.asarray(ONEHOT, BF)
    onehot_t = jnp.asarray(ONEHOT.T, BF)
    pick = jnp.asarray(PICK, BF)
    upper = jnp.asarray(UPPER, BF)
    lower = jnp.asarray(LOWER, BF)

    def flat(lat, lon, sec):
        return ((lat % nlat) * nlon + lon % nlon) * 2 + sec

    def roll_pairs(dl, dn, sec):
        return [(flat(i, j, sec), flat(i + dl, j + dn, 1 - sec)) for i in range(nlat) for j in range(nlon)]

    def cross(value, sec):
        return lax.ppermute(value, axes, roll_pairs(0, 0, sec))

    far_first = [(1, 1), (1, 0), (0, 1), (0, 0)]

    def forth(pieces):
        got = [None] * 4
        for dl, dn in far_first:
            piece = pieces[(1 - dl) * 2 + (1 - dn)]
            got[dl * 2 + dn] = lax.ppermute(piece, axes, roll_pairs(-dl, -dn, 0))
        return got

    def back(pieces):
        got = [None] * 4
        for dl, dn in far_first:
            got[(1 - dl) * 2 + (1 - dn)] = lax.ppermute(pieces[dl * 2 + dn], axes, roll_pairs(dl, dn, 1))
        return got

    def rings(axis, sec):
        made = {}
        for y in range(4):
            for x in range(4):
                for z in range(4):
                    key = {"x": (y, z), "y": (x, z), "z": (x, y)}[axis]
                    made.setdefault(key, []).append(flat((y * 2 + x // 2) * 4 + z, x % 2, sec))
        return [made[key] for key in sorted(made)]

    def deal(values, groups):
        return [values[0]] + [
            lax.ppermute(values[step], axes, [(g[m], g[(m + step) % GROUP]) for g in groups for m in range(GROUP)])
            for step in range(1, GROUP)
        ]

    quarter = [shape(2 * QT, D)] * 4
    block = shape(TOK // 2, 2, D)
    f32 = functools.partial(shape, dtype=F32)
    vf32 = lambda *dims: pltpu.VMEM(dims, F32)
    vbf = lambda *dims: pltpu.VMEM(dims, BF)
    dma = lambda *dims: pltpu.SemaphoreType.DMA(dims)
    wide = shape(TOK, 3 * D)
    whole = shape(TOK, D)
    exps = shape(PAIRS * MICRO * TOK, WT)
    invs = shape(PAIRS * MICRO * WT, 128)
    late_shape = [shape(TOK + BIAS_ROWS, D)] * GROUP
    weights_v = [vbf(D, 3 * D), vbf(D, D)]
    soft_v = [vbf(PAIRS * MICRO * TOK, WT), vbf(PAIRS * MICRO * WT, 128)]
    tall = [vf32(HEADS * WT, 128), vf32(HEADS * WT, 128)]
    pieces_v = [vbf(3 * 1152, 128)] * 3
    front_v = [vf32(HEADS * WT, WT), vbf(TOK, D), vbf(TOK, D), vbf(TOK, 3 * D)] + soft_v + [vf32(TOK, D), vf32(TOK, D)]
    back_v = (
        weights_v
        + [vbf(TOK, D), vbf(TOK, 3 * D)] + soft_v + [vf32(TOK, D), vf32(TOK, D)]
        + [vbf(TOK, D), vbf(TOK, D), vbf(TOK, 3 * D)]
        + tall
        + [vbf(BIAS_ROWS, D), dma(7), dma(4), dma(GROUP, 3)]
    )

    cot = cross(x, 1)
    bias, n_a, c_a, proj_a, e_a, inv_a, first_out = call(
        first_forward_body, "first_forward", [f32(HEADS * WT, WT), whole, whole, wide, exps, invs, whole],
        [SMEM] + [VMEM] * 5 + [HBM] * 2,
        weights_v + front_v + [vf32(HEADS, OPAD)] + pieces_v + tall + [dma(7), dma(6), dma(PAIRS, 2)],
        5_000_000_000, 20_000_000, [HBM] * 6 + [VMEM],
    )(kind, x, offset_bias[0], onehot_t, jnp.asarray(ROWS_DIFFER), jnp.asarray(COLS_DIFFER), win, wout)
    pieces = call(
        pack_body, "pack", quarter, [VMEM] * 3, [vf32(TOK, D)], 340_000_000, 3_000_000, limit=SMALL,
    )(first_out, cot, pick)
    received = forth(pieces)
    both, *pieces = call(
        second_body, "second_both", [shape(GROUP, TOK, 2 * D)] + late_shape + [f32(HEADS * WT, 128)] * 2 + quarter,
        [VMEM] * 5 + [HBM] * 7,
        back_v + [vbf(TOK, D), vf32(HEADS * WT, WT), vbf(TOK, D), dma(GROUP, 2), vbf(4, QT, TOK), vbf(4, TOK, 2 * QT)],
        12_000_000_000, 20_000_000, [HBM] * 7 + [VMEM] * 4,
    )(*received, upper, pick, lower, n_a, c_a, bias, win, wout)
    late_b, sums_b, grads = pieces[:4], pieces[4:6], pieces[6:]
    grads = back(grads)
    both = lax.all_to_all(both, axes, 0, 0, axis_index_groups=rings("z", 0) + rings("y", 1), tiled=True)

    *late, go_a, gp_a = call(
        first_backward_body, "first_backward", late_shape + [whole, wide],
        [HBM] * 17,
        [vbf(D, D), vbf(TOK, D), vbf(TOK, 3 * D)] + soft_v + [vbf(TOK, D), vbf(TOK, D), vbf(TOK, 3 * D)] + tall
        + [vbf(BIAS_ROWS, D), vbf(4, 2 * QT, D), vbf(4, TOK, 2 * QT), vbf(256, 256)]
        + [vbf(GROUP, TOK, D), dma(12), dma(PAIRS), dma(GROUP, 3)],
        30_000_000_000, 20_000_000, [HBM] * 6,
    )(*grads, upper, onehot, c_a, proj_a, e_a, inv_a, wout, *late_b, *sums_b)
    late, go_a, gp_a, grads = lax.optimization_barrier((late, go_a, gp_a, grads))
    late = deal(late, rings("z", 0) + rings("y", 1))

    grad_in = call(
        input_grad_body, "input_grad", block, [VMEM] * 4, [vf32(TOK, D), vf32(TOK, D)], 2_000_000_000, 10_000_000,
    )(x, go_a, gp_a, win)
    flipped = call(
        flip_body, "flip", shape(2 * D, GROUP * TOK), [HBM],
        [vbf(GROUP * TOK, 2 * D), dma(GROUP)], 10_000_000, 10_000_000, limit=SMALL,
    )(both)
    second_out = call(
        second_result_body, "second_result", block, [VMEM] * 5, [vf32(TOK, D)], 170_000_000, 2_000_000, limit=SMALL,
    )(*grads, lower)

    terms = call(
        weight_body, "weight_terms", shape(64, 152, 128), [VMEM] * 5,
        [vbf(GROUP * TOK, D), vbf(64, 152, 128), vf32(HEADS, OPAD), dma(4)], 2_400_000_000, 10_000_000, HBM, limit=SMALL,
    )(flipped, *late)
    terms, second_out = lax.optimization_barrier((terms, cross(second_out, 0)))
    terms = lax.all_to_all(terms, ("lat", "lon"), 0, 0, tiled=True)
    result = jnp.where(section == 0, grad_in, second_out)
    result = result.reshape(1, MICRO, 6, 12, 2, D).transpose(0, 1, 4, 2, 3, 5)
    weights, table = call(
        sum_body, "sum_terms", [f32(16, 4 * D), f32(HEADS, OFFSETS)], [VMEM], [vf32(HEADS, OPAD)], 3_000_000, 3_000_000, limit=SMALL,
    )(terms)
    return (result, weights[None], table[None])


def solution(mesh):
    return jax.shard_map(
        per_device,
        mesh=mesh,
        in_specs=(
            P("section", None, None, "lat", "lon", None),
            P("section", "lat", "lon"),
            P("section", None, None),
            P("section", None, None),
            P("section", None, None),
        ),
        out_specs=(
            P("section", None, None, "lat", "lon", None),
            P("section", ("lat", "lon"), None),
            P("section", None, None),
        ),
        check_vma=False,
    )
```

```python
import functools

import jax
import jax.numpy as jnp
import numpy as np
from jax import lax
from jax.experimental import pallas as pl
from jax.experimental.pallas import tpu as pltpu
from jax.sharding import PartitionSpec as P

D = 1024
HEADS = 16
LEV = 2
MICRO = 2
WIN_LAT = 6
WIN_LON = 12
WT = 144
TOK = MICRO * WT
QT = TOK // 4
OFFSETS = 759
OPAD = 768
LEVEL_STEP = 253
ROW_STEP = 23
PAIRS = HEADS // 2
GROUP = 4
BIAS_ROWS = 16
NORM_EPS = 1e-05
MASKED = -1e30
BF = jnp.bfloat16
F32 = jnp.float32
VLIMIT = 58 * 1024 * 1024
SMALL = 24 * 1024 * 1024

HBM = pl.BlockSpec(memory_space=pltpu.HBM)
VMEM = pl.BlockSpec(memory_space=pltpu.VMEM)
SMEM = pl.BlockSpec(memory_space=pltpu.SMEM)


def constants():
    tok = np.arange(WT)
    row, col, lev = tok // 24, tok // 2 % 12, tok % 2
    onehot = np.zeros((256, 256), np.float32)
    onehot[tok, 128 * lev + 126 - 23 * row - col] = 1
    rows_differ = ((row < 3)[:, None] != (row < 3)[None, :]).astype(np.float32)
    cols_differ = ((col < 6)[:, None] != (col < 6)[None, :]).astype(np.float32)
    pick = np.zeros((4, QT, TOK), np.float32)
    for half_row in range(2):
        for half_col in range(2):
            at = 0
            for micro in range(MICRO):
                for level in range(LEV):
                    for r in range(3):
                        for c in range(6):
                            src = micro * WT + ((3 * half_row + r) * 12 + 6 * half_col + c) * 2 + level
                            pick[half_row * 2 + half_col, at, src] = 1
                            at += 1
    upper = np.concatenate([pick, np.zeros_like(pick)], axis=1).transpose(0, 2, 1)
    lower = np.concatenate([np.zeros_like(pick), pick], axis=1).transpose(0, 2, 1)
    return onehot, rows_differ, cols_differ, pick, upper, lower


ONEHOT, ROWS_DIFFER, COLS_DIFFER, PICK, UPPER, LOWER = constants()


def dot(a, b):
    return jnp.dot(a, b, preferred_element_type=F32)


def dot_nt(a, b):
    return lax.dot_general(a, b, (((1,), (1,)), ((), ())), preferred_element_type=F32)


def dot_tn(a, b):
    return lax.dot_general(a, b, (((0,), (0,)), ((), ())), preferred_element_type=F32)


def call(body, name, out_shape, in_specs, scratch, flops, nbytes, out_specs=None, limit=VLIMIT):
    if out_specs is None:
        out_specs = jax.tree.map(lambda _: VMEM, out_shape)
    return pl.pallas_call(
        body,
        out_shape=out_shape,
        in_specs=in_specs,
        out_specs=out_specs,
        scratch_shapes=scratch,
        compiler_params=pltpu.CompilerParams(vmem_limit_bytes=limit),
        cost_estimate=pl.CostEstimate(flops=flops, bytes_accessed=nbytes, transcendentals=0),
        name=name,
    )


def begin(src, dst, sem):
    copy = pltpu.make_async_copy(src, dst, sem)
    copy.start()
    return copy


def begin_weights(win, wout, win_v, wout_v, sem):
    made = []
    for i in range(6):
        cols = pl.ds(512 * i, 512)
        made.append(begin(win.at[:, cols], win_v.at[:, cols], sem.at[i]))
    made.append(begin(wout, wout_v, sem.at[6]))
    return made


def shape(*dims, dtype=BF):
    return jax.ShapeDtypeStruct(dims, dtype)


def load_block(x_ref, dst):
    dst[...] = x_ref[...].astype(F32).reshape(TOK, D)


def store_block(src, out_ref):
    out_ref[...] = src[...].astype(BF).reshape(TOK // 2, 2, D)


def insert(piece_refs, pick_ref):
    total = dot(pick_ref[0], piece_refs[0][...])
    for q in range(1, 4):
        total = total + dot(pick_ref[q], piece_refs[q][...])
    return total


def extract(first, second, pick_ref, out_refs):
    for q in range(4):
        out_refs[q][...] = jnp.concatenate([dot(pick_ref[q], first), dot(pick_ref[q], second)], axis=0).astype(BF)


def build_bias(kind, table_ref, oht_ref, rdiff, cdiff, out, tab, tops, mids, lows, tall, edge):
    tab[...] = jnp.zeros_like(tab)
    tab[:, :OFFSETS] = table_ref[...]
    for dl in range(3):
        for rq in range(6):
            for cq in range(12):
                start = LEVEL_STEP * dl + ROW_STEP * rq + cq
                at = ((dl * 6 + rq) * 12 + cq) * 16
                x = tab[:, start : start + 128]
                top = x.astype(BF)
                rest = x - top.astype(F32)
                mid = rest.astype(BF)
                tops[at : at + 16, :] = top
                mids[at : at + 16, :] = mid
                lows[at : at + 16, :] = (rest - mid.astype(F32)).astype(BF)
    for lq in range(2):
        for rq in range(6):
            one = ((1 + lq) * 6 + rq) * 192
            two = (lq * 6 + rq) * 192
            got = None
            for piece in (tops, mids, lows):
                x = jnp.concatenate([piece[one : one + 192, :], piece[two : two + 192, :]], axis=1)
                part = dot(x, oht_ref[...])
                got = part if got is None else got + part
            for cq in range(12):
                rows = pl.ds((rq * 12 + cq) * 2 + lq, 16, stride=WT)
                tall[rows, :] = got[cq * 16 : cq * 16 + 16, :128]
                edge[rows, :] = got[cq * 16 : cq * 16 + 16, 128:]
    split_rows = (kind[0] % 2).astype(F32)
    split_cols = (kind[0] // 2).astype(F32)
    closed = rdiff[...] * split_rows + cdiff[...] * split_cols > 0.0
    for h in range(HEADS):
        rows = slice(h * WT, h * WT + WT)
        out[rows, :128] = jnp.where(closed[:, :128], MASKED, tall[rows, :])
        out[rows, 128:] = jnp.where(closed[:, 128:], MASKED, edge[rows, : WT - 128])


def head_masks(scale):
    lane = lax.broadcasted_iota(jnp.int32, (1, 128), 1)
    low = jnp.where(lane < 64, scale, 0.0).astype(BF)
    high = jnp.where(lane >= 64, scale, 0.0).astype(BF)
    return low, high


def stacked(block, masks):
    return jnp.concatenate([block * masks[0], block * masks[1]], axis=0)


def norm_rows(xs, n_ref, at, count):
    x = xs[at : at + count, :]
    mean = jnp.mean(x, axis=-1, keepdims=True)
    centered = x - mean
    var = jnp.mean(centered * centered, axis=-1, keepdims=True)
    n_ref[at : at + count, :] = (centered * lax.rsqrt(var + NORM_EPS)).astype(BF)


def pair_lanes(p, base):
    return pl.ds(pl.multiple_of(base + p * 128, 128), 128)


def pair_rows(p):
    return pl.ds(pl.multiple_of(p * TOK, 8), TOK)


def forward_core(xs, win, wout, bias_ref, n_ref, c_ref, proj_ref, e_ref, inv_ref, out, weights, bias_ready, made, made_pair):
    for at in range(0, TOK, 48):
        norm_rows(xs, n_ref, at, 48)
    made("n")
    for i in range(6):
        weights[i].wait()
        cols = slice(512 * i, 512 * i + 512)
        proj_ref[:, cols] = dot(n_ref[...], win[:, cols]).astype(BF)
    made("proj")
    bias_ready()

    @pl.loop(0, PAIRS, unroll=8)
    def _(p):
        eighth = head_masks(0.125)
        ones = head_masks(1.0)
        for w in range(MICRO):
            rows = slice(w * WT, w * WT + WT)
            qs = stacked(proj_ref[rows, pair_lanes(p, 0)], eighth)
            k = proj_ref[rows, pair_lanes(p, D)]
            v = proj_ref[rows, pair_lanes(p, 2 * D)]
            s = dot_nt(qs, k) + bias_ref[pair_rows(p), :]
            peak = jnp.max(s, axis=-1, keepdims=True)
            e = jnp.exp(s - peak).astype(BF)
            e_ref[pl.ds(pl.multiple_of((p * 2 + w) * TOK, 16), TOK), :] = e
            wide = [
                jnp.concatenate([v * one, jnp.broadcast_to(one, (WT, 128))], axis=1) for one in ones
            ]
            both = dot(e[:WT], wide[0]) + dot(e[WT:], wide[1])
            inv = 1.0 / both[:, 128:]
            c_ref[rows, pair_lanes(p, 0)] = (both[:, :128] * inv).astype(BF)
            inv_ref[pl.ds(pl.multiple_of((p * 2 + w) * WT, 16), WT), :] = inv.astype(BF)
        made_pair(p)

    made("c")
    weights[6].wait()
    for c in range(0, D, 512):
        out[:, c : c + 512] = xs[:, c : c + 512] + dot(c_ref[...], wout[:, c : c + 512])


def ring_depth():
    lat = lax.axis_index("lat")
    return jnp.where(lax.axis_index("section") == 0, lax.rem(lat, GROUP), lax.div(lat, 2 * GROUP))


def fold_bias(bacc, edge, oh_ref, terms, late_ref, late_sem):
    acc = [jnp.zeros((BIAS_ROWS, 256), F32) for _ in range(3)]
    blank = jnp.zeros((BIAS_ROWS, 128), F32)
    for rq in range(6):
        got = []
        for lq in range(2):
            taken = [pl.ds((rq * 12 + cq) * 2 + lq, 16, stride=WT) for cq in range(12)]
            x = jnp.concatenate(
                [jnp.concatenate([ref[rows, :] for rows in taken], axis=0) for ref in (bacc, edge)], axis=1
            )
            top = x.astype(BF)
            low = (x - top.astype(F32)).astype(BF)
            got.append(dot(top, oh_ref[...]) + dot(low, oh_ref[...]))
        levels = [got[0][:, 128:], got[0][:, :128] + got[1][:, 128:], got[1][:, :128]]
        for dl in range(3):
            for cq in range(12):
                one = jnp.concatenate([levels[dl][cq * 16 : cq * 16 + 16], blank], axis=1)
                shift = ROW_STEP * rq + cq
                acc[dl] = acc[dl] + (pltpu.roll(one, shift, 1) if shift else one)
    folded = jnp.zeros((BIAS_ROWS, OPAD), F32)
    for dl in range(3):
        one = jnp.concatenate([acc[dl], jnp.zeros((BIAS_ROWS, OPAD - 256), F32)], axis=1)
        folded = folded + (pltpu.roll(one, LEVEL_STEP * dl, 1) if dl else one)
    terms[:, :OPAD] = folded.astype(BF)
    terms[:, OPAD:] = jnp.zeros((BIAS_ROWS, D - OPAD), BF)
    return [begin(terms, late_ref[step].at[pl.ds(TOK, BIAS_ROWS), :], late_sem.at[step, 2]) for step in range(GROUP)]


def backward_attention(go, wout, c_ref, proj_ref, e_ref, inv_ref, gctx, gp, bacc, edge,
                       ready, ready_pair, late_ref, late_sem):
    sent = []
    depth = ring_depth()
    part = [lax.rem(depth + step, GROUP) for step in range(GROUP)]
    for step in range(GROUP):
        cols = pl.ds(pl.multiple_of(256 * part[step], 128), 256)
        sent.append(begin(go.at[:, cols], late_ref[step].at[pl.ds(0, TOK), pl.ds(768, 256)], late_sem.at[step, 0]))
    ready(0)
    for c in range(0, D, 256):
        gctx[:, c : c + 256] = dot_nt(go[...], wout[c : c + 256, :]).astype(BF)
    edge[...] = jnp.zeros_like(edge)
    ready(1)

    @pl.loop(0, PAIRS, unroll=8)
    def _(p):
        ready_pair(p)
        eighth = head_masks(0.125)
        ones = head_masks(1.0)
        full = jnp.ones((WT, 128), BF)
        total = None
        for w in range(MICRO):
            rows = slice(w * WT, w * WT + WT)
            qs = stacked(proj_ref[rows, pair_lanes(p, 0)], eighth)
            k = proj_ref[rows, pair_lanes(p, D)]
            v = proj_ref[rows, pair_lanes(p, 2 * D)]
            e = e_ref[pl.ds(pl.multiple_of((p * 2 + w) * TOK, 16), TOK), :]
            inv = inv_ref[pl.ds(pl.multiple_of((p * 2 + w) * WT, 16), WT), :]
            dc = (gctx[rows, pair_lanes(p, 0)].astype(F32) * inv.astype(F32)).astype(BF)
            dcs = stacked(dc, ones)
            along = -(dc.astype(F32) * c_ref[rows, pair_lanes(p, 0)].astype(F32))
            alongs = stacked(along.astype(BF), ones)
            slope = dot_nt(jnp.concatenate([dcs, alongs], axis=1), jnp.concatenate([v, full], axis=1))
            ds = e.astype(F32) * slope
            total = ds if total is None else total + ds
            dsb = ds.astype(BF)
            gp[rows, pair_lanes(p, 2 * D)] = dot_tn(e, dcs).astype(BF)
            gp[rows, pair_lanes(p, D)] = dot_tn(dsb, qs).astype(BF)
            ks = [k * one for one in eighth]
            gp[rows, pair_lanes(p, 0)] = (dot(dsb[:WT], ks[0]) + dot(dsb[WT:], ks[1])).astype(BF)
        bacc[pair_rows(p), :] = total[:, :128]
        edge[pair_rows(p), : WT - 128] = total[:, 128:]

    for step in range(GROUP):
        cols = pl.ds(pl.multiple_of(768 * part[step], 128), 768)
        sent.append(begin(gp.at[:, cols], late_ref[step].at[pl.ds(0, TOK), pl.ds(0, 768)], late_sem.at[step, 1]))

    return sent


def backward_input(xs, go, win, gp, out):
    for c in range(0, D, 256):
        out[:, c : c + 256] = dot_nt(gp[...], win[c : c + 256, :]).astype(BF).astype(F32)
    for at in range(0, TOK, 48):
        rows = slice(at, at + 48)
        dn = out[rows, :]
        x = xs[rows, :]
        mean = jnp.mean(x, axis=-1, keepdims=True)
        centered = x - mean
        var = jnp.mean(centered * centered, axis=-1, keepdims=True)
        scale = lax.rsqrt(var + NORM_EPS)
        n = centered * scale
        along = jnp.mean(dn * n, axis=-1, keepdims=True)
        level = jnp.mean(dn, axis=-1, keepdims=True)
        dx = (scale * (dn - level - n * along)).astype(BF).astype(F32)
        out[rows, :] = go[rows, :].astype(F32) + dx


def first_forward_body(kind, x_ref, table_ref, oht_ref, rdiff, cdiff, win, wout,
                       bias_out, n_out, c_out, proj_out, e_out, inv_out, first_out,
                       win_v, wout_v, bias_v, n, c, proj, e, inv, xs, out, tab, tops, mids, lows, tall, edge, wsem, osem, esem):
    @pl.when(lax.axis_index("section") == 0)
    def _():
        begin_weights(win, wout, win_v, wout_v, wsem)

    build_bias(kind, table_ref, oht_ref, rdiff, cdiff, bias_v, tab, tops, mids, lows, tall, edge)
    bias_copy = begin(bias_v, bias_out, osem.at[4])

    @pl.when(lax.axis_index("section") == 0)
    def _():
        weights = [
            pltpu.make_async_copy(win.at[:, pl.ds(512 * i, 512)], win_v.at[:, pl.ds(512 * i, 512)], wsem.at[i])
            for i in range(6)
        ] + [pltpu.make_async_copy(wout, wout_v, wsem.at[6])]
        load_block(x_ref, xs)
        sent = []

        def made(name):
            if name == "n":
                sent.append(begin(n, n_out, osem.at[0]))
            if name == "proj":
                sent.append(begin(proj, proj_out, osem.at[1]))
            if name == "c":
                sent.append(begin(c, c_out, osem.at[2]))

        def pair_copies(p):
            e_rows = pl.ds(pl.multiple_of(p * 2 * TOK, 16), 2 * TOK)
            inv_rows = pl.ds(pl.multiple_of(p * 2 * WT, 16), 2 * WT)
            return [
                pltpu.make_async_copy(e.at[e_rows], e_out.at[e_rows], esem.at[p, 0]),
                pltpu.make_async_copy(inv.at[inv_rows], inv_out.at[inv_rows], esem.at[p, 1]),
            ]

        def made_pair(p):
            for one in pair_copies(p):
                one.start()

        forward_core(xs, win_v, wout_v, bias_v, n, c, proj, e, inv, out, weights, lambda: None, made, made_pair)
        first_out[...] = out[...].astype(BF)
        for p in range(PAIRS):
            sent += pair_copies(p)
        for one in sent:
            one.wait()

    bias_copy.wait()


def pack_body(first_ref, cot_ref, pick_ref, p0, p1, p2, p3, xs):
    @pl.when(lax.axis_index("section") == 0)
    def _():
        load_block(cot_ref, xs)
        extract(first_ref[...], xs[...].astype(BF), pick_ref, (p0, p1, p2, p3))


def second_body(r0, r1, r2, r3, upper_ref, pick_hbm, lower_hbm, na_ref, ca_ref, bias_ref, win, wout,
                nc_out, l0, l1, l2, l3, bacc_out, edge_out, g0, g1, g2, g3,
                win_v, wout_v, c, proj, e, inv, xs, out, go, gctx, gp, bacc, edge, terms,
                wsem, isem, lsem, n, bias_v, second, psem, pick_ref, lower_ref):
    @pl.when(lax.axis_index("section") == 1)
    def _():
        weights = begin_weights(win, wout, win_v, wout_v, wsem)
        bias_copy = begin(bias_ref, bias_v, isem.at[0])
        maps = [begin(pick_hbm, pick_ref, isem.at[1]), begin(lower_hbm, lower_ref, isem.at[2])]
        xs[...] = insert((r0, r1, r2, r3), upper_ref)
        sent = []

        def made(name):
            if name == "n":
                sent.extend(begin(n, nc_out.at[j, :, pl.ds(0, D)], psem.at[j, 0]) for j in range(GROUP))
            if name == "c":
                sent.extend(begin(c, nc_out.at[j, :, pl.ds(D, D)], psem.at[j, 1]) for j in range(GROUP))

        forward_core(xs, win_v, wout_v, bias_v, n, c, proj, e, inv, out, weights, bias_copy.wait, made, lambda p: None)
        second[...] = out[...].astype(BF)
        for one in maps:
            one.wait()
        go[...] = insert((r0, r1, r2, r3), lower_ref).astype(BF)
        sent += backward_attention(go, wout_v, c, proj, e, inv, gctx, gp, bacc, edge,
                                   lambda stage: None, lambda p: None, (l0, l1, l2, l3), lsem)
        sent += [begin(bacc, bacc_out, lsem.at[0, 2]), begin(edge, edge_out, lsem.at[1, 2])]
        backward_input(xs, go, win_v, gp, out)
        extract(out[...].astype(BF), second[...], pick_ref, (g0, g1, g2, g3))
        for one in sent:
            one.wait()

    @pl.when(lax.axis_index("section") == 0)
    def _():
        came = [begin(na_ref, n, isem.at[0]), begin(ca_ref, c, isem.at[1])]
        came[0].wait()
        gone = [begin(n, nc_out.at[j, :, pl.ds(0, D)], psem.at[j, 0]) for j in range(GROUP)]
        came[1].wait()
        gone += [begin(c, nc_out.at[j, :, pl.ds(D, D)], psem.at[j, 1]) for j in range(GROUP)]
        for one in gone:
            one.wait()


def first_backward_body(g0, g1, g2, g3, upper_ref, oh_ref, c_ref, proj_ref, e_ref, inv_ref, wout, b0, b1, b2, b3, bacc_b, edge_b,
                        l0, l1, l2, l3, go_out, gp_out,
                        wout_v, c, proj, e, inv, go, gctx, gp, bacc, edge, terms, grads, upper, oh, hold,
                        isem, esem, lsem):
    @pl.when(lax.axis_index("section") == 0)
    def _():
        first = [begin(src, grads.at[q], isem.at[q]) for q, src in enumerate((g0, g1, g2, g3))]
        first.append(begin(upper_ref, upper, isem.at[4]))
        outer = begin(wout, wout_v, isem.at[5])
        rest = [begin(proj_ref, proj, isem.at[6]), begin(c_ref, c, isem.at[7]), begin(inv_ref, inv, isem.at[8])]

        def pair_copy(p):
            rows = pl.ds(pl.multiple_of(p * 2 * TOK, 16), 2 * TOK)
            return pltpu.make_async_copy(e_ref.at[rows], e.at[rows], esem.at[p])

        for p in range(PAIRS):
            pair_copy(p).start()
        last = begin(oh_ref, oh, isem.at[9])
        for one in first:
            one.wait()
        go[...] = insert([grads.at[q] for q in range(4)], upper).astype(BF)
        go_copy = begin(go, go_out, isem.at[10])

        def ready(stage):
            for one in [outer] if stage == 0 else rest:
                one.wait()

        sent = backward_attention(go, wout_v, c, proj, e, inv, gctx, gp, bacc, edge,
                                  ready, lambda p: pair_copy(p).wait(), (l0, l1, l2, l3), lsem)
        sent += [go_copy, begin(gp, gp_out, isem.at[11])]
        last.wait()
        sent += fold_bias(bacc, edge, oh, terms, (l0, l1, l2, l3), lsem)
        for one in sent:
            one.wait()

    @pl.when(lax.axis_index("section") == 1)
    def _():
        body = pl.ds(0, TOK)
        came = [begin(src.at[body], hold.at[j], lsem.at[j, 0]) for j, src in enumerate((b0, b1, b2, b3))]
        sums = [begin(bacc_b, bacc, isem.at[0]), begin(edge_b, edge, isem.at[1]), begin(oh_ref, oh, isem.at[2])]
        gone = []
        for j, dst in enumerate((l0, l1, l2, l3)):
            came[j].wait()
            gone.append(begin(hold.at[j], dst.at[body], lsem.at[j, 1]))
        for one in sums:
            one.wait()
        for one in gone + fold_bias(bacc, edge, oh, terms, (l0, l1, l2, l3), lsem):
            one.wait()


def input_grad_body(x_ref, go, gp, win, out_ref, xs, out):
    @pl.when(lax.axis_index("section") == 0)
    def _():
        load_block(x_ref, xs)
        backward_input(xs, go, win, gp, out)
        store_block(out, out_ref)


def second_result_body(g0, g1, g2, g3, lower_ref, out_ref, xs):
    @pl.when(lax.axis_index("section") == 0)
    def _():
        xs[...] = insert((g0, g1, g2, g3), lower_ref)
        store_block(xs, out_ref)


def flip_body(in_ref, out_ref, held, sem):
    source = [lax.rem(ring_depth() + GROUP - step, GROUP) for step in range(GROUP)]
    copies = [begin(in_ref.at[source[j]], held.at[pl.ds(TOK * j, TOK)], sem.at[j]) for j in range(GROUP)]
    for one in copies:
        one.wait()

    @pl.loop(0, 8)
    def _(i):
        at = pl.ds(pl.multiple_of(i * 256, 256), 256)
        out_ref[at, :] = held[:, at].T


def weight_body(nct, l0, l1, l2, l3, out, grads, made, tab, sem):
    late = (l0, l1, l2, l3)
    table = late[0][TOK:, :OPAD].astype(F32)
    for j in range(GROUP):
        grads[TOK * j : TOK * j + TOK, :] = late[j][:TOK, :]
        if j:
            table = table + late[j][TOK:, :OPAD].astype(F32)
    tab[...] = table
    depth = ring_depth()
    share = jnp.concatenate(
        [
            tab[:, pl.ds(pl.multiple_of(128 * depth, 128), 128)],
            tab[pl.ds(pl.multiple_of(8 * lax.rem(depth, 2), 8), 8), pl.ds(pl.multiple_of(512 + 128 * lax.div(depth, 2), 128), 128)],
        ],
        axis=0,
    ).astype(BF)
    made[:, 128:, :] = jnp.broadcast_to(share[None], (64, 24, 128))
    sent = []
    for rb in range(4):
        dst = slice(rb * 16, rb * 16 + 16)
        into = dot(nct[rb * 256 : rb * 256 + 256, :], grads[:, :768])
        for cb in range(6):
            made[dst, cb * 16 : cb * 16 + 16, :] = into[:, cb * 128 : cb * 128 + 128].astype(BF).reshape(16, 16, 128)
        outof = dot(nct[D + rb * 256 : D + rb * 256 + 256, :], grads[:, 768:])
        for cb in range(2):
            made[dst, 96 + cb * 16 : 112 + cb * 16, :] = outof[:, cb * 128 : cb * 128 + 128].astype(BF).reshape(16, 16, 128)
        sent.append(begin(made.at[pl.ds(rb * 16, 16)], out.at[pl.ds(rb * 16, 16)], sem.at[rb]))
    for one in sent:
        one.wait()


def sum_body(in_ref, w_ref, b_ref, bias):
    def fill(place):
        for part in range(GROUP):
            total = None
            for i in range(4):
                for xh in range(2):
                    for xl in range(2):
                        y, z = place(part, i)
                        one = in_ref[((y * 2 + xh) * 4 + z) * 2 + xl].astype(F32)
                        total = one if total is None else total + one
            for cb in range(6):
                w_ref[:, part * 768 + cb * 128 : part * 768 + cb * 128 + 128] = total[cb * 16 : cb * 16 + 16]
            for cb in range(2):
                at = 3 * D + part * 256 + cb * 128
                w_ref[:, at : at + 128] = total[96 + cb * 16 : 112 + cb * 16]
            bias[:, part * 128 : part * 128 + 128] = total[128:144]
            at = 8 * (part % 2)
            bias[at : at + 8, 512 + 128 * (part // 2) : 640 + 128 * (part // 2)] = total[144:152]
        b_ref[...] = bias[:, :OFFSETS]

    @pl.when(lax.axis_index("section") == 0)
    def _():
        fill(lambda part, i: (i, part))

    @pl.when(lax.axis_index("section") == 1)
    def _():
        fill(lambda part, i: (part, i))


def per_device(boundary, tile_kinds, proj_in, proj_out, offset_bias):
    axes = ("lat", "lon", "section")
    nlat, nlon = lax.axis_size("lat"), lax.axis_size("lon")
    section = lax.axis_index("section")
    kind = tile_kinds.reshape(1)
    x = boundary.transpose(0, 1, 3, 4, 2, 5).reshape(TOK // 2, 2, D)
    win = proj_in[0]
    wout = proj_out[0]
    onehot = jnp.asarray(ONEHOT, BF)
    onehot_t = jnp.asarray(ONEHOT.T, BF)
    pick = jnp.asarray(PICK, BF)
    upper = jnp.asarray(UPPER, BF)
    lower = jnp.asarray(LOWER, BF)

    def flat(lat, lon, sec):
        return ((lat % nlat) * nlon + lon % nlon) * 2 + sec

    def roll_pairs(dl, dn, sec):
        return [(flat(i, j, sec), flat(i + dl, j + dn, 1 - sec)) for i in range(nlat) for j in range(nlon)]

    def cross(value, sec):
        return lax.ppermute(value, axes, roll_pairs(0, 0, sec))

    far_first = [(1, 1), (1, 0), (0, 1), (0, 0)]

    def forth(pieces):
        got = [None] * 4
        for dl, dn in far_first:
            piece = pieces[(1 - dl) * 2 + (1 - dn)]
            got[dl * 2 + dn] = lax.ppermute(piece, axes, roll_pairs(-dl, -dn, 0))
        return got

    def back(pieces):
        got = [None] * 4
        for dl, dn in far_first:
            got[(1 - dl) * 2 + (1 - dn)] = lax.ppermute(pieces[dl * 2 + dn], axes, roll_pairs(dl, dn, 1))
        return got

    def rings(axis, sec):
        made = {}
        for y in range(4):
            for x in range(4):
                for z in range(4):
                    key = {"x": (y, z), "y": (x, z), "z": (x, y)}[axis]
                    made.setdefault(key, []).append(flat((y * 2 + x // 2) * 4 + z, x % 2, sec))
        return [made[key] for key in sorted(made)]

    def deal(values, groups):
        return [values[0]] + [
            lax.ppermute(values[step], axes, [(g[m], g[(m + step) % GROUP]) for g in groups for m in range(GROUP)])
            for step in range(1, GROUP)
        ]

    quarter = [shape(2 * QT, D)] * 4
    block = shape(TOK // 2, 2, D)
    f32 = functools.partial(shape, dtype=F32)
    vf32 = lambda *dims: pltpu.VMEM(dims, F32)
    vbf = lambda *dims: pltpu.VMEM(dims, BF)
    dma = lambda *dims: pltpu.SemaphoreType.DMA(dims)
    wide = shape(TOK, 3 * D)
    whole = shape(TOK, D)
    exps = shape(PAIRS * MICRO * TOK, WT)
    invs = shape(PAIRS * MICRO * WT, 128)
    late_shape = [shape(TOK + BIAS_ROWS, D)] * GROUP
    weights_v = [vbf(D, 3 * D), vbf(D, D)]
    soft_v = [vbf(PAIRS * MICRO * TOK, WT), vbf(PAIRS * MICRO * WT, 128)]
    tall = [vf32(HEADS * WT, 128), vf32(HEADS * WT, 128)]
    pieces_v = [vbf(3 * 1152, 128)] * 3
    front_v = [vf32(HEADS * WT, WT), vbf(TOK, D), vbf(TOK, D), vbf(TOK, 3 * D)] + soft_v + [vf32(TOK, D), vf32(TOK, D)]
    back_v = (
        weights_v
        + [vbf(TOK, D), vbf(TOK, 3 * D)] + soft_v + [vf32(TOK, D), vf32(TOK, D)]
        + [vbf(TOK, D), vbf(TOK, D), vbf(TOK, 3 * D)]
        + tall
        + [vbf(BIAS_ROWS, D), dma(7), dma(4), dma(GROUP, 3)]
    )

    cot = cross(x, 1)
    bias, n_a, c_a, proj_a, e_a, inv_a, first_out = call(
        first_forward_body, "first_forward", [f32(HEADS * WT, WT), whole, whole, wide, exps, invs, whole],
        [SMEM] + [VMEM] * 5 + [HBM] * 2,
        weights_v + front_v + [vf32(HEADS, OPAD)] + pieces_v + tall + [dma(7), dma(6), dma(PAIRS, 2)],
        5_000_000_000, 20_000_000, [HBM] * 6 + [VMEM],
    )(kind, x, offset_bias[0], onehot_t, jnp.asarray(ROWS_DIFFER), jnp.asarray(COLS_DIFFER), win, wout)
    pieces = call(
        pack_body, "pack", quarter, [VMEM] * 3, [vf32(TOK, D)], 340_000_000, 3_000_000, limit=SMALL,
    )(first_out, cot, pick)
    received = forth(pieces)
    both, *pieces = call(
        second_body, "second_both", [shape(GROUP, TOK, 2 * D)] + late_shape + [f32(HEADS * WT, 128)] * 2 + quarter,
        [VMEM] * 5 + [HBM] * 7,
        back_v + [vbf(TOK, D), vf32(HEADS * WT, WT), vbf(TOK, D), dma(GROUP, 2), vbf(4, QT, TOK), vbf(4, TOK, 2 * QT)],
        12_000_000_000, 20_000_000, [HBM] * 7 + [VMEM] * 4,
    )(*received, upper, pick, lower, n_a, c_a, bias, win, wout)
    late_b, sums_b, grads = pieces[:4], pieces[4:6], pieces[6:]
    grads = back(grads)
    both = lax.all_to_all(both, axes, 0, 0, axis_index_groups=rings("z", 0) + rings("y", 1), tiled=True)

    *late, go_a, gp_a = call(
        first_backward_body, "first_backward", late_shape + [whole, wide],
        [HBM] * 17,
        [vbf(D, D), vbf(TOK, D), vbf(TOK, 3 * D)] + soft_v + [vbf(TOK, D), vbf(TOK, D), vbf(TOK, 3 * D)] + tall
        + [vbf(BIAS_ROWS, D), vbf(4, 2 * QT, D), vbf(4, TOK, 2 * QT), vbf(256, 256)]
        + [vbf(GROUP, TOK, D), dma(12), dma(PAIRS), dma(GROUP, 3)],
        30_000_000_000, 20_000_000, [HBM] * 6,
    )(*grads, upper, onehot, c_a, proj_a, e_a, inv_a, wout, *late_b, *sums_b)
    late, go_a, gp_a, grads = lax.optimization_barrier((late, go_a, gp_a, grads))
    late = deal(late, rings("z", 0) + rings("y", 1))

    grad_in = call(
        input_grad_body, "input_grad", block, [VMEM] * 4, [vf32(TOK, D), vf32(TOK, D)], 2_000_000_000, 10_000_000,
    )(x, go_a, gp_a, win)
    flipped = call(
        flip_body, "flip", shape(2 * D, GROUP * TOK), [HBM],
        [vbf(GROUP * TOK, 2 * D), dma(GROUP)], 10_000_000, 10_000_000, limit=SMALL,
    )(both)
    second_out = call(
        second_result_body, "second_result", block, [VMEM] * 5, [vf32(TOK, D)], 170_000_000, 2_000_000, limit=SMALL,
    )(*grads, lower)

    terms = call(
        weight_body, "weight_terms", shape(64, 152, 128), [VMEM] * 5,
        [vbf(GROUP * TOK, D), vbf(64, 152, 128), vf32(HEADS, OPAD), dma(4)], 2_400_000_000, 10_000_000, HBM, limit=SMALL,
    )(flipped, *late)
    terms, second_out = lax.optimization_barrier((terms, cross(second_out, 0)))
    terms = lax.all_to_all(terms, ("lat", "lon"), 0, 0, tiled=True)
    result = jnp.where(section == 0, grad_in, second_out)
    result = result.reshape(1, MICRO, 6, 12, 2, D).transpose(0, 1, 4, 2, 3, 5)
    weights, table = call(
        sum_body, "sum_terms", [f32(16, 4 * D), f32(HEADS, OFFSETS)], [VMEM], [vf32(HEADS, OPAD)], 3_000_000, 3_000_000, limit=SMALL,
    )(terms)
    return (result, weights[None], table[None])


def solution(mesh):
    return jax.shard_map(
        per_device,
        mesh=mesh,
        in_specs=(
            P("section", None, None, "lat", "lon", None),
            P("section", "lat", "lon"),
            P("section", None, None),
            P("section", None, None),
            P("section", None, None),
        ),
        out_specs=(
            P("section", None, None, "lat", "lon", None),
            P("section", ("lat", "lon"), None),
            P("section", None, None),
        ),
        check_vma=False,
    )
```
